32 devices in a mesh: tm: 8 (over z, y), mark: 4 (over x, core).
Axes of the slice: x: 2, y: 2, z: 4, core: 2. Of those that a mesh axis runs over, the one named last changes fastest.
Arguments:
- event_marks: int32 [32768], P('tm'), may hold values from 0 to 8191
- event_gaps: int32 [32768], P('tm'), may hold values from 1 to 65536, as said below
- excite: bfloat16 [512, 8192], P('mark'), may hold values from 0 to 0.59765625
- source: bfloat16 [512, 8192], P('mark'), may hold values from 0 to 0.59765625
- base_rate: float32 [8192], replicated, may hold values from 0.05 to 0.5
- weights: float32 [8], replicated, may hold values from 0.2 to 2
- decay_rates: float32 [8], replicated, may hold values from 1.0172526041666667e-06 to 0.06666667
Outputs:
- grad_excite: float32 [512, 8192], P('mark', 'tm')
- grad_source: float32 [512, 8192], P('mark', 'tm')
- grad_base: float32 [8192], P('tm')
The draws below stay inside these ranges and needn't reach their ends.
Inputs may be any that keep to these rules, and one draw needn't show every extreme that they name: `event_gaps`: ticks since the previous event, the first counted from time 0.
All inputs are finite; a program needn't handle non-finite values.
Results may differ from the reference program's by a relative error of at most 0.0003.
Values sent between devices are 32-bit elements; how exact they have to be, the bound alone decides.
A program may use at most 64 MiB of HBM per device.

```python
import math
import jax
import jax.numpy as jnp
from jax import lax

MARKS = 8192
RANK = 512
KERNEL_COUNT = 8
ARRIVAL_COUNT = 32768


def draw_event_gaps(key, part):
    first, latter_portion = jax.random.split(key)
    arrival_slot = jnp.arange(ARRIVAL_COUNT)
    upper_limit = 3 + 6 * arrival_slot // ARRIVAL_COUNT
    drawn_arrivals = jax.random.randint(first, (ARRIVAL_COUNT,), 1, upper_limit)
    cluster_moment = jax.random.randint(latter_portion, (3,), 0, ARRIVAL_COUNT)
    cluster_arrival_flags = jnp.any(arrival_slot[:, None] == cluster_moment[None, :], axis=1)
    return jnp.where(cluster_arrival_flags, 2 * ARRIVAL_COUNT, drawn_arrivals).astype(jnp.int32)


def draw_decay_rates(key, part):
    first, latter_portion = jax.random.split(key)
    ranking = jax.random.permutation(first, KERNEL_COUNT)
    kept_count = KERNEL_COUNT // 2
    slow_mask = ranking < kept_count
    spread = jax.random.uniform(latter_portion, (KERNEL_COUNT,), jnp.float32)
    slow_rate = jnp.exp(jnp.log(1.0 / (30.0 * ARRIVAL_COUNT)) + spread * jnp.log(6.0))
    fast_rate = jnp.exp(jnp.log(1.0 / 3000.0) + spread * jnp.log(200.0))
    return jnp.where(slow_mask, slow_rate, fast_rate).astype(jnp.float32)


def plant(entries, key, least, high):
    extent = entries.shape
    place = [jax.random.randint(jax.random.fold_in(key, axis), (), 0, extent[axis]) for axis in range(len(extent))]
    entries = entries.at[tuple(place)].set(least)
    longest = extent.index(max(extent))
    place[longest] = (place[longest] + 1) % extent[longest]
    return entries.at[tuple(place)].set(high)


def shard_levels(stream_key, shape, shards, low, top_value):
    def one(position, blocks):
        draws = jax.random.uniform(jax.random.fold_in(jax.random.fold_in(stream_key, 6), position), (blocks,), jnp.float32, low / len(shards), top_value / len(shards))
        return jnp.repeat(jnp.exp(draws), shape[position] // blocks).reshape((-1,) + (1,) * (len(shape) - position - 1))

    gain = one(*shards[0])
    for cut in shards[1:]:
        gain = gain * one(*cut)
    return gain


def setup_inputs(seed: int = 0) -> dict:
    splits = jax.random.split(jax.random.key(seed), 8)
    event_marks = plant(jax.random.randint(splits[0], (ARRIVAL_COUNT,), 0, MARKS), jax.random.fold_in(splits[0], 1), 0, MARKS - 1).astype(jnp.int32)
    event_gaps = draw_event_gaps(jax.random.fold_in(splits[7], 71), 0)
    excite = jnp.clip(0.59765625 * jax.random.uniform(splits[2], (RANK, MARKS), jnp.float32) ** shard_levels(splits[2], (RANK, MARKS), ((0, 4),), -0.2, 0.2), 0.0, 0.59765625).astype(jnp.bfloat16)
    source = jnp.clip(0.59765625 * jax.random.uniform(splits[3], (RANK, MARKS), jnp.float32) ** shard_levels(splits[3], (RANK, MARKS), ((0, 4),), -0.2, 0.2), 0.0, 0.59765625).astype(jnp.bfloat16)
    base_rate = jnp.clip(jnp.exp(jax.random.uniform(splits[4], (MARKS,), jnp.float32, math.log(0.05), math.log(0.5))), 0.05, 0.5)
    weights = jnp.clip(jnp.exp(jax.random.uniform(splits[5], (KERNEL_COUNT,), jnp.float32, math.log(0.2), math.log(2.0))), 0.2, 2.0)
    decay_rates = draw_decay_rates(jax.random.fold_in(splits[7], 71), 0)
    return {"event_marks": event_marks, "event_gaps": event_gaps, "excite": excite, "source": source, "base_rate": base_rate, "weights": weights, "decay_rates": decay_rates}


def decay_kernel(stamp_block, weights, decay_rates):
    block_size = stamp_block.shape[0]
    elapsed = jnp.maximum(stamp_block[:, None] - stamp_block[None, :], 0.0)
    causal = jnp.arange(block_size)[:, None] > jnp.arange(block_size)[None, :]
    accumulated = jnp.zeros((block_size, block_size), jnp.float32)
    for channel in range(decay_rates.shape[0]):
        accumulated = accumulated + weights[channel] * decay_rates[channel] * jnp.exp(-decay_rates[channel] * elapsed)
    return jnp.where(causal, accumulated, 0.0)


def reference(event_marks, event_gaps, excite, source, base_rate, weights, decay_rates):
    highest = lax.Precision.HIGHEST
    event_count = event_marks.shape[0]
    block_size = 512 if event_count % 512 == 0 else event_count
    block_count = event_count // block_size
    mark_count = excite.shape[1]
    dense_coupling = excite.shape[0]
    channels = decay_rates.shape[0]
    stamps = jnp.cumsum(event_gaps).astype(jnp.float32)
    t_end = stamps[-1]
    excite_full = excite.astype(jnp.float32).T
    source_complete = source.astype(jnp.float32).T
    excite_total = jnp.sum(excite_full, axis=0)
    anchors = jnp.concatenate([jnp.zeros((1,), jnp.float32), stamps[block_size - 1::block_size][:-1]])
    stamp_blocks = stamps.reshape(block_count, block_size)
    mark_blocks = event_marks.reshape(block_count, block_size)

    def forward(carry, pieces):
        carried, excite_sum, base_sum = carry
        stamp_block, mark_block, anchor = pieces
        values = source_complete[mark_block]
        factors = excite_full[mark_block]
        kernel = decay_kernel(stamp_block, weights, decay_rates)
        arrival = weights[None, :] * jnp.exp(-decay_rates[None, :] * (stamp_block - anchor)[:, None])
        excitation = jnp.dot(kernel, values, precision=highest) + jnp.dot(arrival, carried, precision=highest)
        intensity = base_rate[mark_block] + jnp.sum(factors * excitation, axis=1) / dense_coupling
        inverse = 1.0 / intensity
        end_time = stamp_block[-1]
        emission = decay_rates[:, None] * jnp.exp(-decay_rates[:, None] * (end_time - stamp_block)[None, :])
        carried = jnp.exp(-decay_rates * (end_time - anchor))[:, None] * carried + jnp.dot(emission, values, precision=highest)
        excite_sum = excite_sum.at[mark_block].add(inverse[:, None] * excitation)
        base_sum = base_sum.at[mark_block].add(inverse)
        return (carried, excite_sum, base_sum), inverse

    start = (jnp.zeros((channels, dense_coupling), jnp.float32), jnp.zeros((mark_count, dense_coupling), jnp.float32), jnp.zeros((mark_count,), jnp.float32))
    (carried, excite_sum, base_sum), inverses = lax.scan(forward, start, (stamp_blocks, mark_blocks, anchors))

    def backward(carry, pieces):
        pending, source_sum, integrated = carry
        stamp_block, mark_block, anchor, inverse = pieces
        values = source_complete[mark_block]
        weighted = inverse[:, None] * excite_full[mark_block]
        kernel = decay_kernel(stamp_block, weights, decay_rates)
        end_time = stamp_block[-1]
        reaching = weights[None, :] * jnp.exp(-decay_rates[None, :] * (end_time - stamp_block)[:, None])
        feedback = jnp.dot(kernel.T, weighted, precision=highest) + jnp.dot(reaching, pending, precision=highest)
        remainder = jnp.sum(weights[None, :] * (1.0 - jnp.exp(-decay_rates[None, :] * (t_end - stamp_block)[:, None])), axis=1)
        source_sum = source_sum.at[mark_block].add(feedback - remainder[:, None] * excite_total[None, :] / mark_count)
        integrated = integrated + jnp.dot(remainder, values, precision=highest)
        emission = decay_rates[:, None] * jnp.exp(-decay_rates[:, None] * (stamp_block - anchor)[None, :])
        pending = jnp.exp(-decay_rates * (end_time - anchor))[:, None] * pending + jnp.dot(emission, weighted, precision=highest)
        return (pending, source_sum, integrated), remainder

    start_back = (jnp.zeros((channels, dense_coupling), jnp.float32), jnp.zeros((mark_count, dense_coupling), jnp.float32), jnp.zeros((dense_coupling,), jnp.float32))
    (pending, source_sum, integrated), remainders = lax.scan(backward, start_back, (stamp_blocks, mark_blocks, anchors, inverses), reverse=True)
    factor = mark_count / event_count
    grad_excite = factor * excite_sum - integrated[None, :] / event_count
    grad_source = factor * source_sum
    grad_base = factor * base_sum - t_end / event_count
    return grad_excite.T, grad_source.T, grad_base
```

```python
import functools

import jax
import jax.numpy as jnp
from jax import lax
from jax.experimental import pallas as pl
from jax.experimental.pallas import tpu as pltpu
from jax.sharding import PartitionSpec as P

F32 = jnp.float32
BF16 = jnp.bfloat16
B = 128
SUB = 32
PARTS = B // SUB
HIGH = lax.Precision.HIGHEST
MESH = pl.DeviceIdType.MESH
VMEM = pl.BlockSpec(memory_space=pltpu.VMEM)
SMEM = pl.BlockSpec(memory_space=pltpu.SMEM)
ANY = pl.BlockSpec(memory_space=pl.ANY)
NT = (((1,), (1,)), ((), ()))


def iota(shape, axis):
    return lax.broadcasted_iota(jnp.int32, shape, axis)


def dot(a, b):
    return jnp.dot(a, b, preferred_element_type=F32)


def halves(a):
    high = a.astype(BF16).astype(F32)
    return high, a - high


def down(ref, count):
    row = iota((count, B), 0)
    out = jnp.zeros((count, B), F32)
    for k in range(count):
        out = jnp.where(row == k, ref[k], out)
    return out


def parted(a):
    part = lax.div(iota(a.shape, 1), SUB)
    return jnp.concatenate([jnp.where(part == c, a, 0.0) for c in range(PARTS)], 0)


def turned(row):
    return jnp.broadcast_to(row, (B, B)).T


def rows_at(b, size):
    return pl.ds(pl.multiple_of(b * size, size), size)


def front_kernel(
    n, lanes_n, rank,
    weights, decay, marks, gaps, src, exc, base,
    values, grad_base, minus, marks_out,
    factors, table, rows, smarks, own, gshard, u, te, ts, sym, inside, lanes, states, sums, dec, base_e,
    inverse, remain, ends, device, summaries, partial, total, back, behind, base_own, base_parts,
    load_sem, mark_sem, ag_send, ag_recv, f_send, f_recv, p_send, p_recv, b_send, b_recv, g_send, g_recv,
):
    count = decay.shape[0]
    width = count * PARTS
    half = n // 2
    shard_blocks = marks.shape[0]
    blocks = 2 * shard_blocks
    types = table.shape[0]
    groups = types // B
    ranks = src.shape[0] // 2
    edge = B // 2
    me = lax.axis_index("tm")
    mine = lax.axis_index("mark")
    r = lax.div(me, half)
    q = lax.rem(me, half)
    peers = [lax.rem(me + i, n) for i in range(1, n)]
    mates = [r * half + lax.rem(q + i, half) for i in range(1, half)]
    others = [lax.rem(mine + i, lanes_n) for i in range(1, lanes_n)]
    twin = q + (1 - r) * half

    if ranks < edge:
        for a in range(2):
            factors[a * edge + ranks : (a + 1) * edge, :] = jnp.zeros((edge - ranks, types), BF16)
    loads = []
    for a, ref in enumerate((src, exc)):
        copy = pltpu.make_async_copy(
            ref.at[pl.ds(pl.multiple_of(r * ranks, ranks), ranks), :],
            factors.at[a * edge : a * edge + ranks, :],
            load_sem.at[a],
        )
        copy.start()
        loads.append(copy)

    barrier = pltpu.get_barrier_semaphore()
    targets = [{"tm": p, "mark": mine} for p in peers]
    targets += [{"tm": t, "mark": o} for o in others for t in (me, twin)]
    for t in targets:
        pl.semaphore_signal(barrier, inc=1, device_id=t, device_id_type=MESH)
    pl.semaphore_wait(barrier, len(targets))

    slot = lax.rem(me, 2)
    own[...] = marks[...]

    def shard_copy(a, i, j, target):
        ref, dst = ((own, marks_out), (gaps, gshard))[a]
        return pltpu.make_async_remote_copy(
            src_ref=ref, dst_ref=dst.at[j], send_sem=ag_send.at[a, i], recv_sem=ag_recv.at[a, j],
            device_id={"tm": target}, device_id_type=MESH,
        )

    dests = [lax.div(me, 2) + i * half for i in range(2)]
    for i, p in enumerate(dests):

        @pl.when(p != me)
        def _():
            for a in range(2):
                shard_copy(a, i, slot, p).start()

        @pl.when(p == me)
        def _():
            marks_out[slot] = marks[...]
            gshard[slot] = gaps[...]

    for copy in loads:
        copy.wait()

    def build(c, acc):
        s = rows_at(c, B)
        t = factors[:, s].astype(F32).T
        table[s, :] = t
        return acc + jnp.sum(t.reshape(B // 8, 8, B), axis=0)

    acc = lax.fori_loop(0, groups, build, jnp.zeros((8, B), F32), unroll=2)
    xtot = jnp.sum(acc, axis=0, keepdims=True)

    for j in range(2):

        @pl.when(2 * q + j != me)
        def _():
            for a in range(2):
                shard_copy(a, 0, j, twin).wait_recv()

    move = pltpu.make_async_copy(marks_out, smarks, mark_sem.at[0])
    move.start()

    d8, w8 = down(decay, count), down(weights, count)
    gap_all = jnp.concatenate([gshard[0], gshard[1]], 0).astype(F32)
    li, lj = iota((B, B), 0), iota((B, B), 1)
    first = lax.div(lj, SUB) * SUB

    def pick(mask, a):
        return jnp.dot(a, mask.astype(F32), precision=HIGH, preferred_element_type=F32)

    uv = pick(li <= lj, gap_all)
    u[...] = uv
    te[...] = pick(li <= first + SUB - 1, gap_all)
    ts[...] = pick(li < first, gap_all)
    lengths = jnp.broadcast_to(uv[:, B - 1 :], (blocks, B))
    after_mask = (iota((blocks, blocks), 1) > iota((blocks, blocks), 0)).astype(F32)
    endv = jnp.dot(after_mask, lengths, precision=HIGH, preferred_element_type=F32)
    ends[...] = endv
    duration = endv[0:1, :] + lengths[0:1, :]
    move.wait()

    for j in range(2):

        def fetch(b, _):
            def some(g, _):
                for i in range(16):
                    m = smarks[j, b, g * 16 + i]
                    e = (j * shard_blocks + b) * B + g * 16 + i
                    rows[pl.ds(e, 1), :] = table[pl.ds(m, 1), :]
                return 0

            lax.fori_loop(0, B // 16, some, 0)
            return 0

        lax.fori_loop(0, shard_blocks, fetch, 0)

    part_row = lax.div(iota((1, B), 1), SUB)
    lane = iota((1, B), 1)

    def two(a, b):
        k = a.shape[0]
        high, low = halves(a)
        both = dot(jnp.concatenate([high, low], 0).astype(BF16), b)
        return both[:k] + both[k:]

    def emit(b, _):
        ur, er, sr = u[pl.ds(b, 1), :], te[pl.ds(b, 1), :], ts[pl.ds(b, 1), :]
        vals = rows[rows_at(b, B), :].astype(BF16)
        sums[rows_at(b, width), :] = two(parted(d8 * jnp.exp(-d8 * (er - ur))), vals)
        span = er - sr
        for c in range(PARTS):
            dec[pl.ds(pl.multiple_of(b * width + c * count, count), count), :] = jnp.exp(
                -d8 * span[:, c * SUB : c * SUB + 1]
            )
        return 0

    lax.fori_loop(0, blocks, emit, 0, unroll=4)

    def forward_state(start, keep):
        def step(b, state):
            for c in range(PARTS):
                s = pl.ds(pl.multiple_of(b * width + c * count, count), count)
                if keep:
                    states[s, :] = state
                state = state * dec[s, :] + sums[s, :]
            return state

        return lax.fori_loop(0, blocks, step, start, unroll=2)

    def share(source, dest, send, recv):
        copies = []
        for i, p in enumerate(mates):
            copies.append(
                pltpu.make_async_remote_copy(
                    src_ref=source, dst_ref=dest.at[q], send_sem=send.at[i], recv_sem=recv.at[i],
                    device_id={"tm": p}, device_id_type=MESH,
                )
            )
        for copy in copies:
            copy.start()
        dest[q] = source[...]
        return copies

    device[0:count, :] = forward_state(jnp.zeros((count, B), F32), False)
    device[count:, :] = jnp.broadcast_to(duration, (count, B))
    state_copies = share(device, summaries, f_send, f_recv)

    base_high, base_low = halves(base[...])
    base2 = jnp.concatenate([base_high, base_low], 0).T.astype(BF16)
    subi = iota((SUB, B), 0)
    subj = lax.rem(iota((SUB, B), 1), SUB)

    def mark_row(b):
        return marks_out[lax.div(b, shard_blocks), pl.ds(lax.rem(b, shard_blocks), 1), :]

    def within(b, _):
        ur, sr = u[pl.ds(b, 1), :], ts[pl.ds(b, 1), :]
        s = rows_at(b, B)
        col = turned(ur)
        colc = col[0:SUB]
        for c in range(1, PARTS):
            colc = jnp.where(part_row == c, col[c * SUB : (c + 1) * SUB], colc)
        apart = jnp.abs(colc - ur)
        g = jnp.zeros((SUB, B), F32)
        for k in range(count):
            g = g + (weights[k] * decay[k]) * jnp.exp(-decay[k] * apart)
        sym[rows_at(b, SUB), :] = g
        high, low = halves(jnp.where(subi > subj, g, 0.0))
        left = jnp.concatenate([parted(high), parted(low)], 0).astype(BF16)
        both = dot(left, rows[s, :].astype(BF16))
        inside[s, :] = both[:B] + both[B:]
        lh, ll = halves(parted(w8 * jnp.exp(-d8 * (ur - sr))))
        stack = jnp.concatenate([lh, lh, ll, jnp.zeros((B - 3 * width, B), F32)], 0)
        lanes[s, :] = stack.T.astype(BF16)
        m = mark_row(b)
        hi, lo = lax.div(m, B), lax.rem(m, B)
        onehot = (lax.rem(iota((2 * groups, B), 0), groups) == hi).astype(BF16)
        found = dot(base2, onehot)
        base_e[pl.ds(b, 1), :] = jnp.sum(jnp.where(li == lo, found, 0.0), axis=0, keepdims=True)
        return 0

    lax.fori_loop(0, blocks, within, 0, unroll=2)

    for copy in state_copies:
        copy.wait()
    start = jnp.zeros((count, B), F32)
    after = jnp.zeros((1, B), F32)
    t_end = jnp.zeros((1, B), F32)
    for p in range(half):
        span = summaries[p, count : count + 1, :]
        start = jnp.where(p < q, start * jnp.exp(-d8 * span) + summaries[p, 0:count, :], start)
        after = after + jnp.where(p > q, span, 0.0)
        t_end = t_end + span
    forward_state(start, True)

    ones = jnp.ones((8, B), BF16)
    fill = jnp.zeros((B - 3 * width, B), F32)

    def forward(b, _):
        s = rows_at(b, B)
        sh, sl = halves(states[rows_at(b, width), :])
        value = inside[s, :] + dot(lanes[s, :], jnp.concatenate([sh, sl, sh, fill], 0).astype(BF16))
        inside[s, :] = value
        product = jnp.where(lane < edge, value * pltpu.roll(rows[s, :], edge, 1), 0.0)
        high, low = halves(product)
        tot = lax.dot_general(ones, high.astype(BF16), NT, preferred_element_type=F32)
        tot = tot + lax.dot_general(ones, low.astype(BF16), NT, preferred_element_type=F32)
        partial[pl.ds(b, 1), :] = tot[0:1, :] * (1.0 / rank)
        return 0

    lax.fori_loop(0, blocks, forward, 0, unroll=2)

    spot = mine * 2 + r
    part_copies = []
    for i, t in enumerate([(twin, mine)] + [(t, o) for o in others for t in (me, twin)]):
        copy = pltpu.make_async_remote_copy(
            src_ref=partial, dst_ref=total.at[spot], send_sem=p_send.at[i], recv_sem=p_recv.at[i],
            device_id={"tm": t[0], "mark": t[1]}, device_id_type=MESH,
        )
        copy.start()
        part_copies.append(copy)
    total[spot] = partial[...]

    def rest(b, comp):
        left = w8 * (1.0 - jnp.exp(-d8 * (u[pl.ds(b, 1), :] * -1.0 + lengths_row(b) + ends[pl.ds(b, 1), :] + after)))
        rem = jnp.sum(left, axis=0, keepdims=True)
        remain[pl.ds(b, 1), :] = rem
        return comp + two(jnp.broadcast_to(rem, (8, B)), rows[rows_at(b, B), :].astype(BF16))

    def lengths_row(b):
        return u[pl.ds(b, 1), B - 1 :]

    comp = lax.fori_loop(0, blocks, rest, jnp.zeros((8, B), F32), unroll=4)

    for copy in part_copies:
        copy.wait()
    intensity = base_e[...]
    for j in range(2 * lanes_n):
        intensity = intensity + total[j]
    inverse[...] = 1.0 / intensity

    def reverse(b, _):
        e8 = d8 * jnp.exp(-d8 * (u[pl.ds(b, 1), :] - ts[pl.ds(b, 1), :])) * inverse[pl.ds(b, 1), :]
        sums[rows_at(b, width), :] = two(parted(e8), rows[rows_at(b, B), :].astype(BF16))
        return 0

    lax.fori_loop(0, blocks, reverse, 0, unroll=4)

    def reverse_state(start, keep):
        def step(i, state):
            b = blocks - 1 - i
            for c in reversed(range(PARTS)):
                s = pl.ds(pl.multiple_of(b * width + c * count, count), count)
                if keep:
                    states[s, :] = state
                state = state * dec[s, :] + sums[s, :]
            return state

        return lax.fori_loop(0, blocks, step, start, unroll=2)

    behind[0:count, :] = reverse_state(jnp.zeros((count, B), F32), False)
    behind[count:, :] = comp
    back_copies = share(behind, back, b_send, b_recv)

    def spread(i, both):
        b = r * shard_blocks + i
        m = mark_row(b)
        hi, lo = lax.div(m, B), lax.rem(m, B)
        ih, il = halves(inverse[pl.ds(b, 1), :])
        wide = jnp.concatenate([jnp.broadcast_to(ih, (groups, B)), jnp.broadcast_to(il, (groups, B))], 0)
        left = jnp.where(lax.rem(iota((2 * groups, B), 0), groups) == hi, wide, 0.0).astype(BF16)
        right = (li == lo).astype(BF16)
        return both + lax.dot_general(left, right, NT, preferred_element_type=F32)

    both = lax.fori_loop(0, shard_blocks, spread, jnp.zeros((2 * groups, B), F32), unroll=2)
    base_own[...] = (both[:groups] + both[groups:]).reshape(base_own.shape)
    base_copies = []
    for i, p in enumerate(peers):
        copy = pltpu.make_async_remote_copy(
            src_ref=base_own.at[p], dst_ref=base_parts.at[me], send_sem=g_send.at[i], recv_sem=g_recv.at[i],
            device_id={"tm": p}, device_id_type=MESH,
        )
        copy.start()
        base_copies.append(copy)
    base_parts[me] = base_own[me]

    for copy in back_copies:
        copy.wait()
    pending = jnp.zeros((count, B), F32)
    comp_all = jnp.zeros((8, B), F32)
    for p in reversed(range(half)):
        span = summaries[p, count : count + 1, :]
        pending = jnp.where(p > q, pending * jnp.exp(-d8 * span) + back[p, 0:count, :], pending)
        comp_all = comp_all + back[p, count:, :]
    reverse_state(pending, True)
    events_all = blocks * B * half
    minus[...] = jnp.where(lane < edge, comp_all * (1.0 / events_all), 0.0)

    row8 = iota((8, B), 0)

    def thirds(a, places):
        high, rest = halves(a)
        mid, low = halves(rest)
        out = jnp.zeros((8, B), F32)
        for term, where in zip((high, mid, low), places):
            for k in where:
                out = jnp.where(row8 == k, term, out)
        return out

    xstack = thirds(xtot * (-1.0 / types), ((0, 2, 5), (1, 4), (3,)))
    fill24 = jnp.zeros((B - 3 * width - 8, B), F32)

    def feedback(b, _):
        s = rows_at(b, B)
        ur, er, ir = u[pl.ds(b, 1), :], te[pl.ds(b, 1), :], inverse[pl.ds(b, 1), :]
        high, low = halves(jnp.where(subi < subj, sym[rows_at(b, SUB), :] * ir, 0.0))
        left = jnp.concatenate([parted(high), parted(low)], 0).astype(BF16)
        both = dot(left, rows[s, :].astype(BF16))
        lh, ll = halves(parted(w8 * jnp.exp(-d8 * (er - ur))))
        rstack = thirds(remain[pl.ds(b, 1), :], ((0, 1, 3), (2, 4), (5,)))
        turn = jnp.concatenate([lh, lh, ll, rstack, fill24], 0).T.astype(BF16)
        sh, sl = halves(states[rows_at(b, width), :])
        value = both[:B] + both[B:] + dot(
            turn, jnp.concatenate([sh, sl, sh, xstack, fill24], 0).astype(BF16)
        )
        values[s, :] = jnp.where(lane < edge, inside[s, :] * turned(ir), value)
        return 0

    lax.fori_loop(0, blocks, feedback, 0, unroll=2)

    for copy in base_copies:
        copy.wait()
    base_all = base_parts[0]
    for p in range(1, n):
        base_all = base_all + base_parts[p]
    grad_base[...] = base_all * (types / events_all) - t_end * (1.0 / events_all)
    for i, p in enumerate(dests):

        @pl.when(p != me)
        def _():
            for a in range(2):
                shard_copy(a, i, slot, p).wait_send()


def scatter_kernel(marks, values, out, *tables):
    count = len(tables) + 1
    every = (out,) + tables
    types = out.shape[0]

    def zero(i, _):
        for t in every:
            t[pl.ds(pl.multiple_of(i * 32, 32), 32), :] = jnp.zeros((32, B), F32)
        return 0

    lax.fori_loop(0, types // 32, zero, 0)
    shards, blocks, _ = marks.shape
    group = 2 * count
    for j in range(shards):

        def block(b, _):
            def some(g, _):
                for i in range(group):
                    t = every[i % count]
                    m = marks[j, b, g * group + i]
                    e = (j * blocks + b) * B + g * group + i
                    t[pl.ds(m, 1), :] = t[pl.ds(m, 1), :] + values[pl.ds(e, 1), :]
                return 0

            lax.fori_loop(0, B // group, some, 0)
            return 0

        lax.fori_loop(0, blocks, block, 0)

    def add(i, _):
        s = pl.ds(pl.multiple_of(i * 32, 32), 32)
        acc = out[s, :]
        for t in tables:
            acc = acc + t[s, :]
        out[s, :] = acc
        return 0

    lax.fori_loop(0, types // 32, add, 0)


def ring_kernel(n, factor, minus, dense, grad_excite, grad_source, slots, pieces, twin_in, send, recv, t_send, t_recv):
    half = n // 2
    per = dense.shape[0] // n
    rows = per // 2
    edge = B // 2
    ranks = grad_excite.shape[0] // 2
    me = lax.axis_index("tm")
    r = lax.div(me, half)
    q = lax.rem(me, half)
    odd = lax.rem(q, 2)
    at = lax.div(q, 2) + odd * (lax.div(2 * half - 1 - q, 2) - lax.div(q, 2))
    twin = q + (1 - r) * half

    def member(place):
        c = lax.rem(place + 2 * half, half)
        return 2 * c + lax.div(c, half // 2) * (2 * half - 1 - 4 * c)

    towards = [member(at + 1) + r * half, member(at - 1) + r * half]
    barrier = pltpu.get_barrier_semaphore()
    for p in towards + [twin]:
        pl.semaphore_signal(barrier, inc=1, device_id={"tm": p}, device_id_type=MESH)
    pl.semaphore_wait(barrier, 3)

    def span(j, step):
        way, kind = j % 2, j // 2
        place = at + 1 + step if way else at - 1 - step
        where = (1 - r) if kind == 0 else r
        block = member(place) + where * half
        return pl.ds(pl.multiple_of(block * per + way * rows, 8), rows)

    def copy(j, step, source):
        return pltpu.make_async_remote_copy(
            src_ref=source, dst_ref=slots.at[j, step], send_sem=send.at[j, step], recv_sem=recv.at[j, step],
            device_id={"tm": towards[j % 2]}, device_id_type=MESH,
        )

    chains = range(4)
    for j in chains:
        copy(j, 0, dense.at[span(j, 0), :]).start()

    def step(s, _):
        for j in chains:
            held = slots.at[j, s - 1]
            copy(j, s - 1, held).wait_recv()
            held[...] += dense[span(j, s), :]
            copy(j, s, held).start()
        return 0

    lax.fori_loop(1, half - 1, step, 0)

    def twin_copy(j):
        return pltpu.make_async_remote_copy(
            src_ref=pieces.at[j], dst_ref=twin_in.at[j], send_sem=t_send.at[j], recv_sem=t_recv.at[j],
            device_id={"tm": twin}, device_id_type=MESH,
        )

    for j in chains:
        copy(j, half - 2, slots.at[j, half - 2]).wait_recv()
        pieces[j] = (slots[j, half - 2] + dense[span(j, half - 1), :]) * factor - minus[0:1, :]
        if j < 2:
            twin_copy(j).start()
    low = r == 0
    for j in range(2):
        twin_copy(j).wait_recv()
        for i in range(rows // B):
            s = slice(i * B, (i + 1) * B)
            mine, their = pieces[2 + j, s, :].T, twin_in[j, s, :].T
            first = jnp.where(low, mine, their)
            second = jnp.where(low, their, mine)
            t = slice(j * rows + i * B, j * rows + (i + 1) * B)
            grad_excite[:ranks, t] = first[:ranks]
            grad_excite[ranks:, t] = second[:ranks]
            grad_source[:ranks, t] = first[edge : edge + ranks]
            grad_source[ranks:, t] = second[edge : edge + ranks]

    def sent(s, _):
        for j in chains:
            copy(j, s, slots.at[j, s]).wait_send()
        return 0

    lax.fori_loop(0, half - 1, sent, 0)
    for j in range(2):
        twin_copy(j).wait_send()


def body(marks, gaps, excite, source, base_rate, weights, decay):
    shard = marks.shape[0]
    slices, types = excite.shape
    n = lax.axis_size("tm")
    lanes_n = lax.axis_size("mark")
    half = n // 2
    rank = slices * lanes_n
    count = decay.shape[0]
    shard_blocks = shard // B
    blocks = 2 * shard_blocks
    events = 2 * shard
    groups = types // B
    width = count * PARTS
    dma = pltpu.SemaphoreType.DMA
    plane = pltpu.VMEM((blocks, B), F32)
    tall = pltpu.VMEM((events, B), F32)
    small = pltpu.VMEM((blocks * width, B), F32)
    packet = pltpu.VMEM((count + 8, B), F32)
    packets = pltpu.VMEM((half, count + 8, B), F32)
    types_own = types // n

    values, grad_base, minus, marks_all = pl.pallas_call(
        functools.partial(front_kernel, n, lanes_n, rank),
        out_shape=[
            jax.ShapeDtypeStruct((events, B), F32),
            jax.ShapeDtypeStruct((groups // n, B), F32),
            jax.ShapeDtypeStruct((8, B), F32),
            jax.ShapeDtypeStruct((2, shard_blocks, B), jnp.int32),
        ],
        in_specs=[SMEM, SMEM, VMEM, VMEM, ANY, ANY, VMEM],
        out_specs=[VMEM] * 4,
        scratch_shapes=[
            pltpu.VMEM((B, types), BF16),
            pltpu.VMEM((types, B), F32),
            tall,
            pltpu.SMEM((2, shard_blocks, B), jnp.int32),
            pltpu.VMEM((shard_blocks, B), jnp.int32),
            pltpu.VMEM((2, shard_blocks, B), jnp.int32),
            plane, plane, plane,
            pltpu.VMEM((blocks * SUB, B), F32),
            tall,
            pltpu.VMEM((events, B), BF16),
            small, small, small,
            plane, plane, plane, plane,
            packet, packets,
            plane, pltpu.VMEM((2 * lanes_n, blocks, B), F32),
            packets, packet,
            pltpu.VMEM((n, groups // n, B), F32),
            pltpu.VMEM((n, groups // n, B), F32),
            dma((2,)), dma((1,)),
            dma((2, 2)), dma((2, 2)),
            dma((half - 1,)), dma((half - 1,)),
            dma((2 * lanes_n - 1,)), dma((2 * lanes_n - 1,)),
            dma((half - 1,)), dma((half - 1,)),
            dma((n - 1,)), dma((n - 1,)),
        ],
        compiler_params=pltpu.CompilerParams(
            collective_id=0, has_side_effects=True, vmem_limit_bytes=48 * 2**20
        ),
    )(weights, decay, marks.reshape(shard_blocks, B), gaps.reshape(shard_blocks, B), source, excite,
      base_rate.reshape(groups, B))

    dense = pl.pallas_call(
        scatter_kernel,
        out_shape=jax.ShapeDtypeStruct((types, B), F32),
        in_specs=[SMEM, VMEM],
        out_specs=VMEM,
        scratch_shapes=[pltpu.VMEM((types, B), F32)] * 3,
        compiler_params=pltpu.CompilerParams(vmem_limit_bytes=40 * 2**20),
    )(marks_all, values)

    grad_excite, grad_source = pl.pallas_call(
        functools.partial(ring_kernel, n, types / (events * half)),
        out_shape=[jax.ShapeDtypeStruct((slices, types_own), F32)] * 2,
        in_specs=[VMEM] * 2,
        out_specs=[VMEM] * 2,
        scratch_shapes=[
            pltpu.VMEM((4, half - 1, types_own // 2, B), F32),
            pltpu.VMEM((4, types_own // 2, B), F32),
            pltpu.VMEM((2, types_own // 2, B), F32),
            dma((4, half - 1)), dma((4, half - 1)), dma((2,)), dma((2,)),
        ],
        compiler_params=pltpu.CompilerParams(
            collective_id=1, has_side_effects=True, vmem_limit_bytes=40 * 2**20
        ),
    )(minus, dense)
    return grad_excite, grad_source, grad_base.reshape(types_own)


def solution(mesh):
    return jax.shard_map(
        body,
        mesh=mesh,
        in_specs=(P("tm"), P("tm"), P("mark", None), P("mark", None), P(), P(), P()),
        out_specs=(P("mark", "tm"), P("mark", "tm"), P("tm")),
        check_vma=False,
    )
```

```python
import functools

import jax
import jax.numpy as jnp
from jax import lax
from jax.experimental import pallas as pl
from jax.experimental.pallas import tpu as pltpu
from jax.sharding import PartitionSpec as P

F32 = jnp.float32
BF16 = jnp.bfloat16
B = 128
SUB = 32
UNROLL = 16
PARTS = B // SUB
HIGH = lax.Precision.HIGHEST
MESH = pl.DeviceIdType.MESH
VMEM = pl.BlockSpec(memory_space=pltpu.VMEM)
SMEM = pl.BlockSpec(memory_space=pltpu.SMEM)
HBM = pl.BlockSpec(memory_space=pltpu.HBM)
NT = (((1,), (1,)), ((), ()))


def iota(shape, axis):
    return lax.broadcasted_iota(jnp.int32, shape, axis)


def dot(a, b):
    return jnp.dot(a, b, preferred_element_type=F32)


def halves(a):
    high = a.astype(BF16).astype(F32)
    return high, a - high


def down(ref, count):
    row = iota((count, B), 0)
    out = jnp.zeros((count, B), F32)
    for k in range(count):
        out = jnp.where(row == k, ref[k], out)
    return out


def parted(a):
    part = lax.div(iota(a.shape, 1), SUB)
    return jnp.concatenate([jnp.where(part == c, a, 0.0) for c in range(PARTS)], 0)


def turned(row):
    return jnp.broadcast_to(row, (B, B)).T


def batched(count, size, one):
    def body(g, _):
        stores = []
        for i in range(size):
            stores += one(g * size + i)
        for ref, where, value in stores:
            ref[where] = value
        return 0

    lax.fori_loop(0, count // size, body, 0)


def rows_at(b, size):
    return pl.ds(pl.multiple_of(b * size, size), size)


def front_kernel(
    n, lanes_n, rank,
    weights, decay, marks, gaps, src, exc, base,
    values, grad_base, minus, marks_out,
    factors, table, rows, smarks, own, gshard, u, te, ts, sym, inside, excitation, lanes, states, sums, dec, base_e,
    inverse, remain, ends, device, summaries, partial, total, back, behind, base_own, base_parts,
    load_sem, mark_sem, ag_send, ag_recv, f_send, f_recv, p_send, p_recv, b_send, b_recv, g_send, g_recv,
):
    count = decay.shape[0]
    width = count * PARTS
    half = n // 2
    shard_blocks = marks.shape[0]
    blocks = 2 * shard_blocks
    types = table.shape[0]
    groups = types // B
    ranks = src.shape[0] // 2
    edge = B // 2
    me = lax.axis_index("tm")
    mine = lax.axis_index("mark")
    r = lax.div(me, half)
    q = lax.rem(me, half)
    peers = [lax.rem(me + i, n) for i in range(1, n)]
    mates = [r * half + lax.rem(q + i, half) for i in range(1, half)]
    others = [lax.rem(mine + i, lanes_n) for i in range(1, lanes_n)]
    twin = q + (1 - r) * half

    if ranks < edge:
        for a in range(2):
            factors[a * edge + ranks : (a + 1) * edge, :] = jnp.zeros((edge - ranks, types), BF16)
    loads = []
    for a, ref in enumerate((src, exc)):
        copy = pltpu.make_async_copy(
            ref.at[pl.ds(pl.multiple_of(r * ranks, ranks), ranks), :],
            factors.at[a * edge : a * edge + ranks, :],
            load_sem.at[a],
        )
        copy.start()
        loads.append(copy)

    barrier = pltpu.get_barrier_semaphore()
    targets = [{"tm": p, "mark": mine} for p in peers]
    targets += [{"tm": t, "mark": o} for o in others for t in (me, twin)]
    for t in targets:
        pl.semaphore_signal(barrier, inc=1, device_id=t, device_id_type=MESH)
    pl.semaphore_wait(barrier, len(targets))

    slot = lax.rem(me, 2)
    own[...] = marks[...]

    def shard_copy(a, i, j, target):
        ref, dst = ((own, marks_out), (gaps, gshard))[a]
        return pltpu.make_async_remote_copy(
            src_ref=ref, dst_ref=dst.at[j], send_sem=ag_send.at[a, i], recv_sem=ag_recv.at[a, j],
            device_id={"tm": target}, device_id_type=MESH,
        )

    dests = [lax.div(me, 2) + i * half for i in range(2)]
    for i, p in enumerate(dests):

        @pl.when(p != me)
        def _():
            for a in range(2):
                shard_copy(a, i, slot, p).start()

        @pl.when(p == me)
        def _():
            marks_out[slot] = marks[...]
            gshard[slot] = gaps[...]

    for copy in loads:
        copy.wait()

    def build(c, acc):
        s = rows_at(c, B)
        t = factors[:, s].astype(F32).T
        table[s, :] = t
        return acc + jnp.sum(t.reshape(B // 8, 8, B), axis=0)

    acc = lax.fori_loop(0, groups, build, jnp.zeros((8, B), F32), unroll=8)
    xtot = jnp.sum(acc, axis=0, keepdims=True)

    for j in range(2):

        @pl.when(2 * q + j != me)
        def _():
            for a in range(2):
                shard_copy(a, 0, j, twin).wait_recv()

    move = pltpu.make_async_copy(marks_out, smarks, mark_sem.at[0])
    move.start()

    d8, w8 = down(decay, count), down(weights, count)
    gap_all = jnp.concatenate([gshard[0], gshard[1]], 0).astype(F32)
    li, lj = iota((B, B), 0), iota((B, B), 1)
    first = lax.div(lj, SUB) * SUB

    def pick(mask, a):
        return jnp.dot(a, mask.astype(F32), precision=HIGH, preferred_element_type=F32)

    uv = pick(li <= lj, gap_all)
    u[...] = uv
    te[...] = pick(li <= first + SUB - 1, gap_all)
    ts[...] = pick(li < first, gap_all)
    lengths = jnp.broadcast_to(uv[:, B - 1 :], (blocks, B))
    after_mask = (iota((blocks, blocks), 1) > iota((blocks, blocks), 0)).astype(F32)
    endv = jnp.dot(after_mask, lengths, precision=HIGH, preferred_element_type=F32)
    ends[...] = endv
    duration = endv[0:1, :] + lengths[0:1, :]
    move.wait()

    for j in range(2):

        def fetch(g, _):
            for i in range(B):
                m = smarks[j, g, i]
                e = (j * shard_blocks + g) * B + i
                rows[pl.ds(e, 1), :] = table[pl.ds(m, 1), :]
            return 0

        lax.fori_loop(0, shard_blocks, fetch, 0)

    part_row = lax.div(iota((1, B), 1), SUB)
    lane = iota((1, B), 1)

    def two(a, b):
        k = a.shape[0]
        high, low = halves(a)
        both = dot(jnp.concatenate([high, low], 0).astype(BF16), b)
        return both[:k] + both[k:]

    def emit(b):
        ur, er, sr = u[pl.ds(b, 1), :], te[pl.ds(b, 1), :], ts[pl.ds(b, 1), :]
        vals = rows[rows_at(b, B), :].astype(BF16)
        span = er - sr
        decays = [jnp.exp(-d8 * span[:, c * SUB : c * SUB + 1]) for c in range(PARTS)]
        spot = (rows_at(b, width), slice(None))
        return [
            (sums, spot, two(parted(d8 * jnp.exp(-d8 * (er - ur))), vals)),
            (dec, spot, jnp.concatenate([jnp.broadcast_to(t, (count, B)) for t in decays], 0)),
        ]

    batched(blocks, UNROLL, emit)

    def forward_state(start, keep):
        def step(b, state):
            for c in range(PARTS):
                s = pl.ds(pl.multiple_of(b * width + c * count, count), count)
                if keep:
                    states[s, :] = state
                state = state * dec[s, :] + sums[s, :]
            return state

        return lax.fori_loop(0, blocks, step, start, unroll=2)

    def share(source, dest, send, recv):
        copies = []
        for i, p in enumerate(mates):
            copies.append(
                pltpu.make_async_remote_copy(
                    src_ref=source, dst_ref=dest.at[q], send_sem=send.at[i], recv_sem=recv.at[i],
                    device_id={"tm": p}, device_id_type=MESH,
                )
            )
        for copy in copies:
            copy.start()
        dest[q] = source[...]
        return copies

    device[0:count, :] = forward_state(jnp.zeros((count, B), F32), False)
    device[count:, :] = jnp.broadcast_to(duration, (count, B))
    state_copies = share(device, summaries, f_send, f_recv)

    base_high, base_low = halves(base[...])
    base2 = jnp.concatenate([base_high, base_low], 0).T.astype(BF16)
    subi = iota((SUB, B), 0)
    subj = lax.rem(iota((SUB, B), 1), SUB)

    def mark_row(b):
        return marks_out[lax.div(b, shard_blocks), pl.ds(lax.rem(b, shard_blocks), 1), :]

    def within(b):
        ur, sr = u[pl.ds(b, 1), :], ts[pl.ds(b, 1), :]
        s = rows_at(b, B)
        col = turned(ur)
        colc = col[0:SUB]
        for c in range(1, PARTS):
            colc = jnp.where(part_row == c, col[c * SUB : (c + 1) * SUB], colc)
        apart = jnp.abs(colc - ur)
        g = jnp.zeros((SUB, B), F32)
        for k in range(count):
            g = g + (weights[k] * decay[k]) * jnp.exp(-decay[k] * apart)
        high, low = halves(jnp.where(subi > subj, g, 0.0))
        left = jnp.concatenate([parted(high), parted(low)], 0).astype(BF16)
        both = dot(left, rows[s, :].astype(BF16))
        lh, ll = halves(parted(w8 * jnp.exp(-d8 * (ur - sr))))
        stack = jnp.concatenate([lh, lh, ll, jnp.zeros((B - 3 * width, B), F32)], 0)
        m = mark_row(b)
        hi, lo = lax.div(m, B), lax.rem(m, B)
        onehot = (lax.rem(iota((2 * groups, B), 0), groups) == hi).astype(BF16)
        found = dot(base2, onehot)
        return [
            (sym, (rows_at(b, SUB), slice(None)), g),
            (inside, (s, slice(None)), both[:B] + both[B:]),
            (lanes, (s, slice(None)), stack.T.astype(BF16)),
            (base_e, (pl.ds(b, 1), slice(None)), jnp.sum(jnp.where(li == lo, found, 0.0), axis=0, keepdims=True)),
        ]

    batched(blocks, UNROLL, within)

    for copy in state_copies:
        copy.wait()
    start = jnp.zeros((count, B), F32)
    after = jnp.zeros((1, B), F32)
    t_end = jnp.zeros((1, B), F32)
    for p in range(half):
        span = summaries[p, count : count + 1, :]
        start = jnp.where(p < q, start * jnp.exp(-d8 * span) + summaries[p, 0:count, :], start)
        after = after + jnp.where(p > q, span, 0.0)
        t_end = t_end + span
    forward_state(start, True)

    ones = jnp.ones((8, B), BF16)
    fill = jnp.zeros((B - 3 * width, B), F32)

    def forward(b):
        s = rows_at(b, B)
        sh, sl = halves(states[rows_at(b, width), :])
        value = inside[s, :] + dot(lanes[s, :], jnp.concatenate([sh, sl, sh, fill], 0).astype(BF16))
        product = jnp.where(lane < edge, value * pltpu.roll(rows[s, :], edge, 1), 0.0)
        high, low = halves(product)
        tot = lax.dot_general(ones, high.astype(BF16), NT, preferred_element_type=F32)
        tot = tot + lax.dot_general(ones, low.astype(BF16), NT, preferred_element_type=F32)
        return [
            (excitation, (s, slice(None)), value),
            (partial, (pl.ds(b, 1), slice(None)), tot[0:1, :] * (1.0 / rank)),
        ]

    batched(blocks, UNROLL, forward)

    spot = mine * 2 + r
    part_copies = []
    for i, t in enumerate([(twin, mine)] + [(t, o) for o in others for t in (me, twin)]):
        copy = pltpu.make_async_remote_copy(
            src_ref=partial, dst_ref=total.at[spot], send_sem=p_send.at[i], recv_sem=p_recv.at[i],
            device_id={"tm": t[0], "mark": t[1]}, device_id_type=MESH,
        )
        copy.start()
        part_copies.append(copy)
    total[spot] = partial[...]

    def rest(b, comp):
        left = w8 * (1.0 - jnp.exp(-d8 * (u[pl.ds(b, 1), :] * -1.0 + lengths_row(b) + ends[pl.ds(b, 1), :] + after)))
        rem = jnp.sum(left, axis=0, keepdims=True)
        remain[pl.ds(b, 1), :] = rem
        return comp + two(jnp.broadcast_to(rem, (8, B)), rows[rows_at(b, B), :].astype(BF16))

    def lengths_row(b):
        return u[pl.ds(b, 1), B - 1 :]

    comp = lax.fori_loop(0, blocks, rest, jnp.zeros((8, B), F32), unroll=4)

    for copy in part_copies:
        copy.wait()
    intensity = base_e[...]
    for j in range(2 * lanes_n):
        intensity = intensity + total[j]
    inverse[...] = 1.0 / intensity

    def reverse(b):
        e8 = d8 * jnp.exp(-d8 * (u[pl.ds(b, 1), :] - ts[pl.ds(b, 1), :])) * inverse[pl.ds(b, 1), :]
        return [(sums, (rows_at(b, width), slice(None)), two(parted(e8), rows[rows_at(b, B), :].astype(BF16)))]

    batched(blocks, UNROLL, reverse)

    def reverse_state(start, keep):
        def step(i, state):
            b = blocks - 1 - i
            for c in reversed(range(PARTS)):
                s = pl.ds(pl.multiple_of(b * width + c * count, count), count)
                if keep:
                    states[s, :] = state
                state = state * dec[s, :] + sums[s, :]
            return state

        return lax.fori_loop(0, blocks, step, start, unroll=2)

    behind[0:count, :] = reverse_state(jnp.zeros((count, B), F32), False)
    behind[count:, :] = comp
    back_copies = share(behind, back, b_send, b_recv)

    def spread(i, both):
        b = r * shard_blocks + i
        m = mark_row(b)
        hi, lo = lax.div(m, B), lax.rem(m, B)
        ih, il = halves(inverse[pl.ds(b, 1), :])
        wide = jnp.concatenate([jnp.broadcast_to(ih, (groups, B)), jnp.broadcast_to(il, (groups, B))], 0)
        left = jnp.where(lax.rem(iota((2 * groups, B), 0), groups) == hi, wide, 0.0).astype(BF16)
        right = (li == lo).astype(BF16)
        return both + lax.dot_general(left, right, NT, preferred_element_type=F32)

    both = lax.fori_loop(0, shard_blocks, spread, jnp.zeros((2 * groups, B), F32), unroll=2)
    base_own[...] = (both[:groups] + both[groups:]).reshape(base_own.shape)
    base_copies = []
    for i, p in enumerate(peers):
        copy = pltpu.make_async_remote_copy(
            src_ref=base_own.at[p], dst_ref=base_parts.at[me], send_sem=g_send.at[i], recv_sem=g_recv.at[i],
            device_id={"tm": p}, device_id_type=MESH,
        )
        copy.start()
        base_copies.append(copy)
    base_parts[me] = base_own[me]

    for copy in back_copies:
        copy.wait()
    pending = jnp.zeros((count, B), F32)
    comp_all = jnp.zeros((8, B), F32)
    for p in reversed(range(half)):
        span = summaries[p, count : count + 1, :]
        pending = jnp.where(p > q, pending * jnp.exp(-d8 * span) + back[p, 0:count, :], pending)
        comp_all = comp_all + back[p, count:, :]
    reverse_state(pending, True)
    events_all = blocks * B * half
    minus[...] = jnp.where(lane < edge, comp_all * (1.0 / events_all), 0.0)

    row8 = iota((8, B), 0)

    def thirds(a, places):
        high, rest = halves(a)
        mid, low = halves(rest)
        out = jnp.zeros((8, B), F32)
        for term, where in zip((high, mid, low), places):
            for k in where:
                out = jnp.where(row8 == k, term, out)
        return out

    xstack = thirds(xtot * (-1.0 / types), ((0, 2, 5), (1, 4), (3,)))
    fill24 = jnp.zeros((B - 3 * width - 8, B), F32)

    def feedback(b):
        s = rows_at(b, B)
        ur, er, ir = u[pl.ds(b, 1), :], te[pl.ds(b, 1), :], inverse[pl.ds(b, 1), :]
        high, low = halves(jnp.where(subi < subj, sym[rows_at(b, SUB), :] * ir, 0.0))
        left = jnp.concatenate([parted(high), parted(low)], 0).astype(BF16)
        both = dot(left, rows[s, :].astype(BF16))
        lh, ll = halves(parted(w8 * jnp.exp(-d8 * (er - ur))))
        rstack = thirds(remain[pl.ds(b, 1), :], ((0, 1, 3), (2, 4), (5,)))
        turn = jnp.concatenate([lh, lh, ll, rstack, fill24], 0).T.astype(BF16)
        sh, sl = halves(states[rows_at(b, width), :])
        value = both[:B] + both[B:] + dot(
            turn, jnp.concatenate([sh, sl, sh, xstack, fill24], 0).astype(BF16)
        )
        return [(values, (s, slice(None)), jnp.where(lane < edge, excitation[s, :] * turned(ir), value))]

    batched(blocks, UNROLL, feedback)

    for copy in base_copies:
        copy.wait()
    base_all = base_parts[0]
    for p in range(1, n):
        base_all = base_all + base_parts[p]
    grad_base[...] = base_all * (types / events_all) - t_end * (1.0 / events_all)
    for i, p in enumerate(dests):

        @pl.when(p != me)
        def _():
            for a in range(2):
                shard_copy(a, i, slot, p).wait_send()


def scatter_kernel(marks, values, out, *tables):
    count = len(tables) + 1
    every = (out,) + tables
    types = out.shape[0]

    def zero(i, _):
        for t in every:
            t[pl.ds(pl.multiple_of(i * 32, 32), 32), :] = jnp.zeros((32, B), F32)
        return 0

    lax.fori_loop(0, types // 32, zero, 0)
    shards, blocks, _ = marks.shape
    for j in range(shards):

        def block(b, _):
            for i in range(B):
                t = every[i % count]
                m = marks[j, b, i]
                e = (j * blocks + b) * B + i
                t[pl.ds(m, 1), :] = t[pl.ds(m, 1), :] + values[pl.ds(e, 1), :]
            return 0

        lax.fori_loop(0, blocks, block, 0)

    def add(i, _):
        s = pl.ds(pl.multiple_of(i * 32, 32), 32)
        acc = out[s, :]
        for t in tables:
            acc = acc + t[s, :]
        out[s, :] = acc
        return 0

    lax.fori_loop(0, types // 32, add, 0)


def ring_kernel(n, factor, minus, dense, grad_excite, grad_source, slots, pieces, twin_in, send, recv, t_send, t_recv):
    half = n // 2
    per = dense.shape[0] // n
    rows = per // 2
    edge = B // 2
    ranks = grad_excite.shape[0] // 2
    me = lax.axis_index("tm")
    r = lax.div(me, half)
    q = lax.rem(me, half)
    odd = lax.rem(q, 2)
    at = lax.div(q, 2) + odd * (lax.div(2 * half - 1 - q, 2) - lax.div(q, 2))
    twin = q + (1 - r) * half

    def member(place):
        c = lax.rem(place + 2 * half, half)
        return 2 * c + lax.div(c, half // 2) * (2 * half - 1 - 4 * c)

    towards = [member(at + 1) + r * half, member(at - 1) + r * half]
    barrier = pltpu.get_barrier_semaphore()
    for p in towards + [twin]:
        pl.semaphore_signal(barrier, inc=1, device_id={"tm": p}, device_id_type=MESH)
    pl.semaphore_wait(barrier, 3)

    def span(j, step):
        way, kind = j % 2, j // 2
        place = at + 1 + step if way else at - 1 - step
        where = (1 - r) if kind == 0 else r
        block = member(place) + where * half
        return pl.ds(pl.multiple_of(block * per + way * rows, 8), rows)

    def copy(j, step, source):
        return pltpu.make_async_remote_copy(
            src_ref=source, dst_ref=slots.at[j, step], send_sem=send.at[j, step], recv_sem=recv.at[j, step],
            device_id={"tm": towards[j % 2]}, device_id_type=MESH,
        )

    chains = range(4)
    for j in chains:
        copy(j, 0, dense.at[span(j, 0), :]).start()

    def step(s, _):
        for j in chains:
            held = slots.at[j, s - 1]
            copy(j, s - 1, held).wait_recv()
            held[...] += dense[span(j, s), :]
            copy(j, s, held).start()
        return 0

    lax.fori_loop(1, half - 1, step, 0)

    def twin_copy(j):
        return pltpu.make_async_remote_copy(
            src_ref=pieces.at[j], dst_ref=twin_in.at[j], send_sem=t_send.at[j], recv_sem=t_recv.at[j],
            device_id={"tm": twin}, device_id_type=MESH,
        )

    for j in chains:
        copy(j, half - 2, slots.at[j, half - 2]).wait_recv()
        pieces[j] = (slots[j, half - 2] + dense[span(j, half - 1), :]) * factor - minus[0:1, :]
        if j < 2:
            twin_copy(j).start()
    low = r == 0
    for j in range(2):
        twin_copy(j).wait_recv()
        for i in range(rows // B):
            s = slice(i * B, (i + 1) * B)
            mine, their = pieces[2 + j, s, :].T, twin_in[j, s, :].T
            first = jnp.where(low, mine, their)
            second = jnp.where(low, their, mine)
            t = slice(j * rows + i * B, j * rows + (i + 1) * B)
            grad_excite[:ranks, t] = first[:ranks]
            grad_excite[ranks:, t] = second[:ranks]
            grad_source[:ranks, t] = first[edge : edge + ranks]
            grad_source[ranks:, t] = second[edge : edge + ranks]

    def sent(s, _):
        for j in chains:
            copy(j, s, slots.at[j, s]).wait_send()
        return 0

    lax.fori_loop(0, half - 1, sent, 0)
    for j in range(2):
        twin_copy(j).wait_send()


def body(marks, gaps, excite, source, base_rate, weights, decay):
    shard = marks.shape[0]
    slices, types = excite.shape
    n = lax.axis_size("tm")
    lanes_n = lax.axis_size("mark")
    half = n // 2
    rank = slices * lanes_n
    count = decay.shape[0]
    shard_blocks = shard // B
    blocks = 2 * shard_blocks
    events = 2 * shard
    groups = types // B
    width = count * PARTS
    dma = pltpu.SemaphoreType.DMA
    plane = pltpu.VMEM((blocks, B), F32)
    tall = pltpu.VMEM((events, B), F32)
    small = pltpu.VMEM((blocks * width, B), F32)
    packet = pltpu.VMEM((count + 8, B), F32)
    packets = pltpu.VMEM((half, count + 8, B), F32)
    types_own = types // n

    values, grad_base, minus, marks_all = pl.pallas_call(
        functools.partial(front_kernel, n, lanes_n, rank),
        out_shape=[
            jax.ShapeDtypeStruct((events, B), F32),
            jax.ShapeDtypeStruct((groups // n, B), F32),
            jax.ShapeDtypeStruct((8, B), F32),
            jax.ShapeDtypeStruct((2, shard_blocks, B), jnp.int32),
        ],
        in_specs=[SMEM, SMEM, VMEM, VMEM, HBM, HBM, VMEM],
        out_specs=[VMEM] * 4,
        scratch_shapes=[
            pltpu.VMEM((B, types), BF16),
            pltpu.VMEM((types, B), F32),
            tall,
            pltpu.SMEM((2, shard_blocks, B), jnp.int32),
            pltpu.VMEM((shard_blocks, B), jnp.int32),
            pltpu.VMEM((2, shard_blocks, B), jnp.int32),
            plane, plane, plane,
            pltpu.VMEM((blocks * SUB, B), F32),
            tall, tall,
            pltpu.VMEM((events, B), BF16),
            small, small, small,
            plane, plane, plane, plane,
            packet, packets,
            plane, pltpu.VMEM((2 * lanes_n, blocks, B), F32),
            packets, packet,
            pltpu.VMEM((n, groups // n, B), F32),
            pltpu.VMEM((n, groups // n, B), F32),
            dma((2,)), dma((1,)),
            dma((2, 2)), dma((2, 2)),
            dma((half - 1,)), dma((half - 1,)),
            dma((2 * lanes_n - 1,)), dma((2 * lanes_n - 1,)),
            dma((half - 1,)), dma((half - 1,)),
            dma((n - 1,)), dma((n - 1,)),
        ],
        compiler_params=pltpu.CompilerParams(
            collective_id=0, has_side_effects=True, vmem_limit_bytes=48 * 2**20
        ),
    )(weights, decay, marks.reshape(shard_blocks, B), gaps.reshape(shard_blocks, B), source, excite,
      base_rate.reshape(groups, B))

    dense = pl.pallas_call(
        scatter_kernel,
        out_shape=jax.ShapeDtypeStruct((types, B), F32),
        in_specs=[SMEM, VMEM],
        out_specs=VMEM,
        scratch_shapes=[pltpu.VMEM((types, B), F32)] * 7,
        compiler_params=pltpu.CompilerParams(vmem_limit_bytes=40 * 2**20),
    )(marks_all, values)

    grad_excite, grad_source = pl.pallas_call(
        functools.partial(ring_kernel, n, types / (events * half)),
        out_shape=[jax.ShapeDtypeStruct((slices, types_own), F32)] * 2,
        in_specs=[VMEM] * 2,
        out_specs=[VMEM] * 2,
        scratch_shapes=[
            pltpu.VMEM((4, half - 1, types_own // 2, B), F32),
            pltpu.VMEM((4, types_own // 2, B), F32),
            pltpu.VMEM((2, types_own // 2, B), F32),
            dma((4, half - 1)), dma((4, half - 1)), dma((2,)), dma((2,)),
        ],
        compiler_params=pltpu.CompilerParams(
            collective_id=1, has_side_effects=True, vmem_limit_bytes=40 * 2**20
        ),
    )(minus, dense)
    return grad_excite, grad_source, grad_base.reshape(types_own)


def solution(mesh):
    return jax.shard_map(
        body,
        mesh=mesh,
        in_specs=(P("tm"), P("tm"), P("mark", None), P("mark", None), P(), P(), P()),
        out_specs=(P("mark", "tm"), P("mark", "tm"), P("tm")),
        check_vma=False,
    )
```

```python
import functools

import jax
import jax.numpy as jnp
from jax import lax
from jax.experimental import pallas as pl
from jax.experimental.pallas import tpu as pltpu
from jax.sharding import PartitionSpec as P

F32 = jnp.float32
BF16 = jnp.bfloat16
B = 128
SUB = 32
UNROLL = 16
ALL_VMEM = 60 * 2**20
PARTS = B // SUB
HIGH = lax.Precision.HIGHEST
MESH = pl.DeviceIdType.MESH
VMEM = pl.BlockSpec(memory_space=pltpu.VMEM)
SMEM = pl.BlockSpec(memory_space=pltpu.SMEM)
HBM = pl.BlockSpec(memory_space=pltpu.HBM)
NT = (((1,), (1,)), ((), ()))


def iota(shape, axis):
    return lax.broadcasted_iota(jnp.int32, shape, axis)


def dot(a, b):
    return jnp.dot(a, b, preferred_element_type=F32)


def halves(a):
    high = a.astype(BF16).astype(F32)
    return high, a - high


def down(ref, count):
    row = iota((count, B), 0)
    out = jnp.zeros((count, B), F32)
    for k in range(count):
        out = jnp.where(row == k, ref[k], out)
    return out


def parted(a):
    part = lax.div(iota(a.shape, 1), SUB)
    return jnp.concatenate([jnp.where(part == c, a, 0.0) for c in range(PARTS)], 0)


def turned(row):
    return jnp.broadcast_to(row, (B, B)).T


def batched(count, size, one, then=None):
    def body(g, _):
        stores = []
        for i in range(size):
            stores += one(g * size + i)
        for ref, where, value in stores:
            ref[where] = value
        if then is not None:
            then(g)
        return 0

    lax.fori_loop(0, count // size, body, 0)


def rows_at(b, size):
    return pl.ds(pl.multiple_of(b * size, size), size)


def front_kernel(
    n, lanes_n, rank,
    weights, decay, marks, gaps, src, exc, base,
    values_out, grad_base, minus, marks_out,
    factors, table, rows, smarks, own, gshard, u, te, ts, sym, inside, excitation, lanes, states, sums, dec, base_e,
    inverse, remain, ends, device, summaries, partial, total, back, behind, base_own, base_parts,
    load_sem, mark_sem, ag_send, ag_recv, f_send, f_recv, p_send, p_recv, b_send, b_recv, g_send, g_recv, values, out_sem,
):
    count = decay.shape[0]
    width = count * PARTS
    half = n // 2
    shard_blocks = marks.shape[0]
    blocks = 2 * shard_blocks
    types = table.shape[0]
    groups = types // B
    ranks = src.shape[0] // 2
    edge = B // 2
    me = lax.axis_index("tm")
    mine = lax.axis_index("mark")
    r = lax.div(me, half)
    q = lax.rem(me, half)
    peers = [lax.rem(me + i, n) for i in range(1, n)]
    mates = [r * half + lax.rem(q + i, half) for i in range(1, half)]
    others = [lax.rem(mine + i, lanes_n) for i in range(1, lanes_n)]
    twin = q + (1 - r) * half

    if ranks < edge:
        for a in range(2):
            factors[a * edge + ranks : (a + 1) * edge, :] = jnp.zeros((edge - ranks, types), BF16)
    loads = []
    for a, ref in enumerate((src, exc)):
        copy = pltpu.make_async_copy(
            ref.at[pl.ds(pl.multiple_of(r * ranks, ranks), ranks), :],
            factors.at[a * edge : a * edge + ranks, :],
            load_sem.at[a],
        )
        copy.start()
        loads.append(copy)

    barrier = pltpu.get_barrier_semaphore()
    targets = [{"tm": p, "mark": mine} for p in peers]
    targets += [{"tm": t, "mark": o} for o in others for t in (me, twin)]
    for t in targets:
        pl.semaphore_signal(barrier, inc=1, device_id=t, device_id_type=MESH)
    pl.semaphore_wait(barrier, len(targets))

    slot = lax.rem(me, 2)
    own[...] = marks[...]

    def shard_copy(a, i, j, target):
        ref, dst = ((own, marks_out), (gaps, gshard))[a]
        return pltpu.make_async_remote_copy(
            src_ref=ref, dst_ref=dst.at[j], send_sem=ag_send.at[a, i], recv_sem=ag_recv.at[a, j],
            device_id={"tm": target}, device_id_type=MESH,
        )

    dests = [lax.div(me, 2) + i * half for i in range(2)]
    for i, p in enumerate(dests):

        @pl.when(p != me)
        def _():
            for a in range(2):
                shard_copy(a, i, slot, p).start()

        @pl.when(p == me)
        def _():
            marks_out[slot] = marks[...]
            gshard[slot] = gaps[...]

    for copy in loads:
        copy.wait()

    def build(c, acc):
        s = rows_at(c, B)
        t = factors[:, s].astype(F32).T
        table[s, :] = t
        return acc + jnp.sum(t.reshape(B // 8, 8, B), axis=0)

    acc = lax.fori_loop(0, groups, build, jnp.zeros((8, B), F32), unroll=8)
    xtot = jnp.sum(acc, axis=0, keepdims=True)

    for j in range(2):

        @pl.when(2 * q + j != me)
        def _():
            for a in range(2):
                shard_copy(a, 0, j, twin).wait_recv()

    move = pltpu.make_async_copy(marks_out, smarks, mark_sem.at[0])
    move.start()

    d8, w8 = down(decay, count), down(weights, count)
    gap_all = jnp.concatenate([gshard[0], gshard[1]], 0).astype(F32)
    li, lj = iota((B, B), 0), iota((B, B), 1)
    first = lax.div(lj, SUB) * SUB

    def pick(mask, a):
        return jnp.dot(a, mask.astype(F32), precision=HIGH, preferred_element_type=F32)

    uv = pick(li <= lj, gap_all)
    u[...] = uv
    te[...] = pick(li <= first + SUB - 1, gap_all)
    ts[...] = pick(li < first, gap_all)
    lengths = jnp.broadcast_to(uv[:, B - 1 :], (blocks, B))
    after_mask = (iota((blocks, blocks), 1) > iota((blocks, blocks), 0)).astype(F32)
    endv = jnp.dot(after_mask, lengths, precision=HIGH, preferred_element_type=F32)
    ends[...] = endv
    duration = endv[0:1, :] + lengths[0:1, :]
    move.wait()

    for j in range(2):

        def fetch(g, _):
            for i in range(B):
                m = smarks[j, g, i]
                e = (j * shard_blocks + g) * B + i
                rows[pl.ds(e, 1), :] = table[pl.ds(m, 1), :]
            return 0

        lax.fori_loop(0, shard_blocks, fetch, 0)

    part_row = lax.div(iota((1, B), 1), SUB)
    lane = iota((1, B), 1)

    def two(a, b):
        k = a.shape[0]
        high, low = halves(a)
        both = dot(jnp.concatenate([high, low], 0).astype(BF16), b)
        return both[:k] + both[k:]

    def emit(b):
        ur, er, sr = u[pl.ds(b, 1), :], te[pl.ds(b, 1), :], ts[pl.ds(b, 1), :]
        vals = rows[rows_at(b, B), :].astype(BF16)
        span = er - sr
        decays = [jnp.exp(-d8 * span[:, c * SUB : c * SUB + 1]) for c in range(PARTS)]
        spot = (rows_at(b, width), slice(None))
        return [
            (sums, spot, two(parted(d8 * jnp.exp(-d8 * (er - ur))), vals)),
            (dec, spot, jnp.concatenate([jnp.broadcast_to(t, (count, B)) for t in decays], 0)),
        ]

    batched(blocks, UNROLL, emit)

    def forward_state(start, keep):
        def step(b, state):
            for c in range(PARTS):
                s = pl.ds(pl.multiple_of(b * width + c * count, count), count)
                if keep:
                    states[s, :] = state
                state = state * dec[s, :] + sums[s, :]
            return state

        return lax.fori_loop(0, blocks, step, start, unroll=2)

    def share(source, dest, send, recv):
        copies = []
        for i, p in enumerate(mates):
            copies.append(
                pltpu.make_async_remote_copy(
                    src_ref=source, dst_ref=dest.at[q], send_sem=send.at[i], recv_sem=recv.at[i],
                    device_id={"tm": p}, device_id_type=MESH,
                )
            )
        for copy in copies:
            copy.start()
        dest[q] = source[...]
        return copies

    device[0:count, :] = forward_state(jnp.zeros((count, B), F32), False)
    device[count:, :] = jnp.broadcast_to(duration, (count, B))
    state_copies = share(device, summaries, f_send, f_recv)

    base_high, base_low = halves(base[...])
    base2 = jnp.concatenate([base_high, base_low], 0).T.astype(BF16)
    subi = iota((SUB, B), 0)
    subj = lax.rem(iota((SUB, B), 1), SUB)

    def mark_row(b):
        return marks_out[lax.div(b, shard_blocks), pl.ds(lax.rem(b, shard_blocks), 1), :]

    def within(b):
        ur, sr = u[pl.ds(b, 1), :], ts[pl.ds(b, 1), :]
        s = rows_at(b, B)
        col = turned(ur)
        colc = col[0:SUB]
        for c in range(1, PARTS):
            colc = jnp.where(part_row == c, col[c * SUB : (c + 1) * SUB], colc)
        apart = jnp.abs(colc - ur)
        g = jnp.zeros((SUB, B), F32)
        for k in range(count):
            g = g + (weights[k] * decay[k]) * jnp.exp(-decay[k] * apart)
        high, low = halves(jnp.where(subi > subj, g, 0.0))
        left = jnp.concatenate([parted(high), parted(low)], 0).astype(BF16)
        both = dot(left, rows[s, :].astype(BF16))
        lh, ll = halves(parted(w8 * jnp.exp(-d8 * (ur - sr))))
        stack = jnp.concatenate([lh, lh, ll, jnp.zeros((B - 3 * width, B), F32)], 0)
        m = mark_row(b)
        hi, lo = lax.div(m, B), lax.rem(m, B)
        onehot = (lax.rem(iota((2 * groups, B), 0), groups) == hi).astype(BF16)
        found = dot(base2, onehot)
        return [
            (sym, (rows_at(b, SUB), slice(None)), g),
            (inside, (s, slice(None)), both[:B] + both[B:]),
            (lanes, (s, slice(None)), stack.T.astype(BF16)),
            (base_e, (pl.ds(b, 1), slice(None)), jnp.sum(jnp.where(li == lo, found, 0.0), axis=0, keepdims=True)),
        ]

    batched(blocks, UNROLL, within)

    for copy in state_copies:
        copy.wait()
    start = jnp.zeros((count, B), F32)
    after = jnp.zeros((1, B), F32)
    t_end = jnp.zeros((1, B), F32)
    for p in range(half):
        span = summaries[p, count : count + 1, :]
        start = jnp.where(p < q, start * jnp.exp(-d8 * span) + summaries[p, 0:count, :], start)
        after = after + jnp.where(p > q, span, 0.0)
        t_end = t_end + span
    forward_state(start, True)

    ones = jnp.ones((8, B), BF16)
    fill = jnp.zeros((B - 3 * width, B), F32)

    def forward(b):
        s = rows_at(b, B)
        sh, sl = halves(states[rows_at(b, width), :])
        value = inside[s, :] + dot(lanes[s, :], jnp.concatenate([sh, sl, sh, fill], 0).astype(BF16))
        product = jnp.where(lane < edge, value * pltpu.roll(rows[s, :], edge, 1), 0.0)
        high, low = halves(product)
        tot = lax.dot_general(ones, high.astype(BF16), NT, preferred_element_type=F32)
        tot = tot + lax.dot_general(ones, low.astype(BF16), NT, preferred_element_type=F32)
        return [
            (excitation, (s, slice(None)), value),
            (partial, (pl.ds(b, 1), slice(None)), tot[0:1, :] * (1.0 / rank)),
        ]

    batched(blocks, UNROLL, forward)

    spot = mine * 2 + r
    part_copies = []
    for i, t in enumerate([(twin, mine)] + [(t, o) for o in others for t in (me, twin)]):
        copy = pltpu.make_async_remote_copy(
            src_ref=partial, dst_ref=total.at[spot], send_sem=p_send.at[i], recv_sem=p_recv.at[i],
            device_id={"tm": t[0], "mark": t[1]}, device_id_type=MESH,
        )
        copy.start()
        part_copies.append(copy)
    total[spot] = partial[...]

    def rest(b, comp):
        left = w8 * (1.0 - jnp.exp(-d8 * (u[pl.ds(b, 1), :] * -1.0 + lengths_row(b) + ends[pl.ds(b, 1), :] + after)))
        rem = jnp.sum(left, axis=0, keepdims=True)
        remain[pl.ds(b, 1), :] = rem
        return comp + two(jnp.broadcast_to(rem, (8, B)), rows[rows_at(b, B), :].astype(BF16))

    def lengths_row(b):
        return u[pl.ds(b, 1), B - 1 :]

    comp = lax.fori_loop(0, blocks, rest, jnp.zeros((8, B), F32), unroll=4)

    for copy in part_copies:
        copy.wait()
    intensity = base_e[...]
    for j in range(2 * lanes_n):
        intensity = intensity + total[j]
    inverse[...] = 1.0 / intensity

    def reverse(b):
        e8 = d8 * jnp.exp(-d8 * (u[pl.ds(b, 1), :] - ts[pl.ds(b, 1), :])) * inverse[pl.ds(b, 1), :]
        return [(sums, (rows_at(b, width), slice(None)), two(parted(e8), rows[rows_at(b, B), :].astype(BF16)))]

    batched(blocks, UNROLL, reverse)

    def reverse_state(start, keep):
        def step(i, state):
            b = blocks - 1 - i
            for c in reversed(range(PARTS)):
                s = pl.ds(pl.multiple_of(b * width + c * count, count), count)
                if keep:
                    states[s, :] = state
                state = state * dec[s, :] + sums[s, :]
            return state

        return lax.fori_loop(0, blocks, step, start, unroll=2)

    behind[0:count, :] = reverse_state(jnp.zeros((count, B), F32), False)
    behind[count:, :] = comp
    back_copies = share(behind, back, b_send, b_recv)

    def spread(i, both):
        b = r * shard_blocks + i
        m = mark_row(b)
        hi, lo = lax.div(m, B), lax.rem(m, B)
        ih, il = halves(inverse[pl.ds(b, 1), :])
        wide = jnp.concatenate([jnp.broadcast_to(ih, (groups, B)), jnp.broadcast_to(il, (groups, B))], 0)
        left = jnp.where(lax.rem(iota((2 * groups, B), 0), groups) == hi, wide, 0.0).astype(BF16)
        right = (li == lo).astype(BF16)
        return both + lax.dot_general(left, right, NT, preferred_element_type=F32)

    both = lax.fori_loop(0, shard_blocks, spread, jnp.zeros((2 * groups, B), F32), unroll=2)
    base_own[...] = (both[:groups] + both[groups:]).reshape(base_own.shape)
    base_copies = []
    for i, p in enumerate(peers):
        copy = pltpu.make_async_remote_copy(
            src_ref=base_own.at[p], dst_ref=base_parts.at[me], send_sem=g_send.at[i], recv_sem=g_recv.at[i],
            device_id={"tm": p}, device_id_type=MESH,
        )
        copy.start()
        base_copies.append(copy)
    base_parts[me] = base_own[me]

    for copy in back_copies:
        copy.wait()
    pending = jnp.zeros((count, B), F32)
    comp_all = jnp.zeros((8, B), F32)
    for p in reversed(range(half)):
        span = summaries[p, count : count + 1, :]
        pending = jnp.where(p > q, pending * jnp.exp(-d8 * span) + back[p, 0:count, :], pending)
        comp_all = comp_all + back[p, count:, :]
    reverse_state(pending, True)
    events_all = blocks * B * half
    minus[...] = jnp.where(lane < edge, comp_all * (1.0 / events_all), 0.0)

    row8 = iota((8, B), 0)

    def thirds(a, places):
        high, rest = halves(a)
        mid, low = halves(rest)
        out = jnp.zeros((8, B), F32)
        for term, where in zip((high, mid, low), places):
            for k in where:
                out = jnp.where(row8 == k, term, out)
        return out

    xstack = thirds(xtot * (-1.0 / types), ((0, 2, 5), (1, 4), (3,)))
    fill24 = jnp.zeros((B - 3 * width - 8, B), F32)

    def feedback(b):
        s = rows_at(b, B)
        ur, er, ir = u[pl.ds(b, 1), :], te[pl.ds(b, 1), :], inverse[pl.ds(b, 1), :]
        high, low = halves(jnp.where(subi < subj, sym[rows_at(b, SUB), :] * ir, 0.0))
        left = jnp.concatenate([parted(high), parted(low)], 0).astype(BF16)
        both = dot(left, rows[s, :].astype(BF16))
        lh, ll = halves(parted(w8 * jnp.exp(-d8 * (er - ur))))
        rstack = thirds(remain[pl.ds(b, 1), :], ((0, 1, 3), (2, 4), (5,)))
        turn = jnp.concatenate([lh, lh, ll, rstack, fill24], 0).T.astype(BF16)
        sh, sl = halves(states[rows_at(b, width), :])
        value = both[:B] + both[B:] + dot(
            turn, jnp.concatenate([sh, sl, sh, xstack, fill24], 0).astype(BF16)
        )
        return [(values, (s, slice(None)), jnp.where(lane < edge, excitation[s, :] * turned(ir), value))]

    def piece(g):
        s = rows_at(g, UNROLL * B)
        return pltpu.make_async_copy(values.at[s, :], values_out.at[s, :], out_sem.at[g])

    batched(blocks, UNROLL, feedback, lambda g: piece(g).start())

    for copy in base_copies:
        copy.wait()
    base_all = base_parts[0]
    for p in range(1, n):
        base_all = base_all + base_parts[p]
    grad_base[...] = base_all * (types / events_all) - t_end * (1.0 / events_all)
    for i, p in enumerate(dests):

        @pl.when(p != me)
        def _():
            for a in range(2):
                shard_copy(a, i, slot, p).wait_send()

    for g in range(blocks // UNROLL):
        piece(g).wait()


def scatter_kernel(marks, values_in, out, values, load_sem, out_sem, *tables):
    count = len(tables)
    types = out.shape[0]
    load = pltpu.make_async_copy(values_in, values, load_sem.at[0])
    load.start()

    def zero(i, _):
        for t in tables:
            t[rows_at(i, 32), :] = jnp.zeros((32, B), F32)
        return 0

    lax.fori_loop(0, types // 32, zero, 0)
    load.wait()
    shards, blocks, _ = marks.shape
    for j in range(shards):

        def block(b, _):
            for i in range(B):
                t = tables[i % count]
                m = marks[j, b, i]
                e = (j * blocks + b) * B + i
                t[pl.ds(m, 1), :] = t[pl.ds(m, 1), :] + values[pl.ds(e, 1), :]
            return 0

        lax.fori_loop(0, blocks, block, 0)

    pieces = out_sem.shape[0]
    size = types // pieces

    def piece(c):
        s = rows_at(c, size)
        return pltpu.make_async_copy(tables[0].at[s, :], out.at[s, :], out_sem.at[c])

    def total(c, _):
        def add(i, _):
            s = pl.ds(pl.multiple_of(c * size + i * 32, 32), 32)
            acc = [t[s, :] for t in tables]
            while len(acc) > 1:
                acc = [acc[i] + acc[i + 1] for i in range(0, len(acc), 2)]
            tables[0][s, :] = acc[0]
            return 0

        lax.fori_loop(0, size // 32, add, 0, unroll=2)
        piece(c).start()
        return 0

    lax.fori_loop(0, pieces, total, 0)
    for c in range(pieces):
        piece(c).wait()


def ring_kernel(n, factor, minus, source, grad_excite, grad_source, dense, load_sem, slots, pieces, twin_in, send, recv, t_send, t_recv):
    half = n // 2
    per = dense.shape[0] // n
    rows = per // 2
    edge = B // 2
    ranks = grad_excite.shape[0] // 2
    me = lax.axis_index("tm")
    r = lax.div(me, half)
    q = lax.rem(me, half)
    odd = lax.rem(q, 2)
    at = lax.div(q, 2) + odd * (lax.div(2 * half - 1 - q, 2) - lax.div(q, 2))
    twin = q + (1 - r) * half

    def member(place):
        c = lax.rem(place + 2 * half, half)
        return 2 * c + lax.div(c, half // 2) * (2 * half - 1 - 4 * c)

    towards = [member(at + 1) + r * half, member(at - 1) + r * half]
    load = pltpu.make_async_copy(source, dense, load_sem.at[0])
    load.start()
    barrier = pltpu.get_barrier_semaphore()
    for p in towards + [twin]:
        pl.semaphore_signal(barrier, inc=1, device_id={"tm": p}, device_id_type=MESH)
    pl.semaphore_wait(barrier, 3)

    def span(j, step):
        way, kind = j % 2, j // 2
        place = at + 1 + step if way else at - 1 - step
        where = (1 - r) if kind == 0 else r
        block = member(place) + where * half
        return pl.ds(pl.multiple_of(block * per + way * rows, 8), rows)

    def copy(j, step, source):
        return pltpu.make_async_remote_copy(
            src_ref=source, dst_ref=slots.at[j, step], send_sem=send.at[j, step], recv_sem=recv.at[j, step],
            device_id={"tm": towards[j % 2]}, device_id_type=MESH,
        )

    chains = range(4)
    for j in chains:
        copy(j, 0, source.at[span(j, 0), :]).start()
    load.wait()

    def step(s, _):
        for j in chains:
            held = slots.at[j, s - 1]
            copy(j, s - 1, held).wait_recv()
            held[...] += dense[span(j, s), :]
            copy(j, s, held).start()
        return 0

    lax.fori_loop(1, half - 1, step, 0)

    def twin_copy(j):
        return pltpu.make_async_remote_copy(
            src_ref=pieces.at[j], dst_ref=twin_in.at[j], send_sem=t_send.at[j], recv_sem=t_recv.at[j],
            device_id={"tm": twin}, device_id_type=MESH,
        )

    for j in chains:
        copy(j, half - 2, slots.at[j, half - 2]).wait_recv()
        pieces[j] = (slots[j, half - 2] + dense[span(j, half - 1), :]) * factor - minus[0:1, :]
        if j < 2:
            twin_copy(j).start()
    low = r == 0
    for j in range(2):
        twin_copy(j).wait_recv()
        for i in range(rows // B):
            s = slice(i * B, (i + 1) * B)
            mine, their = pieces[2 + j, s, :].T, twin_in[j, s, :].T
            first = jnp.where(low, mine, their)
            second = jnp.where(low, their, mine)
            t = slice(j * rows + i * B, j * rows + (i + 1) * B)
            grad_excite[:ranks, t] = first[:ranks]
            grad_excite[ranks:, t] = second[:ranks]
            grad_source[:ranks, t] = first[edge : edge + ranks]
            grad_source[ranks:, t] = second[edge : edge + ranks]

    def sent(s, _):
        for j in chains:
            copy(j, s, slots.at[j, s]).wait_send()
        return 0

    lax.fori_loop(0, half - 1, sent, 0)
    for j in range(2):
        twin_copy(j).wait_send()


def square_kernel(
    n, factor, minus, source, grad_excite, grad_source,
    dense, load_sem, first, second, pieces, twin_in, a_send, a_recv, b_send, b_recv, t_send, t_recv,
):
    half = n // 2
    per = source.shape[0] // n
    rows = per // 4
    edge = B // 2
    ranks = grad_excite.shape[0] // 2
    me = lax.axis_index("tm")
    r = lax.div(me, half)
    q = lax.rem(me, half)
    qa, qb = lax.div(q, 2), lax.rem(q, 2)
    near = r * half + qa * 2 + 1 - qb
    far = r * half + (1 - qa) * 2 + qb
    twin = q + (1 - r) * half
    load = pltpu.make_async_copy(source, dense, load_sem.at[0])
    load.start()
    barrier = pltpu.get_barrier_semaphore()
    for p in (near, far, twin):
        pl.semaphore_signal(barrier, inc=1, device_id={"tm": p}, device_id_type=MESH)
    pl.semaphore_wait(barrier, 3)

    def span(j, a, b):
        block = a * 2 + b + ((1 - r) if j < 4 else r) * half
        return pl.ds(pl.multiple_of(block * per + (j % 4) * rows, 8), rows)

    def across(j):
        return j % 4 == 3

    def place(j, k, theirs):
        if across(j):
            return span(j, 1 - qa if theirs else qa, qb if k else 1 - qb)
        return span(j, qa if k else 1 - qa, 1 - qb if theirs else qb)

    def copy_a(j, k):
        return pltpu.make_async_remote_copy(
            src_ref=source.at[place(j, k, True), :], dst_ref=first.at[j, k],
            send_sem=a_send.at[j, k], recv_sem=a_recv.at[j, k],
            device_id={"tm": far if across(j) else near}, device_id_type=MESH,
        )

    def copy_b(j):
        return pltpu.make_async_remote_copy(
            src_ref=first.at[j, 0], dst_ref=second.at[j], send_sem=b_send.at[j], recv_sem=b_recv.at[j],
            device_id={"tm": near if across(j) else far}, device_id_type=MESH,
        )

    def copy_t(j):
        return pltpu.make_async_remote_copy(
            src_ref=pieces.at[j], dst_ref=twin_in.at[j], send_sem=t_send.at[j], recv_sem=t_recv.at[j],
            device_id={"tm": twin}, device_id_type=MESH,
        )

    def begin(j):
        for k in range(2):
            copy_a(j, k).start()

    def middle(j):
        copy_a(j, 0).wait_recv()
        first[j, 0] = first[j, 0] + dense[place(j, 0, False), :]
        copy_b(j).start()
        copy_a(j, 1).wait_recv()

    def put(value, j, who):
        for i in range(rows // B):
            t = value[i * B : (i + 1) * B].T
            lanes = slice((j % 4) * rows + i * B, (j % 4) * rows + (i + 1) * B)
            at = pl.ds(pl.multiple_of(who * ranks, ranks), ranks)
            grad_excite[at, lanes] = t[:ranks]
            grad_source[at, lanes] = t[edge : edge + ranks]

    def last(j):
        copy_b(j).wait_recv()
        value = (second[j] + first[j, 1] + dense[place(j, 1, False), :]) * factor - minus[0:1, :]
        if j < 4:
            pieces[j] = value
            copy_t(j).start()
        else:
            put(value, j, r)

    begin(0)
    begin(3)
    begin(1)
    load.wait()
    middle(0)
    begin(2)
    middle(3)
    begin(7)
    middle(1)
    begin(4)
    last(0)
    middle(2)
    begin(5)
    last(3)
    last(1)
    middle(4)
    begin(6)
    last(2)
    middle(7)
    middle(5)
    last(4)
    last(7)
    middle(6)
    last(5)
    for j in (0, 3, 1):
        copy_t(j).wait_recv()
        put(twin_in[j], j, 1 - r)
    last(6)
    copy_t(2).wait_recv()
    put(twin_in[2], 2, 1 - r)
    for j in range(8):
        for k in range(2):
            copy_a(j, k).wait_send()
        copy_b(j).wait_send()
    for j in range(4):
        copy_t(j).wait_send()


def body(marks, gaps, excite, source, base_rate, weights, decay):
    shard = marks.shape[0]
    slices, types = excite.shape
    n = lax.axis_size("tm")
    lanes_n = lax.axis_size("mark")
    half = n // 2
    rank = slices * lanes_n
    count = decay.shape[0]
    shard_blocks = shard // B
    blocks = 2 * shard_blocks
    events = 2 * shard
    groups = types // B
    width = count * PARTS
    dma = pltpu.SemaphoreType.DMA
    plane = pltpu.VMEM((blocks, B), F32)
    tall = pltpu.VMEM((events, B), F32)
    small = pltpu.VMEM((blocks * width, B), F32)
    packet = pltpu.VMEM((count + 8, B), F32)
    packets = pltpu.VMEM((half, count + 8, B), F32)
    types_own = types // n

    values, grad_base, minus, marks_all = pl.pallas_call(
        functools.partial(front_kernel, n, lanes_n, rank),
        out_shape=[
            jax.ShapeDtypeStruct((events, B), F32),
            jax.ShapeDtypeStruct((groups // n, B), F32),
            jax.ShapeDtypeStruct((8, B), F32),
            jax.ShapeDtypeStruct((2, shard_blocks, B), jnp.int32),
        ],
        in_specs=[SMEM, SMEM, VMEM, VMEM, HBM, HBM, VMEM],
        out_specs=[HBM] + [VMEM] * 3,
        scratch_shapes=[
            pltpu.VMEM((B, types), BF16),
            pltpu.VMEM((types, B), F32),
            tall,
            pltpu.SMEM((2, shard_blocks, B), jnp.int32),
            pltpu.VMEM((shard_blocks, B), jnp.int32),
            pltpu.VMEM((2, shard_blocks, B), jnp.int32),
            plane, plane, plane,
            pltpu.VMEM((blocks * SUB, B), F32),
            tall, tall,
            pltpu.VMEM((events, B), BF16),
            small, small, small,
            plane, plane, plane, plane,
            packet, packets,
            plane, pltpu.VMEM((2 * lanes_n, blocks, B), F32),
            packets, packet,
            pltpu.VMEM((n, groups // n, B), F32),
            pltpu.VMEM((n, groups // n, B), F32),
            dma((2,)), dma((1,)),
            dma((2, 2)), dma((2, 2)),
            dma((half - 1,)), dma((half - 1,)),
            dma((2 * lanes_n - 1,)), dma((2 * lanes_n - 1,)),
            dma((half - 1,)), dma((half - 1,)),
            dma((n - 1,)), dma((n - 1,)),
            tall, dma((blocks // UNROLL,)),
        ],
        compiler_params=pltpu.CompilerParams(
            collective_id=0, has_side_effects=True, vmem_limit_bytes=ALL_VMEM
        ),
    )(weights, decay, marks.reshape(shard_blocks, B), gaps.reshape(shard_blocks, B), source, excite,
      base_rate.reshape(groups, B))

    dense = pl.pallas_call(
        scatter_kernel,
        out_shape=jax.ShapeDtypeStruct((types, B), F32),
        in_specs=[SMEM, HBM],
        out_specs=HBM,
        scratch_shapes=[tall, dma((1,)), dma((8,))] + [pltpu.VMEM((types, B), F32)] * 8,
        compiler_params=pltpu.CompilerParams(vmem_limit_bytes=ALL_VMEM),
    )(marks_all, values)

    quarter = types_own // 4
    if half == 4 and quarter % B == 0:
        kernel = square_kernel
        scratch = [
            pltpu.VMEM((8, 2, quarter, B), F32),
            pltpu.VMEM((8, quarter, B), F32),
            pltpu.VMEM((4, quarter, B), F32),
            pltpu.VMEM((4, quarter, B), F32),
            dma((8, 2)), dma((8, 2)), dma((8,)), dma((8,)), dma((4,)), dma((4,)),
        ]
    else:
        kernel = ring_kernel
        scratch = [
            pltpu.VMEM((4, half - 1, types_own // 2, B), F32),
            pltpu.VMEM((4, types_own // 2, B), F32),
            pltpu.VMEM((2, types_own // 2, B), F32),
            dma((4, half - 1)), dma((4, half - 1)), dma((2,)), dma((2,)),
        ]
    grad_excite, grad_source = pl.pallas_call(
        functools.partial(kernel, n, types / (events * half)),
        out_shape=[jax.ShapeDtypeStruct((slices, types_own), F32)] * 2,
        in_specs=[VMEM, HBM],
        out_specs=[VMEM] * 2,
        scratch_shapes=[pltpu.VMEM((types, B), F32), dma((1,))] + scratch,
        compiler_params=pltpu.CompilerParams(
            collective_id=1, has_side_effects=True, vmem_limit_bytes=52 * 2**20
        ),
    )(minus, dense)
    return grad_excite, grad_source, grad_base.reshape(types_own)


def solution(mesh):
    return jax.shard_map(
        body,
        mesh=mesh,
        in_specs=(P("tm"), P("tm"), P("mark", None), P("mark", None), P(), P(), P()),
        out_specs=(P("mark", "tm"), P("mark", "tm"), P("tm")),
        check_vma=False,
    )
```

```python
import functools

import jax
import jax.numpy as jnp
from jax import lax
from jax.experimental import pallas as pl
from jax.experimental.pallas import tpu as pltpu
from jax.sharding import PartitionSpec as P

F32 = jnp.float32
BF16 = jnp.bfloat16
B = 128
SUB = 32
UNROLL = 16
ALL_VMEM = 60 * 2**20
PARTS = B // SUB
HIGH = lax.Precision.HIGHEST
MESH = pl.DeviceIdType.MESH
VMEM = pl.BlockSpec(memory_space=pltpu.VMEM)
SMEM = pl.BlockSpec(memory_space=pltpu.SMEM)
HBM = pl.BlockSpec(memory_space=pltpu.HBM)
NT = (((1,), (1,)), ((), ()))


def iota(shape, axis):
    return lax.broadcasted_iota(jnp.int32, shape, axis)


def dot(a, b):
    return jnp.dot(a, b, preferred_element_type=F32)


def halves(a):
    high = a.astype(BF16).astype(F32)
    return high, a - high


def down(ref, count):
    row = iota((count, B), 0)
    out = jnp.zeros((count, B), F32)
    for k in range(count):
        out = jnp.where(row == k, ref[k], out)
    return out


def parted(a):
    part = lax.div(iota(a.shape, 1), SUB)
    return jnp.concatenate([jnp.where(part == c, a, 0.0) for c in range(PARTS)], 0)


def turned(row):
    return jnp.broadcast_to(row, (B, B)).T


def batched(count, size, one, then=None):
    def body(g, _):
        stores = []
        for i in range(size):
            stores += one(g * size + i)
        for ref, where, value in stores:
            ref[where] = value
        if then is not None:
            then(g)
        return 0

    lax.fori_loop(0, count // size, body, 0)


def rows_at(b, size):
    return pl.ds(pl.multiple_of(b * size, size), size)


def front_kernel(
    n, lanes_n, rank,
    weights, decay, marks, gaps, src, exc, base,
    values_out, grad_base, minus, marks_out,
    factors, table, rows, smarks, own, gshard, u, te, ts, sym, inside, excitation, lanes, states, sums, dec, base_e,
    inverse, remain, ends, device, summaries, partial, total, back, behind, base_own, base_parts,
    load_sem, mark_sem, ag_send, ag_recv, f_send, f_recv, p_send, p_recv, b_send, b_recv, g_send, g_recv, values, out_sem,
):
    count = decay.shape[0]
    width = count * PARTS
    half = n // 2
    shard_blocks = marks.shape[0]
    blocks = 2 * shard_blocks
    types = table.shape[0]
    groups = types // B
    ranks = src.shape[0] // 2
    edge = B // 2
    me = lax.axis_index("tm")
    mine = lax.axis_index("mark")
    r = lax.div(me, half)
    q = lax.rem(me, half)
    peers = [lax.rem(me + i, n) for i in range(1, n)]
    mates = [r * half + lax.rem(q + i, half) for i in range(1, half)]
    others = [lax.rem(mine + i, lanes_n) for i in range(1, lanes_n)]
    twin = q + (1 - r) * half

    if ranks < edge:
        for a in range(2):
            factors[a * edge + ranks : (a + 1) * edge, :] = jnp.zeros((edge - ranks, types), BF16)
    loads = []
    for a, ref in enumerate((src, exc)):
        copy = pltpu.make_async_copy(
            ref.at[pl.ds(pl.multiple_of(r * ranks, ranks), ranks), :],
            factors.at[a * edge : a * edge + ranks, :],
            load_sem.at[a],
        )
        copy.start()
        loads.append(copy)

    barrier = pltpu.get_barrier_semaphore()
    targets = [{"tm": p, "mark": mine} for p in peers]
    targets += [{"tm": t, "mark": o} for o in others for t in (me, twin)]
    for t in targets:
        pl.semaphore_signal(barrier, inc=1, device_id=t, device_id_type=MESH)
    pl.semaphore_wait(barrier, len(targets))

    own[...] = marks[...]
    marks_out[r] = marks[...]
    gshard[r] = gaps[...]
    first_move = pltpu.make_async_copy(own, smarks.at[r], mark_sem.at[0])
    first_move.start()
    gathers = []
    for a, (ref, dst) in enumerate(((own, marks_out), (gaps, gshard))):
        copy = pltpu.make_async_remote_copy(
            src_ref=ref, dst_ref=dst.at[r], send_sem=ag_send.at[a], recv_sem=ag_recv.at[a],
            device_id={"tm": twin}, device_id_type=MESH,
        )
        copy.start()
        gathers.append(copy)

    for copy in loads:
        copy.wait()

    def build(c, acc):
        s = rows_at(c, B)
        t = factors[:, s].astype(F32).T
        table[s, :] = t
        return acc + jnp.sum(t.reshape(B // 8, 8, B), axis=0)

    acc = lax.fori_loop(0, groups, build, jnp.zeros((8, B), F32), unroll=8)
    xtot = jnp.sum(acc, axis=0, keepdims=True)

    d8, w8 = down(decay, count), down(weights, count)
    li, lj = iota((B, B), 0), iota((B, B), 1)
    start_lane = lax.div(lj, SUB) * SUB
    part_row = lax.div(iota((1, B), 1), SUB)
    lane = iota((1, B), 1)

    def pick(mask, a):
        return jnp.dot(a, mask.astype(F32), precision=HIGH, preferred_element_type=F32)

    def two(a, b):
        k = a.shape[0]
        high, low = halves(a)
        both = dot(jnp.concatenate([high, low], 0).astype(BF16), b)
        return both[:k] + both[k:]

    def prepare(j):
        gap = gshard[j].astype(F32)
        uv = pick(li <= lj, gap)
        at = rows_at(j, shard_blocks)
        u[at, :] = uv
        te[at, :] = pick(li <= start_lane + SUB - 1, gap)
        ts[at, :] = pick(li < start_lane, gap)
        lengths = jnp.broadcast_to(uv[:, B - 1 :], (shard_blocks, B))
        later = (iota((shard_blocks, shard_blocks), 1) > iota((shard_blocks, shard_blocks), 0)).astype(F32)
        left = jnp.dot(later, lengths, precision=HIGH, preferred_element_type=F32)
        ends[at, :] = left
        device[j, count:, :] = jnp.broadcast_to(left[0:1, :] + lengths[0:1, :], (8, B))

    def fetch(j):
        def block(b, _):
            for i in range(B):
                m = smarks[j, b, i]
                rows[pl.ds((j * shard_blocks + b) * B + i, 1), :] = table[pl.ds(m, 1), :]
            return 0

        lax.fori_loop(0, shard_blocks, block, 0)

    def emit(b):
        ur, er, sr = u[pl.ds(b, 1), :], te[pl.ds(b, 1), :], ts[pl.ds(b, 1), :]
        vals = rows[rows_at(b, B), :].astype(BF16)
        span = er - sr
        decays = [jnp.exp(-d8 * span[:, c * SUB : c * SUB + 1]) for c in range(PARTS)]
        spot = (rows_at(b, width), slice(None))
        return [
            (sums, spot, two(parted(d8 * jnp.exp(-d8 * (er - ur))), vals)),
            (dec, spot, jnp.concatenate([jnp.broadcast_to(t, (count, B)) for t in decays], 0)),
        ]

    prepare(r)
    first_move.wait()
    fetch(r)
    batched(shard_blocks, UNROLL, lambda b: emit(r * shard_blocks + b))
    for copy in gathers:
        copy.wait_recv()
    second_move = pltpu.make_async_copy(marks_out.at[1 - r], smarks.at[1 - r], mark_sem.at[1])
    second_move.start()
    prepare(1 - r)
    second_move.wait()
    fetch(1 - r)
    batched(shard_blocks, UNROLL, lambda b: emit((1 - r) * shard_blocks + b))

    zero = jnp.zeros((count, B), F32)

    def recur(start, keep, ahead):
        def step(i, pair):
            b = i if ahead else shard_blocks - 1 - i
            for c in range(PARTS) if ahead else reversed(range(PARTS)):
                nxt = []
                for j in range(2):
                    s = pl.ds(pl.multiple_of((j * shard_blocks + b) * width + c * count, count), count)
                    if keep:
                        states[s, :] = pair[j]
                    nxt.append(pair[j] * dec[s, :] + sums[s, :])
                pair = tuple(nxt)
            return pair

        return lax.fori_loop(0, shard_blocks, step, start, unroll=2)

    def share(source, dest, send, recv):
        copies = []
        for i, p in enumerate(mates):
            copies.append(
                pltpu.make_async_remote_copy(
                    src_ref=source, dst_ref=dest.at[q], send_sem=send.at[i], recv_sem=recv.at[i],
                    device_id={"tm": p}, device_id_type=MESH,
                )
            )
        for copy in copies:
            copy.start()
        dest[q] = source[...]
        return copies

    for j, state in enumerate(recur((zero, zero), False, True)):
        device[j, 0:count, :] = state
    state_copies = share(device, summaries, f_send, f_recv)

    base_high, base_low = halves(base[...])
    base2 = jnp.concatenate([base_high, base_low], 0).T.astype(BF16)
    subi = iota((SUB, B), 0)
    subj = lax.rem(iota((SUB, B), 1), SUB)

    def mark_row(b):
        return marks_out[lax.div(b, shard_blocks), pl.ds(lax.rem(b, shard_blocks), 1), :]

    def within(b):
        ur, sr = u[pl.ds(b, 1), :], ts[pl.ds(b, 1), :]
        s = rows_at(b, B)
        col = turned(ur)
        colc = col[0:SUB]
        for c in range(1, PARTS):
            colc = jnp.where(part_row == c, col[c * SUB : (c + 1) * SUB], colc)
        apart = jnp.abs(colc - ur)
        g = jnp.zeros((SUB, B), F32)
        for k in range(count):
            g = g + (weights[k] * decay[k]) * jnp.exp(-decay[k] * apart)
        high, low = halves(jnp.where(subi > subj, g, 0.0))
        left = jnp.concatenate([parted(high), parted(low)], 0).astype(BF16)
        both = dot(left, rows[s, :].astype(BF16))
        lh, ll = halves(parted(w8 * jnp.exp(-d8 * (ur - sr))))
        stack = jnp.concatenate([lh, lh, ll, jnp.zeros((B - 3 * width, B), F32)], 0)
        m = mark_row(b)
        hi, lo = lax.div(m, B), lax.rem(m, B)
        onehot = (lax.rem(iota((2 * groups, B), 0), groups) == hi).astype(BF16)
        found = dot(base2, onehot)
        return [
            (sym, (rows_at(b, SUB), slice(None)), g),
            (inside, (s, slice(None)), both[:B] + both[B:]),
            (lanes, (s, slice(None)), stack.T.astype(BF16)),
            (base_e, (pl.ds(b, 1), slice(None)), jnp.sum(jnp.where(li == lo, found, 0.0), axis=0, keepdims=True)),
        ]

    batched(blocks, UNROLL, within)

    for copy in state_copies:
        copy.wait()
    start = [zero, zero]
    after = [jnp.zeros((1, B), F32)] * 2
    t_end = jnp.zeros((1, B), F32)
    for t in range(n):
        held = summaries[t % half, t // half]
        span = held[count : count + 1]
        t_end = t_end + span
        for j in range(2):
            mark = q + j * half
            start[j] = jnp.where(t < mark, start[j] * jnp.exp(-d8 * span) + held[0:count], start[j])
            after[j] = after[j] + jnp.where(t > mark, span, 0.0)
    recur(tuple(start), True, True)
    for j in range(2):
        at = slice(j * shard_blocks, (j + 1) * shard_blocks)
        ends[at, :] = ends[at, :] + after[j]

    fill = jnp.zeros((B - 3 * width, B), F32)

    def forward(b):
        s = rows_at(b, B)
        sh, sl = halves(states[rows_at(b, width), :])
        value = inside[s, :] + dot(lanes[s, :], jnp.concatenate([sh, sl, sh, fill], 0).astype(BF16))
        product = value * pltpu.roll(rows[s, :], edge, 1)
        tot = jnp.sum(product.T[:edge], axis=0, keepdims=True)
        return [
            (excitation, (s, slice(None)), value),
            (partial, (pl.ds(b, 1), slice(None)), tot * (1.0 / rank)),
        ]

    spot = mine * 2 + r

    def part_copies(g):
        s = rows_at(g, UNROLL)
        copies = []
        for i, t in enumerate([(twin, mine)] + [(t, o) for o in others for t in (me, twin)]):
            copies.append(
                pltpu.make_async_remote_copy(
                    src_ref=partial.at[s, :], dst_ref=total.at[spot, s, :],
                    send_sem=p_send.at[i, g], recv_sem=p_recv.at[i, g],
                    device_id={"tm": t[0], "mark": t[1]}, device_id_type=MESH,
                )
            )
        return copies

    def send_part(g):
        for copy in part_copies(g):
            copy.start()

    batched(blocks, UNROLL, forward, send_part)
    total[spot] = partial[...]

    def rest(b, comp):
        left = w8 * (1.0 - jnp.exp(-d8 * (u[pl.ds(b, 1), :] * -1.0 + lengths_row(b) + ends[pl.ds(b, 1), :])))
        rem = jnp.sum(left, axis=0, keepdims=True)
        remain[pl.ds(b, 1), :] = rem
        return comp + two(jnp.broadcast_to(rem, (8, B)), rows[rows_at(b, B), :].astype(BF16))

    def lengths_row(b):
        return u[pl.ds(b, 1), B - 1 :]

    comp = lax.fori_loop(0, blocks, rest, jnp.zeros((8, B), F32), unroll=4)

    for g in range(blocks // UNROLL):
        for copy in part_copies(g):
            copy.wait()
    intensity = base_e[...]
    for j in range(2 * lanes_n):
        intensity = intensity + total[j]
    inverse[...] = 1.0 / intensity

    def reverse(b):
        e8 = d8 * jnp.exp(-d8 * (u[pl.ds(b, 1), :] - ts[pl.ds(b, 1), :])) * inverse[pl.ds(b, 1), :]
        return [(sums, (rows_at(b, width), slice(None)), two(parted(e8), rows[rows_at(b, B), :].astype(BF16)))]

    batched(blocks, UNROLL, reverse)

    for j, state in enumerate(recur((zero, zero), False, False)):
        behind[j * count : (j + 1) * count, :] = state
    behind[2 * count :, :] = comp
    back_copies = share(behind, back, b_send, b_recv)

    def spread(i, both):
        b = r * shard_blocks + i
        m = mark_row(b)
        hi, lo = lax.div(m, B), lax.rem(m, B)
        ih, il = halves(inverse[pl.ds(b, 1), :])
        wide = jnp.concatenate([jnp.broadcast_to(ih, (groups, B)), jnp.broadcast_to(il, (groups, B))], 0)
        left = jnp.where(lax.rem(iota((2 * groups, B), 0), groups) == hi, wide, 0.0).astype(BF16)
        right = (li == lo).astype(BF16)
        return both + lax.dot_general(left, right, NT, preferred_element_type=F32)

    both = lax.fori_loop(0, shard_blocks, spread, jnp.zeros((2 * groups, B), F32), unroll=2)
    base_own[...] = (both[:groups] + both[groups:]).reshape(base_own.shape)
    base_copies = []
    for i, p in enumerate(peers):
        copy = pltpu.make_async_remote_copy(
            src_ref=base_own.at[p], dst_ref=base_parts.at[me], send_sem=g_send.at[i], recv_sem=g_recv.at[i],
            device_id={"tm": p}, device_id_type=MESH,
        )
        copy.start()
        base_copies.append(copy)
    base_parts[me] = base_own[me]

    def feedback(b):
        s = rows_at(b, B)
        ir = inverse[pl.ds(b, 1), :]
        high, low = halves(jnp.where(subi < subj, sym[rows_at(b, SUB), :] * ir, 0.0))
        left = jnp.concatenate([parted(high), parted(low)], 0).astype(BF16)
        both = dot(left, rows[s, :].astype(BF16))
        return [(inside, (s, slice(None)), jnp.where(lane < edge, excitation[s, :] * turned(ir), both[:B] + both[B:]))]

    batched(blocks, UNROLL, feedback)

    for copy in back_copies:
        copy.wait()
    pending = [zero, zero]
    comp_all = jnp.zeros((8, B), F32)
    for p in range(half):
        comp_all = comp_all + back[p, 2 * count :, :]
    for t in reversed(range(n)):
        p, k = t % half, t // half
        span = summaries[p, k, count : count + 1, :]
        for j in range(2):
            pending[j] = jnp.where(
                t > q + j * half,
                pending[j] * jnp.exp(-d8 * span) + back[p, k * count : (k + 1) * count, :],
                pending[j],
            )
    recur(tuple(pending), True, False)
    events_all = blocks * B * half
    minus[...] = jnp.where(lane < edge, comp_all * (1.0 / events_all), 0.0)

    row8 = iota((8, B), 0)

    def thirds(a, places):
        high, rest = halves(a)
        mid, low = halves(rest)
        out = jnp.zeros((8, B), F32)
        for term, where in zip((high, mid, low), places):
            for k in where:
                out = jnp.where(row8 == k, term, out)
        return out

    xstack = thirds(xtot * (-1.0 / types), ((0, 2, 5), (1, 4), (3,)))
    fill24 = jnp.zeros((B - 3 * width - 8, B), F32)

    def distant(b):
        s = rows_at(b, B)
        lh, ll = halves(parted(w8 * jnp.exp(-d8 * (te[pl.ds(b, 1), :] - u[pl.ds(b, 1), :]))))
        rstack = thirds(remain[pl.ds(b, 1), :], ((0, 1, 3), (2, 4), (5,)))
        turn = jnp.concatenate([lh, lh, ll, rstack, fill24], 0).T.astype(BF16)
        sh, sl = halves(states[rows_at(b, width), :])
        stack = jnp.concatenate([sh, sl, sh, xstack, fill24], 0)
        value = dot(turn, jnp.where(lane < edge, 0.0, stack).astype(BF16))
        return [(values, (s, slice(None)), inside[s, :] + value)]

    def piece(g):
        s = rows_at(g, UNROLL * B)
        return pltpu.make_async_copy(values.at[s, :], values_out.at[s, :], out_sem.at[g])

    batched(blocks, UNROLL, distant, lambda g: piece(g).start())

    for copy in base_copies:
        copy.wait()
    base_all = base_parts[0]
    for p in range(1, n):
        base_all = base_all + base_parts[p]
    grad_base[...] = base_all * (types / events_all) - t_end * (1.0 / events_all)
    for copy in gathers:
        copy.wait_send()
    for g in range(blocks // UNROLL):
        piece(g).wait()


def scatter_kernel(marks, values_in, out, values, load_sem, out_sem, *tables):
    count = len(tables)
    types = out.shape[0]
    load = pltpu.make_async_copy(values_in, values, load_sem.at[0])
    load.start()

    def zero(i, _):
        for t in tables:
            t[rows_at(i, 32), :] = jnp.zeros((32, B), F32)
        return 0

    lax.fori_loop(0, types // 32, zero, 0)
    load.wait()
    shards, blocks, _ = marks.shape
    for j in range(shards):

        def block(b, _):
            for i in range(B):
                t = tables[i % count]
                m = marks[j, b, i]
                e = (j * blocks + b) * B + i
                t[pl.ds(m, 1), :] = t[pl.ds(m, 1), :] + values[pl.ds(e, 1), :]
            return 0

        lax.fori_loop(0, blocks, block, 0)

    pieces = out_sem.shape[0]
    size = types // pieces

    def piece(c):
        s = rows_at(c, size)
        return pltpu.make_async_copy(tables[0].at[s, :], out.at[s, :], out_sem.at[c])

    def total(c, _):
        def add(i, _):
            s = pl.ds(pl.multiple_of(c * size + i * 32, 32), 32)
            acc = [t[s, :] for t in tables]
            while len(acc) > 1:
                acc = [acc[i] + acc[i + 1] for i in range(0, len(acc), 2)]
            tables[0][s, :] = acc[0]
            return 0

        lax.fori_loop(0, size // 32, add, 0, unroll=2)
        piece(c).start()
        return 0

    lax.fori_loop(0, pieces, total, 0)
    for c in range(pieces):
        piece(c).wait()


def ring_kernel(n, factor, minus, source, grad_excite, grad_source, dense, load_sem, slots, pieces, twin_in, send, recv, t_send, t_recv):
    half = n // 2
    per = dense.shape[0] // n
    rows = per // 2
    edge = B // 2
    ranks = grad_excite.shape[0] // 2
    me = lax.axis_index("tm")
    r = lax.div(me, half)
    q = lax.rem(me, half)
    odd = lax.rem(q, 2)
    at = lax.div(q, 2) + odd * (lax.div(2 * half - 1 - q, 2) - lax.div(q, 2))
    twin = q + (1 - r) * half

    def member(place):
        c = lax.rem(place + 2 * half, half)
        return 2 * c + lax.div(c, half // 2) * (2 * half - 1 - 4 * c)

    towards = [member(at + 1) + r * half, member(at - 1) + r * half]
    load = pltpu.make_async_copy(source, dense, load_sem.at[0])
    load.start()
    barrier = pltpu.get_barrier_semaphore()
    for p in towards + [twin]:
        pl.semaphore_signal(barrier, inc=1, device_id={"tm": p}, device_id_type=MESH)
    pl.semaphore_wait(barrier, 3)

    def span(j, step):
        way, kind = j % 2, j // 2
        place = at + 1 + step if way else at - 1 - step
        where = (1 - r) if kind == 0 else r
        block = member(place) + where * half
        return pl.ds(pl.multiple_of(block * per + way * rows, 8), rows)

    def copy(j, step, source):
        return pltpu.make_async_remote_copy(
            src_ref=source, dst_ref=slots.at[j, step], send_sem=send.at[j, step], recv_sem=recv.at[j, step],
            device_id={"tm": towards[j % 2]}, device_id_type=MESH,
        )

    chains = range(4)
    for j in chains:
        copy(j, 0, source.at[span(j, 0), :]).start()
    load.wait()

    def step(s, _):
        for j in chains:
            held = slots.at[j, s - 1]
            copy(j, s - 1, held).wait_recv()
            held[...] += dense[span(j, s), :]
            copy(j, s, held).start()
        return 0

    lax.fori_loop(1, half - 1, step, 0)

    def twin_copy(j):
        return pltpu.make_async_remote_copy(
            src_ref=pieces.at[j], dst_ref=twin_in.at[j], send_sem=t_send.at[j], recv_sem=t_recv.at[j],
            device_id={"tm": twin}, device_id_type=MESH,
        )

    for j in chains:
        copy(j, half - 2, slots.at[j, half - 2]).wait_recv()
        pieces[j] = (slots[j, half - 2] + dense[span(j, half - 1), :]) * factor - minus[0:1, :]
        if j < 2:
            twin_copy(j).start()
    low = r == 0
    for j in range(2):
        twin_copy(j).wait_recv()
        for i in range(rows // B):
            s = slice(i * B, (i + 1) * B)
            mine, their = pieces[2 + j, s, :].T, twin_in[j, s, :].T
            first = jnp.where(low, mine, their)
            second = jnp.where(low, their, mine)
            t = slice(j * rows + i * B, j * rows + (i + 1) * B)
            grad_excite[:ranks, t] = first[:ranks]
            grad_excite[ranks:, t] = second[:ranks]
            grad_source[:ranks, t] = first[edge : edge + ranks]
            grad_source[ranks:, t] = second[edge : edge + ranks]

    def sent(s, _):
        for j in chains:
            copy(j, s, slots.at[j, s]).wait_send()
        return 0

    lax.fori_loop(0, half - 1, sent, 0)
    for j in range(2):
        twin_copy(j).wait_send()


def square_kernel(
    n, factor, minus, source, grad_excite, grad_source,
    dense, load_sem, first, second, pieces, twin_in, a_send, a_recv, b_send, b_recv, t_send, t_recv,
):
    half = n // 2
    per = source.shape[0] // n
    rows = per // 4
    edge = B // 2
    ranks = grad_excite.shape[0] // 2
    me = lax.axis_index("tm")
    r = lax.div(me, half)
    q = lax.rem(me, half)
    qa, qb = lax.div(q, 2), lax.rem(q, 2)
    near = r * half + qa * 2 + 1 - qb
    far = r * half + (1 - qa) * 2 + qb
    twin = q + (1 - r) * half
    load = pltpu.make_async_copy(source, dense, load_sem.at[0])
    load.start()
    barrier = pltpu.get_barrier_semaphore()
    for p in (near, far, twin):
        pl.semaphore_signal(barrier, inc=1, device_id={"tm": p}, device_id_type=MESH)
    pl.semaphore_wait(barrier, 3)

    def span(j, a, b):
        block = a * 2 + b + ((1 - r) if j < 4 else r) * half
        return pl.ds(pl.multiple_of(block * per + (j % 4) * rows, 8), rows)

    def across(j):
        return j % 4 == 3

    def place(j, k, theirs):
        if across(j):
            return span(j, 1 - qa if theirs else qa, qb if k else 1 - qb)
        return span(j, qa if k else 1 - qa, 1 - qb if theirs else qb)

    def copy_a(j, k):
        return pltpu.make_async_remote_copy(
            src_ref=source.at[place(j, k, True), :], dst_ref=first.at[j, k],
            send_sem=a_send.at[j, k], recv_sem=a_recv.at[j, k],
            device_id={"tm": far if across(j) else near}, device_id_type=MESH,
        )

    def copy_b(j):
        return pltpu.make_async_remote_copy(
            src_ref=first.at[j, 0], dst_ref=second.at[j], send_sem=b_send.at[j], recv_sem=b_recv.at[j],
            device_id={"tm": near if across(j) else far}, device_id_type=MESH,
        )

    def copy_t(j):
        return pltpu.make_async_remote_copy(
            src_ref=pieces.at[j], dst_ref=twin_in.at[j], send_sem=t_send.at[j], recv_sem=t_recv.at[j],
            device_id={"tm": twin}, device_id_type=MESH,
        )

    def begin(j):
        for k in range(2):
            copy_a(j, k).start()

    def middle(j):
        copy_a(j, 0).wait_recv()
        first[j, 0] = first[j, 0] + dense[place(j, 0, False), :]
        copy_b(j).start()

    def put(value, j, who):
        for i in range(rows // B):
            t = value[i * B : (i + 1) * B].T
            lanes = slice((j % 4) * rows + i * B, (j % 4) * rows + (i + 1) * B)
            at = pl.ds(pl.multiple_of(who * ranks, ranks), ranks)
            grad_excite[at, lanes] = t[:ranks]
            grad_source[at, lanes] = t[edge : edge + ranks]

    def last(j):
        copy_a(j, 1).wait_recv()
        copy_b(j).wait_recv()
        value = (second[j] + first[j, 1] + dense[place(j, 1, False), :]) * factor - minus[0:1, :]
        if j < 4:
            pieces[j] = value
            copy_t(j).start()
        else:
            put(value, j, r)

    copy_a(0, 0).start()
    copy_a(3, 0).start()
    copy_a(1, 0).start()
    copy_a(0, 1).start()
    copy_a(3, 1).start()
    load.wait()
    middle(0)
    copy_a(2, 0).start()
    copy_a(1, 1).start()
    middle(3)
    copy_a(7, 0).start()
    middle(1)
    copy_a(4, 0).start()
    copy_a(2, 1).start()
    last(0)
    middle(2)
    copy_a(5, 0).start()
    copy_a(7, 1).start()
    last(3)
    last(1)
    middle(4)
    copy_a(6, 0).start()
    copy_a(4, 1).start()
    last(2)
    middle(7)
    middle(5)
    copy_a(5, 1).start()
    copy_a(6, 1).start()
    last(4)
    last(7)
    middle(6)
    last(5)
    for j in (0, 3, 1):
        copy_t(j).wait_recv()
        put(twin_in[j], j, 1 - r)
    last(6)
    copy_t(2).wait_recv()
    put(twin_in[2], 2, 1 - r)
    for j in range(8):
        for k in range(2):
            copy_a(j, k).wait_send()
        copy_b(j).wait_send()
    for j in range(4):
        copy_t(j).wait_send()


def body(marks, gaps, excite, source, base_rate, weights, decay):
    shard = marks.shape[0]
    slices, types = excite.shape
    n = lax.axis_size("tm")
    lanes_n = lax.axis_size("mark")
    half = n // 2
    rank = slices * lanes_n
    count = decay.shape[0]
    shard_blocks = shard // B
    blocks = 2 * shard_blocks
    events = 2 * shard
    groups = types // B
    width = count * PARTS
    dma = pltpu.SemaphoreType.DMA
    plane = pltpu.VMEM((blocks, B), F32)
    tall = pltpu.VMEM((events, B), F32)
    small = pltpu.VMEM((blocks * width, B), F32)
    types_own = types // n

    values, grad_base, minus, marks_all = pl.pallas_call(
        functools.partial(front_kernel, n, lanes_n, rank),
        out_shape=[
            jax.ShapeDtypeStruct((events, B), F32),
            jax.ShapeDtypeStruct((groups // n, B), F32),
            jax.ShapeDtypeStruct((8, B), F32),
            jax.ShapeDtypeStruct((2, shard_blocks, B), jnp.int32),
        ],
        in_specs=[SMEM, SMEM, VMEM, VMEM, HBM, HBM, VMEM],
        out_specs=[HBM] + [VMEM] * 3,
        scratch_shapes=[
            pltpu.VMEM((B, types), BF16),
            pltpu.VMEM((types, B), F32),
            tall,
            pltpu.SMEM((2, shard_blocks, B), jnp.int32),
            pltpu.VMEM((shard_blocks, B), jnp.int32),
            pltpu.VMEM((2, shard_blocks, B), jnp.int32),
            plane, plane, plane,
            pltpu.VMEM((blocks * SUB, B), F32),
            tall, tall,
            pltpu.VMEM((events, B), BF16),
            small, small, small,
            plane, plane, plane, plane,
            pltpu.VMEM((2, count + 8, B), F32), pltpu.VMEM((half, 2, count + 8, B), F32),
            plane, pltpu.VMEM((2 * lanes_n, blocks, B), F32),
            pltpu.VMEM((half, 2 * count + 8, B), F32), pltpu.VMEM((2 * count + 8, B), F32),
            pltpu.VMEM((n, groups // n, B), F32),
            pltpu.VMEM((n, groups // n, B), F32),
            dma((2,)), dma((2,)),
            dma((2,)), dma((2,)),
            dma((half - 1,)), dma((half - 1,)),
            dma((2 * lanes_n - 1, blocks // UNROLL)), dma((2 * lanes_n - 1, blocks // UNROLL)),
            dma((half - 1,)), dma((half - 1,)),
            dma((n - 1,)), dma((n - 1,)),
            tall, dma((blocks // UNROLL,)),
        ],
        compiler_params=pltpu.CompilerParams(
            collective_id=0, has_side_effects=True, vmem_limit_bytes=ALL_VMEM
        ),
    )(weights, decay, marks.reshape(shard_blocks, B), gaps.reshape(shard_blocks, B), source, excite,
      base_rate.reshape(groups, B))

    dense = pl.pallas_call(
        scatter_kernel,
        out_shape=jax.ShapeDtypeStruct((types, B), F32),
        in_specs=[SMEM, HBM],
        out_specs=HBM,
        scratch_shapes=[tall, dma((1,)), dma((8,))] + [pltpu.VMEM((types, B), F32)] * 8,
        compiler_params=pltpu.CompilerParams(vmem_limit_bytes=ALL_VMEM),
    )(marks_all, values)

    quarter = types_own // 4
    if half == 4 and quarter % B == 0:
        kernel = square_kernel
        scratch = [
            pltpu.VMEM((8, 2, quarter, B), F32),
            pltpu.VMEM((8, quarter, B), F32),
            pltpu.VMEM((4, quarter, B), F32),
            pltpu.VMEM((4, quarter, B), F32),
            dma((8, 2)), dma((8, 2)), dma((8,)), dma((8,)), dma((4,)), dma((4,)),
        ]
    else:
        kernel = ring_kernel
        scratch = [
            pltpu.VMEM((4, half - 1, types_own // 2, B), F32),
            pltpu.VMEM((4, types_own // 2, B), F32),
            pltpu.VMEM((2, types_own // 2, B), F32),
            dma((4, half - 1)), dma((4, half - 1)), dma((2,)), dma((2,)),
        ]
    grad_excite, grad_source = pl.pallas_call(
        functools.partial(kernel, n, types / (events * half)),
        out_shape=[jax.ShapeDtypeStruct((slices, types_own), F32)] * 2,
        in_specs=[VMEM, HBM],
        out_specs=[VMEM] * 2,
        scratch_shapes=[pltpu.VMEM((types, B), F32), dma((1,))] + scratch,
        compiler_params=pltpu.CompilerParams(
            collective_id=1, has_side_effects=True, vmem_limit_bytes=52 * 2**20
        ),
    )(minus, dense)
    return grad_excite, grad_source, grad_base.reshape(types_own)


def solution(mesh):
    return jax.shard_map(
        body,
        mesh=mesh,
        in_specs=(P("tm"), P("tm"), P("mark", None), P("mark", None), P(), P(), P()),
        out_specs=(P("mark", "tm"), P("mark", "tm"), P("tm")),
        check_vma=False,
    )
```

```python
import functools

import jax
import jax.numpy as jnp
from jax import lax
from jax.experimental import pallas as pl
from jax.experimental.pallas import tpu as pltpu
from jax.sharding import PartitionSpec as P

F32 = jnp.float32
BF16 = jnp.bfloat16
B = 128
SUB = 32
UNROLL = 16
ALL_VMEM = 60 * 2**20
PARTS = B // SUB
HIGH = lax.Precision.HIGHEST
MESH = pl.DeviceIdType.MESH
VMEM = pl.BlockSpec(memory_space=pltpu.VMEM)
SMEM = pl.BlockSpec(memory_space=pltpu.SMEM)
HBM = pl.BlockSpec(memory_space=pltpu.HBM)
NT = (((1,), (1,)), ((), ()))


def iota(shape, axis):
    return lax.broadcasted_iota(jnp.int32, shape, axis)


def dot(a, b):
    return jnp.dot(a, b, preferred_element_type=F32)


def halves(a):
    high = a.astype(BF16).astype(F32)
    return high, a - high


def down(ref, count):
    row = iota((count, B), 0)
    out = jnp.zeros((count, B), F32)
    for k in range(count):
        out = jnp.where(row == k, ref[k], out)
    return out


def parted(a):
    part = lax.div(iota(a.shape, 1), SUB)
    return jnp.concatenate([jnp.where(part == c, a, 0.0) for c in range(PARTS)], 0)


def turned(row):
    return jnp.broadcast_to(row, (B, B)).T


def batched(count, size, one, then=None):
    def body(g, _):
        stores = []
        for i in range(size):
            stores += one(g * size + i)
        for ref, where, value in stores:
            ref[where] = value
        if then is not None:
            then(g)
        return 0

    lax.fori_loop(0, count // size, body, 0)


def rows_at(b, size):
    return pl.ds(pl.multiple_of(b * size, size), size)


def front_kernel(
    n, lanes_n, rank,
    weights_in, decay_in, marks_in, gaps_in, src, exc, base_in,
    values_out, base_out, minus_out, marks_all,
    factors, table, rows, smarks, own, gshard, u, te, ts, sym, inside, excitation, lanes, states, sums, dec, base_e,
    inverse, remain, ends, device, summaries, partial, total, back, behind, base_own, base_parts,
    load_sem, mark_sem, ag_send, ag_recv, f_send, f_recv, p_send, p_recv, b_send, b_recv, g_send, g_recv, values, out_sem,
    weights, decay, marks, gaps, base, grad_base, minus, marks_out, in_sem, end_sem,
):
    count = decay.shape[0]
    width = count * PARTS
    half = n // 2
    shard_blocks = marks.shape[0]
    blocks = 2 * shard_blocks
    types = table.shape[0]
    groups = types // B
    ranks = src.shape[0] // 2
    edge = B // 2
    me = lax.axis_index("tm")
    mine = lax.axis_index("mark")
    r = lax.div(me, half)
    q = lax.rem(me, half)
    peers = [lax.rem(me + i, n) for i in range(1, n)]
    mates = [r * half + lax.rem(q + i, half) for i in range(1, half)]
    others = [lax.rem(mine + i, lanes_n) for i in range(1, lanes_n)]
    twin = q + (1 - r) * half

    if ranks < edge:
        for a in range(2):
            factors[a * edge + ranks : (a + 1) * edge, :] = jnp.zeros((edge - ranks, types), BF16)
    barrier = pltpu.get_barrier_semaphore()
    targets = [{"tm": p, "mark": mine} for p in peers]
    targets += [{"tm": t, "mark": o} for o in others for t in (me, twin)]
    for t in targets:
        pl.semaphore_signal(barrier, inc=1, device_id=t, device_id_type=MESH)
    small = [
        pltpu.make_async_copy(a, b, in_sem.at[i])
        for i, (a, b) in enumerate(
            ((marks_in, marks), (gaps_in, gaps), (weights_in, weights), (decay_in, decay), (base_in, base))
        )
    ]
    for copy in small:
        copy.start()
    loads = []
    for a, ref in enumerate((src, exc)):
        copy = pltpu.make_async_copy(
            ref.at[pl.ds(pl.multiple_of(r * ranks, ranks), ranks), :],
            factors.at[a * edge : a * edge + ranks, :],
            load_sem.at[a],
        )
        copy.start()
        loads.append(copy)

    small[0].wait()
    small[1].wait()
    own[...] = marks[...]
    marks_out[r] = marks[...]
    gshard[r] = gaps[...]
    first_move = pltpu.make_async_copy(own, smarks.at[r], mark_sem.at[0])
    first_move.start()
    gathers = []
    pl.semaphore_wait(barrier, len(targets))
    for a, (ref, dst) in enumerate(((own, marks_out), (gaps, gshard))):
        copy = pltpu.make_async_remote_copy(
            src_ref=ref, dst_ref=dst.at[r], send_sem=ag_send.at[a], recv_sem=ag_recv.at[a],
            device_id={"tm": twin}, device_id_type=MESH,
        )
        copy.start()
        gathers.append(copy)

    for copy in loads:
        copy.wait()

    def build(c, acc):
        s = rows_at(c, B)
        t = factors[:, s].astype(F32).T
        table[s, :] = t
        return acc + jnp.sum(t.reshape(B // 8, 8, B), axis=0)

    acc = lax.fori_loop(0, groups, build, jnp.zeros((8, B), F32), unroll=8)
    xtot = jnp.sum(acc, axis=0, keepdims=True)

    for copy in small[2:]:
        copy.wait()
    d8, w8 = down(decay, count), down(weights, count)
    li, lj = iota((B, B), 0), iota((B, B), 1)
    start_lane = lax.div(lj, SUB) * SUB
    part_row = lax.div(iota((1, B), 1), SUB)
    lane = iota((1, B), 1)

    def pick(mask, a):
        return jnp.dot(a, mask.astype(F32), precision=HIGH, preferred_element_type=F32)

    def two(a, b):
        k = a.shape[0]
        high, low = halves(a)
        both = dot(jnp.concatenate([high, low], 0).astype(BF16), b)
        return both[:k] + both[k:]

    def prepare(j):
        gap = gshard[j].astype(F32)
        uv = pick(li <= lj, gap)
        at = rows_at(j, shard_blocks)
        u[at, :] = uv
        te[at, :] = pick(li <= start_lane + SUB - 1, gap)
        ts[at, :] = pick(li < start_lane, gap)
        lengths = jnp.broadcast_to(uv[:, B - 1 :], (shard_blocks, B))
        later = (iota((shard_blocks, shard_blocks), 1) > iota((shard_blocks, shard_blocks), 0)).astype(F32)
        left = jnp.dot(later, lengths, precision=HIGH, preferred_element_type=F32)
        ends[at, :] = left
        device[j, count:, :] = jnp.broadcast_to(left[0:1, :] + lengths[0:1, :], (8, B))

    def fetch(j):
        def block(b, _):
            for k in range(4):
                for i in range(B):
                    m = smarks[j, b * 4 + k, i]
                    rows[pl.ds((j * shard_blocks + b * 4 + k) * B + i, 1), :] = table[pl.ds(m, 1), :]
            return 0

        lax.fori_loop(0, shard_blocks // 4, block, 0)

    def emit(b):
        ur, er, sr = u[pl.ds(b, 1), :], te[pl.ds(b, 1), :], ts[pl.ds(b, 1), :]
        vals = rows[rows_at(b, B), :].astype(BF16)
        span = er - sr
        decays = [jnp.exp(-d8 * span[:, c * SUB : c * SUB + 1]) for c in range(PARTS)]
        spot = (rows_at(b, width), slice(None))
        return [
            (sums, spot, two(parted(d8 * jnp.exp(-d8 * (er - ur))), vals)),
            (dec, spot, jnp.concatenate([jnp.broadcast_to(t, (count, B)) for t in decays], 0)),
        ]

    prepare(r)
    first_move.wait()
    fetch(r)
    batched(shard_blocks, UNROLL, lambda b: emit(r * shard_blocks + b))
    for copy in gathers:
        copy.wait_recv()
    second_move = pltpu.make_async_copy(marks_out.at[1 - r], smarks.at[1 - r], mark_sem.at[1])
    second_move.start()
    marks_copy = pltpu.make_async_copy(marks_out, marks_all, end_sem.at[0])
    marks_copy.start()
    prepare(1 - r)
    second_move.wait()
    fetch(1 - r)
    batched(shard_blocks, UNROLL, lambda b: emit((1 - r) * shard_blocks + b))

    zero = jnp.zeros((count, B), F32)

    def recur(start, keep, ahead):
        def step(i, pair):
            b = i if ahead else shard_blocks - 1 - i
            for c in range(PARTS) if ahead else reversed(range(PARTS)):
                nxt = []
                for j in range(2):
                    s = pl.ds(pl.multiple_of((j * shard_blocks + b) * width + c * count, count), count)
                    if keep:
                        states[s, :] = pair[j]
                    nxt.append(pair[j] * dec[s, :] + sums[s, :])
                pair = tuple(nxt)
            return pair

        return lax.fori_loop(0, shard_blocks, step, start, unroll=2)

    def share(source, dest, send, recv):
        copies = []
        for i, p in enumerate(mates):
            copies.append(
                pltpu.make_async_remote_copy(
                    src_ref=source, dst_ref=dest.at[q], send_sem=send.at[i], recv_sem=recv.at[i],
                    device_id={"tm": p}, device_id_type=MESH,
                )
            )
        for copy in copies:
            copy.start()
        dest[q] = source[...]
        return copies

    for j, state in enumerate(recur((zero, zero), False, True)):
        device[j, 0:count, :] = state
    state_copies = share(device, summaries, f_send, f_recv)

    base_high, base_low = halves(base[...])
    base2 = jnp.concatenate([base_high, base_low], 0).T.astype(BF16)
    subi = iota((SUB, B), 0)
    subj = lax.rem(iota((SUB, B), 1), SUB)

    def mark_row(b):
        return marks_out[lax.div(b, shard_blocks), pl.ds(lax.rem(b, shard_blocks), 1), :]

    def within(b):
        ur, sr = u[pl.ds(b, 1), :], ts[pl.ds(b, 1), :]
        s = rows_at(b, B)
        col = turned(ur)
        colc = col[0:SUB]
        for c in range(1, PARTS):
            colc = jnp.where(part_row == c, col[c * SUB : (c + 1) * SUB], colc)
        apart = jnp.abs(colc - ur)
        g = jnp.zeros((SUB, B), F32)
        for k in range(count):
            g = g + (weights[k] * decay[k]) * jnp.exp(-decay[k] * apart)
        high, low = halves(jnp.where(subi > subj, g, 0.0))
        left = jnp.concatenate([parted(high), parted(low)], 0).astype(BF16)
        both = dot(left, rows[s, :].astype(BF16))
        lh, ll = halves(parted(w8 * jnp.exp(-d8 * (ur - sr))))
        stack = jnp.concatenate([lh, lh, ll, jnp.zeros((B - 3 * width, B), F32)], 0)
        m = mark_row(b)
        hi, lo = lax.div(m, B), lax.rem(m, B)
        onehot = (lax.rem(iota((2 * groups, B), 0), groups) == hi).astype(BF16)
        found = dot(base2, onehot)
        return [
            (sym, (rows_at(b, SUB), slice(None)), g),
            (inside, (s, slice(None)), both[:B] + both[B:]),
            (lanes, (s, slice(None)), stack.T.astype(BF16)),
            (base_e, (pl.ds(b, 1), slice(None)), jnp.sum(jnp.where(li == lo, found, 0.0), axis=0, keepdims=True)),
        ]

    batched(blocks, UNROLL, within)

    for copy in state_copies:
        copy.wait()
    start = [zero, zero]
    after = [jnp.zeros((1, B), F32)] * 2
    t_end = jnp.zeros((1, B), F32)
    for t in range(n):
        held = summaries[t % half, t // half]
        span = held[count : count + 1]
        t_end = t_end + span
        for j in range(2):
            mark = q + j * half
            start[j] = jnp.where(t < mark, start[j] * jnp.exp(-d8 * span) + held[0:count], start[j])
            after[j] = after[j] + jnp.where(t > mark, span, 0.0)
    recur(tuple(start), True, True)
    for j in range(2):
        at = slice(j * shard_blocks, (j + 1) * shard_blocks)
        ends[at, :] = ends[at, :] + after[j]

    fill = jnp.zeros((B - 3 * width, B), F32)

    def forward(b):
        s = rows_at(b, B)
        sh, sl = halves(states[rows_at(b, width), :])
        value = inside[s, :] + dot(lanes[s, :], jnp.concatenate([sh, sl, sh, fill], 0).astype(BF16))
        product = value * pltpu.roll(rows[s, :], edge, 1)
        tot = jnp.sum(product.T[:edge], axis=0, keepdims=True)
        return [
            (excitation, (s, slice(None)), value),
            (partial, (pl.ds(b, 1), slice(None)), tot * (1.0 / rank)),
        ]

    spot = mine * 2 + r

    def part_copies(g):
        s = rows_at(g, UNROLL)
        copies = []
        for i, t in enumerate([(twin, mine)] + [(t, o) for o in others for t in (me, twin)]):
            copies.append(
                pltpu.make_async_remote_copy(
                    src_ref=partial.at[s, :], dst_ref=total.at[spot, s, :],
                    send_sem=p_send.at[i, g], recv_sem=p_recv.at[i, g],
                    device_id={"tm": t[0], "mark": t[1]}, device_id_type=MESH,
                )
            )
        return copies

    def send_part(g):
        for copy in part_copies(g):
            copy.start()

    batched(blocks, UNROLL, forward, send_part)
    total[spot] = partial[...]

    def rest(b):
        left = w8 * (1.0 - jnp.exp(-d8 * (u[pl.ds(b, 1), :] * -1.0 + lengths_row(b) + ends[pl.ds(b, 1), :])))
        rem = jnp.sum(left, axis=0, keepdims=True)
        return rem, two(jnp.broadcast_to(rem, (8, B)), rows[rows_at(b, B), :].astype(BF16))

    def lengths_row(b):
        return u[pl.ds(b, 1), B - 1 :]

    def summed(values):
        while len(values) > 1:
            values = [sum(values[i : i + 2]) for i in range(0, len(values), 2)]
        return values[0]

    def rests(g, comp):
        found = [rest(g * UNROLL + i) for i in range(UNROLL)]
        remain[rows_at(g, UNROLL), :] = jnp.concatenate([f[0] for f in found], 0)
        return comp + summed([f[1] for f in found])

    comp = lax.fori_loop(0, blocks // UNROLL, rests, jnp.zeros((8, B), F32))

    row8 = iota((8, B), 0)

    def thirds(a, places):
        high, rest = halves(a)
        mid, low = halves(rest)
        out = jnp.zeros((8, B), F32)
        for term, where in zip((high, mid, low), places):
            for k in where:
                out = jnp.where(row8 == k, term, out)
        return out

    xstack = thirds(xtot * (-1.0 / types), ((0, 2, 5), (1, 4), (3,)))
    fill24 = jnp.zeros((B - 3 * width - 8, B), F32)

    def prepare_turn(b):
        lh, ll = halves(parted(w8 * jnp.exp(-d8 * (te[pl.ds(b, 1), :] - u[pl.ds(b, 1), :]))))
        rstack = thirds(remain[pl.ds(b, 1), :], ((0, 1, 3), (2, 4), (5,)))
        turn = jnp.concatenate([lh, lh, ll, rstack, fill24], 0).T.astype(BF16)
        return [(lanes, (rows_at(b, B), slice(None)), turn)]

    batched(blocks, UNROLL, prepare_turn)
    for g in range(blocks // UNROLL):
        for copy in part_copies(g):
            copy.wait()
    intensity = base_e[...]
    for j in range(2 * lanes_n):
        intensity = intensity + total[j]
    inverse[...] = 1.0 / intensity

    def reverse(b):
        e8 = d8 * jnp.exp(-d8 * (u[pl.ds(b, 1), :] - ts[pl.ds(b, 1), :])) * inverse[pl.ds(b, 1), :]
        return [(sums, (rows_at(b, width), slice(None)), two(parted(e8), rows[rows_at(b, B), :].astype(BF16)))]

    batched(blocks, UNROLL, reverse)

    for j, state in enumerate(recur((zero, zero), False, False)):
        behind[j * count : (j + 1) * count, :] = state
    behind[2 * count :, :] = comp
    back_copies = share(behind, back, b_send, b_recv)

    def spread(b):
        m = mark_row(b)
        hi, lo = lax.div(m, B), lax.rem(m, B)
        ih, il = halves(inverse[pl.ds(b, 1), :])
        wide = jnp.concatenate([jnp.broadcast_to(ih, (groups, B)), jnp.broadcast_to(il, (groups, B))], 0)
        left = jnp.where(lax.rem(iota((2 * groups, B), 0), groups) == hi, wide, 0.0).astype(BF16)
        right = (li == lo).astype(BF16)
        return left, right

    def spreads(g, both):
        pairs = [spread(r * shard_blocks + g * 8 + i) for i in range(8)]
        left = jnp.concatenate([p[0] for p in pairs], 1)
        right = jnp.concatenate([p[1] for p in pairs], 1)
        return both + lax.dot_general(left, right, NT, preferred_element_type=F32)

    both = lax.fori_loop(0, shard_blocks // 8, spreads, jnp.zeros((2 * groups, B), F32))
    base_own[...] = (both[:groups] + both[groups:]).reshape(base_own.shape)
    base_copies = []
    for i, p in enumerate(peers):
        copy = pltpu.make_async_remote_copy(
            src_ref=base_own.at[p], dst_ref=base_parts.at[me], send_sem=g_send.at[i], recv_sem=g_recv.at[i],
            device_id={"tm": p}, device_id_type=MESH,
        )
        copy.start()
        base_copies.append(copy)
    base_parts[me] = base_own[me]

    def feedback(b):
        s = rows_at(b, B)
        ir = inverse[pl.ds(b, 1), :]
        high, low = halves(jnp.where(subi < subj, sym[rows_at(b, SUB), :] * ir, 0.0))
        left = jnp.concatenate([parted(high), parted(low)], 0).astype(BF16)
        both = dot(left, rows[s, :].astype(BF16))
        return [(inside, (s, slice(None)), jnp.where(lane < edge, excitation[s, :] * turned(ir), both[:B] + both[B:]))]

    batched(blocks, UNROLL, feedback)

    for copy in back_copies:
        copy.wait()
    pending = [zero, zero]
    comp_all = jnp.zeros((8, B), F32)
    for p in range(half):
        comp_all = comp_all + back[p, 2 * count :, :]
    for t in reversed(range(n)):
        p, k = t % half, t // half
        span = summaries[p, k, count : count + 1, :]
        for j in range(2):
            pending[j] = jnp.where(
                t > q + j * half,
                pending[j] * jnp.exp(-d8 * span) + back[p, k * count : (k + 1) * count, :],
                pending[j],
            )
    recur(tuple(pending), True, False)
    events_all = blocks * B * half
    for copy in base_copies:
        copy.wait()
    base_all = base_parts[0]
    for p in range(1, n):
        base_all = base_all + base_parts[p]
    grad_base[...] = base_all * (types / events_all) - t_end * (1.0 / events_all)
    minus[...] = jnp.where(lane < edge, comp_all * (1.0 / events_all), 0.0)
    finals = [
        pltpu.make_async_copy(grad_base, base_out, end_sem.at[1]),
        pltpu.make_async_copy(minus, minus_out, end_sem.at[2]),
    ]
    for copy in finals:
        copy.start()

    def distant(b):
        s = rows_at(b, B)
        sh, sl = halves(states[rows_at(b, width), :])
        stack = jnp.concatenate([sh, sl, sh, xstack, fill24], 0)
        value = dot(lanes[s, :], jnp.where(lane < edge, 0.0, stack).astype(BF16))
        return [(values, (s, slice(None)), inside[s, :] + value)]

    def piece(g):
        s = rows_at(g, UNROLL * B)
        return pltpu.make_async_copy(values.at[s, :], values_out.at[s, :], out_sem.at[g])

    batched(blocks, UNROLL, distant, lambda g: piece(g).start())

    for copy in gathers:
        copy.wait_send()
    for copy in finals + [marks_copy]:
        copy.wait()
    for g in range(blocks // UNROLL):
        piece(g).wait()


def scatter_kernel(marks_in, values_in, out, marks, values, load_sem, out_sem, *tables):
    count = len(tables)
    types = out.shape[0]
    loads = [
        pltpu.make_async_copy(values_in, values, load_sem.at[0]),
        pltpu.make_async_copy(marks_in, marks, load_sem.at[1]),
    ]
    for copy in loads:
        copy.start()

    def zero(i, _):
        for t in tables:
            t[rows_at(i, 32), :] = jnp.zeros((32, B), F32)
        return 0

    lax.fori_loop(0, types // 32, zero, 0)
    for copy in loads:
        copy.wait()
    shards, blocks, _ = marks.shape
    for j in range(shards):

        def block(b, _):
            for i in range(B):
                t = tables[i % count]
                m = marks[j, b, i]
                e = (j * blocks + b) * B + i
                t[pl.ds(m, 1), :] = t[pl.ds(m, 1), :] + values[pl.ds(e, 1), :]
            return 0

        lax.fori_loop(0, blocks, block, 0)

    pieces = out_sem.shape[0]
    size = types // pieces

    def piece(c):
        s = rows_at(c, size)
        return pltpu.make_async_copy(tables[0].at[s, :], out.at[s, :], out_sem.at[c])

    def total(c, _):
        def add(i, _):
            s = pl.ds(pl.multiple_of(c * size + i * 32, 32), 32)
            acc = [t[s, :] for t in tables]
            while len(acc) > 1:
                acc = [acc[i] + acc[i + 1] for i in range(0, len(acc), 2)]
            tables[0][s, :] = acc[0]
            return 0

        lax.fori_loop(0, size // 32, add, 0, unroll=2)
        piece(c).start()
        return 0

    lax.fori_loop(0, pieces, total, 0)
    for c in range(pieces):
        piece(c).wait()


def ring_kernel(n, factor, minus, source, grad_excite, grad_source, dense, load_sem, slots, pieces, twin_in, send, recv, t_send, t_recv):
    half = n // 2
    per = dense.shape[0] // n
    rows = per // 2
    edge = B // 2
    ranks = grad_excite.shape[0] // 2
    me = lax.axis_index("tm")
    r = lax.div(me, half)
    q = lax.rem(me, half)
    odd = lax.rem(q, 2)
    at = lax.div(q, 2) + odd * (lax.div(2 * half - 1 - q, 2) - lax.div(q, 2))
    twin = q + (1 - r) * half

    def member(place):
        c = lax.rem(place + 2 * half, half)
        return 2 * c + lax.div(c, half // 2) * (2 * half - 1 - 4 * c)

    towards = [member(at + 1) + r * half, member(at - 1) + r * half]
    load = pltpu.make_async_copy(source, dense, load_sem.at[0])
    load.start()
    barrier = pltpu.get_barrier_semaphore()
    for p in towards + [twin]:
        pl.semaphore_signal(barrier, inc=1, device_id={"tm": p}, device_id_type=MESH)
    pl.semaphore_wait(barrier, 3)

    def span(j, step):
        way, kind = j % 2, j // 2
        place = at + 1 + step if way else at - 1 - step
        where = (1 - r) if kind == 0 else r
        block = member(place) + where * half
        return pl.ds(pl.multiple_of(block * per + way * rows, 8), rows)

    def copy(j, step, source):
        return pltpu.make_async_remote_copy(
            src_ref=source, dst_ref=slots.at[j, step], send_sem=send.at[j, step], recv_sem=recv.at[j, step],
            device_id={"tm": towards[j % 2]}, device_id_type=MESH,
        )

    chains = range(4)
    for j in chains:
        copy(j, 0, source.at[span(j, 0), :]).start()
    load.wait()

    def step(s, _):
        for j in chains:
            held = slots.at[j, s - 1]
            copy(j, s - 1, held).wait_recv()
            held[...] += dense[span(j, s), :]
            copy(j, s, held).start()
        return 0

    lax.fori_loop(1, half - 1, step, 0)

    def twin_copy(j):
        return pltpu.make_async_remote_copy(
            src_ref=pieces.at[j], dst_ref=twin_in.at[j], send_sem=t_send.at[j], recv_sem=t_recv.at[j],
            device_id={"tm": twin}, device_id_type=MESH,
        )

    for j in chains:
        copy(j, half - 2, slots.at[j, half - 2]).wait_recv()
        pieces[j] = (slots[j, half - 2] + dense[span(j, half - 1), :]) * factor - minus[0:1, :]
        if j < 2:
            twin_copy(j).start()
    low = r == 0
    for j in range(2):
        twin_copy(j).wait_recv()
        for i in range(rows // B):
            s = slice(i * B, (i + 1) * B)
            mine, their = pieces[2 + j, s, :].T, twin_in[j, s, :].T
            first = jnp.where(low, mine, their)
            second = jnp.where(low, their, mine)
            t = slice(j * rows + i * B, j * rows + (i + 1) * B)
            grad_excite[:ranks, t] = first[:ranks]
            grad_excite[ranks:, t] = second[:ranks]
            grad_source[:ranks, t] = first[edge : edge + ranks]
            grad_source[ranks:, t] = second[edge : edge + ranks]

    def sent(s, _):
        for j in chains:
            copy(j, s, slots.at[j, s]).wait_send()
        return 0

    lax.fori_loop(0, half - 1, sent, 0)
    for j in range(2):
        twin_copy(j).wait_send()


def square_kernel(
    n, factor, minus, source, grad_excite, grad_source,
    dense, load_sem, first, second, pieces, twin_in, a_send, a_recv, b_send, b_recv, t_send, t_recv,
):
    half = n // 2
    per = source.shape[0] // n
    rows = per // 4
    edge = B // 2
    ranks = grad_excite.shape[0] // 2
    me = lax.axis_index("tm")
    r = lax.div(me, half)
    q = lax.rem(me, half)
    qa, qb = lax.div(q, 2), lax.rem(q, 2)
    near = r * half + qa * 2 + 1 - qb
    far = r * half + (1 - qa) * 2 + qb
    twin = q + (1 - r) * half
    load = pltpu.make_async_copy(source, dense, load_sem.at[0])
    load.start()
    barrier = pltpu.get_barrier_semaphore()
    for p in (near, far, twin):
        pl.semaphore_signal(barrier, inc=1, device_id={"tm": p}, device_id_type=MESH)
    pl.semaphore_wait(barrier, 3)

    def span(j, a, b):
        block = a * 2 + b + ((1 - r) if j < 4 else r) * half
        return pl.ds(pl.multiple_of(block * per + (j % 4) * rows, 8), rows)

    def across(j):
        return j % 4 == 3

    def place(j, k, theirs):
        if across(j):
            return span(j, 1 - qa if theirs else qa, qb if k else 1 - qb)
        return span(j, qa if k else 1 - qa, 1 - qb if theirs else qb)

    def copy_a(j, k):
        return pltpu.make_async_remote_copy(
            src_ref=source.at[place(j, k, True), :], dst_ref=first.at[j, k],
            send_sem=a_send.at[j, k], recv_sem=a_recv.at[j, k],
            device_id={"tm": far if across(j) else near}, device_id_type=MESH,
        )

    def copy_b(j):
        return pltpu.make_async_remote_copy(
            src_ref=first.at[j, 0], dst_ref=second.at[j], send_sem=b_send.at[j], recv_sem=b_recv.at[j],
            device_id={"tm": near if across(j) else far}, device_id_type=MESH,
        )

    def copy_t(j):
        return pltpu.make_async_remote_copy(
            src_ref=pieces.at[j], dst_ref=twin_in.at[j], send_sem=t_send.at[j], recv_sem=t_recv.at[j],
            device_id={"tm": twin}, device_id_type=MESH,
        )

    def begin(j):
        for k in range(2):
            copy_a(j, k).start()

    def middle(j):
        copy_a(j, 0).wait_recv()
        first[j, 0] = first[j, 0] + dense[place(j, 0, False), :]
        copy_b(j).start()

    def put(value, j, who):
        for i in range(rows // B):
            t = value[i * B : (i + 1) * B].T
            lanes = slice((j % 4) * rows + i * B, (j % 4) * rows + (i + 1) * B)
            at = pl.ds(pl.multiple_of(who * ranks, ranks), ranks)
            grad_excite[at, lanes] = t[:ranks]
            grad_source[at, lanes] = t[edge : edge + ranks]

    def last(j):
        copy_a(j, 1).wait_recv()
        copy_b(j).wait_recv()
        value = (second[j] + first[j, 1] + dense[place(j, 1, False), :]) * factor - minus[0:1, :]
        if j < 4:
            pieces[j] = value
            copy_t(j).start()
        else:
            put(value, j, r)

    copy_a(0, 0).start()
    copy_a(3, 0).start()
    copy_a(1, 0).start()
    copy_a(0, 1).start()
    copy_a(3, 1).start()
    load.wait()
    middle(0)
    copy_a(2, 0).start()
    copy_a(1, 1).start()
    middle(3)
    copy_a(7, 0).start()
    middle(1)
    copy_a(4, 0).start()
    copy_a(2, 1).start()
    last(0)
    middle(2)
    copy_a(5, 0).start()
    copy_a(7, 1).start()
    last(3)
    last(1)
    middle(4)
    copy_a(6, 0).start()
    copy_a(4, 1).start()
    last(2)
    middle(7)
    middle(5)
    copy_a(5, 1).start()
    copy_a(6, 1).start()
    last(4)
    last(7)
    middle(6)
    last(5)
    for j in (0, 3, 1):
        copy_t(j).wait_recv()
        put(twin_in[j], j, 1 - r)
    last(6)
    copy_t(2).wait_recv()
    put(twin_in[2], 2, 1 - r)
    for j in range(8):
        for k in range(2):
            copy_a(j, k).wait_send()
        copy_b(j).wait_send()
    for j in range(4):
        copy_t(j).wait_send()


def body(marks, gaps, excite, source, base_rate, weights, decay):
    shard = marks.shape[0]
    slices, types = excite.shape
    n = lax.axis_size("tm")
    lanes_n = lax.axis_size("mark")
    half = n // 2
    rank = slices * lanes_n
    count = decay.shape[0]
    shard_blocks = shard // B
    blocks = 2 * shard_blocks
    events = 2 * shard
    groups = types // B
    width = count * PARTS
    dma = pltpu.SemaphoreType.DMA
    plane = pltpu.VMEM((blocks, B), F32)
    tall = pltpu.VMEM((events, B), F32)
    small = pltpu.VMEM((blocks * width, B), F32)
    types_own = types // n

    values, grad_base, minus, marks_all = pl.pallas_call(
        functools.partial(front_kernel, n, lanes_n, rank),
        out_shape=[
            jax.ShapeDtypeStruct((events, B), F32),
            jax.ShapeDtypeStruct((groups // n, B), F32),
            jax.ShapeDtypeStruct((8, B), F32),
            jax.ShapeDtypeStruct((2, shard_blocks, B), jnp.int32),
        ],
        in_specs=[HBM] * 7,
        out_specs=[HBM] * 4,
        scratch_shapes=[
            pltpu.VMEM((B, types), BF16),
            pltpu.VMEM((types, B), F32),
            tall,
            pltpu.SMEM((2, shard_blocks, B), jnp.int32),
            pltpu.VMEM((shard_blocks, B), jnp.int32),
            pltpu.VMEM((2, shard_blocks, B), jnp.int32),
            plane, plane, plane,
            pltpu.VMEM((blocks * SUB, B), F32),
            tall, tall,
            pltpu.VMEM((events, B), BF16),
            small, small, small,
            plane, plane, plane, plane,
            pltpu.VMEM((2, count + 8, B), F32), pltpu.VMEM((half, 2, count + 8, B), F32),
            plane, pltpu.VMEM((2 * lanes_n, blocks, B), F32),
            pltpu.VMEM((half, 2 * count + 8, B), F32), pltpu.VMEM((2 * count + 8, B), F32),
            pltpu.VMEM((n, groups // n, B), F32),
            pltpu.VMEM((n, groups // n, B), F32),
            dma((2,)), dma((2,)),
            dma((2,)), dma((2,)),
            dma((half - 1,)), dma((half - 1,)),
            dma((2 * lanes_n - 1, blocks // UNROLL)), dma((2 * lanes_n - 1, blocks // UNROLL)),
            dma((half - 1,)), dma((half - 1,)),
            dma((n - 1,)), dma((n - 1,)),
            tall, dma((blocks // UNROLL,)),
            pltpu.SMEM((count,), F32), pltpu.SMEM((count,), F32),
            pltpu.VMEM((shard_blocks, B), jnp.int32), pltpu.VMEM((shard_blocks, B), jnp.int32),
            pltpu.VMEM((groups, B), F32), pltpu.VMEM((groups // n, B), F32), pltpu.VMEM((8, B), F32),
            pltpu.VMEM((2, shard_blocks, B), jnp.int32), dma((5,)), dma((3,)),
        ],
        compiler_params=pltpu.CompilerParams(
            collective_id=0, has_side_effects=True, vmem_limit_bytes=ALL_VMEM
        ),
    )(weights, decay, marks.reshape(shard_blocks, B), gaps.reshape(shard_blocks, B), source, excite,
      base_rate.reshape(groups, B))

    dense = pl.pallas_call(
        scatter_kernel,
        out_shape=jax.ShapeDtypeStruct((types, B), F32),
        in_specs=[HBM] * 2,
        out_specs=HBM,
        scratch_shapes=[pltpu.SMEM((2, shard_blocks, B), jnp.int32), tall, dma((2,)), dma((8,))] + [pltpu.VMEM((types, B), F32)] * 8,
        compiler_params=pltpu.CompilerParams(vmem_limit_bytes=ALL_VMEM),
    )(marks_all, values)

    quarter = types_own // 4
    if half == 4 and quarter % B == 0:
        kernel = square_kernel
        scratch = [
            pltpu.VMEM((8, 2, quarter, B), F32),
            pltpu.VMEM((8, quarter, B), F32),
            pltpu.VMEM((4, quarter, B), F32),
            pltpu.VMEM((4, quarter, B), F32),
            dma((8, 2)), dma((8, 2)), dma((8,)), dma((8,)), dma((4,)), dma((4,)),
        ]
    else:
        kernel = ring_kernel
        scratch = [
            pltpu.VMEM((4, half - 1, types_own // 2, B), F32),
            pltpu.VMEM((4, types_own // 2, B), F32),
            pltpu.VMEM((2, types_own // 2, B), F32),
            dma((4, half - 1)), dma((4, half - 1)), dma((2,)), dma((2,)),
        ]
    grad_excite, grad_source = pl.pallas_call(
        functools.partial(kernel, n, types / (events * half)),
        out_shape=[jax.ShapeDtypeStruct((slices, types_own), F32)] * 2,
        in_specs=[VMEM, HBM],
        out_specs=[VMEM] * 2,
        scratch_shapes=[pltpu.VMEM((types, B), F32), dma((1,))] + scratch,
        compiler_params=pltpu.CompilerParams(
            collective_id=1, has_side_effects=True, vmem_limit_bytes=52 * 2**20
        ),
    )(minus, dense)
    return grad_excite, grad_source, grad_base.reshape(types_own)


def solution(mesh):
    return jax.shard_map(
        body,
        mesh=mesh,
        in_specs=(P("tm"), P("tm"), P("mark", None), P("mark", None), P(), P(), P()),
        out_specs=(P("mark", "tm"), P("mark", "tm"), P("tm")),
        check_vma=False,
    )
```

```python
import functools

import jax
import jax.numpy as jnp
from jax import lax
from jax.experimental import pallas as pl
from jax.experimental.pallas import tpu as pltpu
from jax.sharding import PartitionSpec as P

F32 = jnp.float32
BF16 = jnp.bfloat16
B = 128
SUB = 32
UNROLL = 16
ALL_VMEM = 60 * 2**20
PARTS = B // SUB
HIGH = lax.Precision.HIGHEST
MESH = pl.DeviceIdType.MESH
VMEM = pl.BlockSpec(memory_space=pltpu.VMEM)
SMEM = pl.BlockSpec(memory_space=pltpu.SMEM)
HBM = pl.BlockSpec(memory_space=pltpu.HBM)
NT = (((1,), (1,)), ((), ()))


def iota(shape, axis):
    return lax.broadcasted_iota(jnp.int32, shape, axis)


def dot(a, b):
    return jnp.dot(a, b, preferred_element_type=F32)


def halves(a):
    high = a.astype(BF16).astype(F32)
    return high, a - high


def down(ref, count):
    row = iota((count, B), 0)
    out = jnp.zeros((count, B), F32)
    for k in range(count):
        out = jnp.where(row == k, ref[k], out)
    return out


def parted(a):
    part = lax.div(iota(a.shape, 1), SUB)
    return jnp.concatenate([jnp.where(part == c, a, 0.0) for c in range(PARTS)], 0)


def turned(row):
    return jnp.broadcast_to(row, (B, B)).T


def batched(count, size, one, then=None):
    def body(g, _):
        stores = []
        for i in range(size):
            stores += one(g * size + i)
        for ref, where, value in stores:
            ref[where] = value
        if then is not None:
            then(g)
        return 0

    lax.fori_loop(0, count // size, body, 0)


def rows_at(b, size):
    return pl.ds(pl.multiple_of(b * size, size), size)


def front_kernel(
    n, lanes_n, rank,
    weights_in, decay_in, marks_in, gaps_in, src, exc, base_in,
    values_out, base_out, minus_out, marks_all,
    factors, table, rows, smarks, own, gshard, u, te, ts, sym, inside, excitation, lanes, states, sums, dec, base_e,
    inverse, remain, ends, device, summaries, partial, total, back, behind, base_own, base_parts,
    load_sem, mark_sem, ag_send, ag_recv, f_send, f_recv, p_send, p_recv, b_send, b_recv, g_send, g_recv, values, out_sem,
    weights, decay, marks, gaps, base, grad_base, minus, marks_out, in_sem, end_sem,
):
    count = decay.shape[0]
    width = count * PARTS
    half = n // 2
    shard_blocks = marks.shape[0]
    blocks = 2 * shard_blocks
    types = table.shape[0]
    groups = types // B
    ranks = src.shape[0] // 2
    edge = B // 2
    me = lax.axis_index("tm")
    mine = lax.axis_index("mark")
    r = lax.div(me, half)
    q = lax.rem(me, half)
    peers = [lax.rem(me + i, n) for i in range(1, n)]
    mates = [r * half + lax.rem(q + i, half) for i in range(1, half)]
    others = [lax.rem(mine + i, lanes_n) for i in range(1, lanes_n)]
    twin = q + (1 - r) * half

    if ranks < edge:
        for a in range(2):
            factors[a * edge + ranks : (a + 1) * edge, :] = jnp.zeros((edge - ranks, types), BF16)
    barrier = pltpu.get_barrier_semaphore()
    targets = [{"tm": p, "mark": mine} for p in peers]
    targets += [{"tm": t, "mark": o} for o in others for t in (me, twin)]
    for t in targets:
        pl.semaphore_signal(barrier, inc=1, device_id=t, device_id_type=MESH)
    small = [
        pltpu.make_async_copy(a, b, in_sem.at[i])
        for i, (a, b) in enumerate(
            ((marks_in, marks), (gaps_in, gaps), (weights_in, weights), (decay_in, decay), (base_in, base))
        )
    ]
    for copy in small:
        copy.start()
    loads = []
    for a, ref in enumerate((src, exc)):
        copy = pltpu.make_async_copy(
            ref.at[pl.ds(pl.multiple_of(r * ranks, ranks), ranks), :],
            factors.at[a * edge : a * edge + ranks, :],
            load_sem.at[a],
        )
        copy.start()
        loads.append(copy)

    small[0].wait()
    small[1].wait()
    own[...] = marks[...]
    marks_out[r] = marks[...]
    gshard[r] = gaps[...]
    first_move = pltpu.make_async_copy(own, smarks.at[r], mark_sem.at[0])
    first_move.start()
    gathers = []
    pl.semaphore_wait(barrier, len(targets))
    for a, (ref, dst) in enumerate(((own, marks_out), (gaps, gshard))):
        copy = pltpu.make_async_remote_copy(
            src_ref=ref, dst_ref=dst.at[r], send_sem=ag_send.at[a], recv_sem=ag_recv.at[a],
            device_id={"tm": twin}, device_id_type=MESH,
        )
        copy.start()
        gathers.append(copy)

    for copy in loads:
        copy.wait()

    def build(c, acc):
        s = rows_at(c, B)
        t = factors[:, s].astype(F32).T
        table[s, :] = t
        return acc + jnp.sum(t.reshape(B // 8, 8, B), axis=0)

    acc = lax.fori_loop(0, groups, build, jnp.zeros((8, B), F32), unroll=8)
    xtot = jnp.sum(acc, axis=0, keepdims=True)

    for copy in small[2:]:
        copy.wait()
    d8, w8 = down(decay, count), down(weights, count)
    li, lj = iota((B, B), 0), iota((B, B), 1)
    start_lane = lax.div(lj, SUB) * SUB
    part_row = lax.div(iota((1, B), 1), SUB)
    lane = iota((1, B), 1)

    def pick(mask, a):
        return jnp.dot(a, mask.astype(F32), precision=HIGH, preferred_element_type=F32)

    def two(a, b):
        k = a.shape[0]
        high, low = halves(a)
        both = dot(jnp.concatenate([high, low], 0).astype(BF16), b)
        return both[:k] + both[k:]

    def prepare(j):
        gap = gshard[j].astype(F32)
        uv = pick(li <= lj, gap)
        at = rows_at(j, shard_blocks)
        u[at, :] = uv
        te[at, :] = pick(li <= start_lane + SUB - 1, gap)
        ts[at, :] = pick(li < start_lane, gap)
        lengths = jnp.broadcast_to(uv[:, B - 1 :], (shard_blocks, B))
        later = (iota((shard_blocks, shard_blocks), 1) > iota((shard_blocks, shard_blocks), 0)).astype(F32)
        left = jnp.dot(later, lengths, precision=HIGH, preferred_element_type=F32)
        ends[at, :] = left
        device[j, count:, :] = jnp.broadcast_to(left[0:1, :] + lengths[0:1, :], (8, B))

    def fetch(j):
        def block(b, _):
            for k in range(4):
                for i in range(B):
                    m = smarks[j, b * 4 + k, i]
                    rows[pl.ds((j * shard_blocks + b * 4 + k) * B + i, 1), :] = table[pl.ds(m, 1), :]
            return 0

        lax.fori_loop(0, shard_blocks // 4, block, 0)

    def emit(b):
        ur, er, sr = u[pl.ds(b, 1), :], te[pl.ds(b, 1), :], ts[pl.ds(b, 1), :]
        vals = rows[rows_at(b, B), :].astype(BF16)
        span = er - sr
        decays = [jnp.exp(-d8 * span[:, c * SUB : c * SUB + 1]) for c in range(PARTS)]
        spot = (rows_at(b, width), slice(None))
        return [
            (sums, spot, two(parted(d8 * jnp.exp(-d8 * (er - ur))), vals)),
            (dec, spot, jnp.concatenate([jnp.broadcast_to(t, (count, B)) for t in decays], 0)),
        ]

    prepare(r)
    first_move.wait()
    fetch(r)
    batched(shard_blocks, UNROLL, lambda b: emit(r * shard_blocks + b))
    for copy in gathers:
        copy.wait_recv()
    second_move = pltpu.make_async_copy(marks_out.at[1 - r], smarks.at[1 - r], mark_sem.at[1])
    second_move.start()
    marks_copy = pltpu.make_async_copy(marks_out, marks_all, end_sem.at[0])
    marks_copy.start()
    prepare(1 - r)
    second_move.wait()
    fetch(1 - r)
    batched(shard_blocks, UNROLL, lambda b: emit((1 - r) * shard_blocks + b))

    zero = jnp.zeros((count, B), F32)

    def recur(start, keep, ahead):
        def step(i, pair):
            b = i if ahead else shard_blocks - 1 - i
            for c in range(PARTS) if ahead else reversed(range(PARTS)):
                nxt = []
                for j in range(2):
                    s = pl.ds(pl.multiple_of((j * shard_blocks + b) * width + c * count, count), count)
                    if keep:
                        states[s, :] = pair[j]
                    nxt.append(pair[j] * dec[s, :] + sums[s, :])
                pair = tuple(nxt)
            return pair

        return lax.fori_loop(0, shard_blocks, step, start, unroll=8)

    def share(source, dest, send, recv):
        copies = []
        for i, p in enumerate(mates):
            copies.append(
                pltpu.make_async_remote_copy(
                    src_ref=source, dst_ref=dest.at[q], send_sem=send.at[i], recv_sem=recv.at[i],
                    device_id={"tm": p}, device_id_type=MESH,
                )
            )
        for copy in copies:
            copy.start()
        dest[q] = source[...]
        return copies

    for j, state in enumerate(recur((zero, zero), False, True)):
        device[j, 0:count, :] = state
    state_copies = share(device, summaries, f_send, f_recv)

    base_high, base_low = halves(base[...])
    base2 = jnp.concatenate([base_high, base_low], 0).T.astype(BF16)
    subi = iota((SUB, B), 0)
    subj = lax.rem(iota((SUB, B), 1), SUB)

    def mark_row(b):
        return marks_out[lax.div(b, shard_blocks), pl.ds(lax.rem(b, shard_blocks), 1), :]

    def within(b):
        ur, sr = u[pl.ds(b, 1), :], ts[pl.ds(b, 1), :]
        s = rows_at(b, B)
        col = turned(ur)
        colc = col[0:SUB]
        for c in range(1, PARTS):
            colc = jnp.where(part_row == c, col[c * SUB : (c + 1) * SUB], colc)
        apart = jnp.abs(colc - ur)
        g = jnp.zeros((SUB, B), F32)
        for k in range(count):
            g = g + (weights[k] * decay[k]) * jnp.exp(-decay[k] * apart)
        high, low = halves(jnp.where(subi > subj, g, 0.0))
        left = jnp.concatenate([parted(high), parted(low)], 0).astype(BF16)
        both = dot(left, rows[s, :].astype(BF16))
        lh, ll = halves(parted(w8 * jnp.exp(-d8 * (ur - sr))))
        stack = jnp.concatenate([lh, lh, ll, jnp.zeros((B - 3 * width, B), F32)], 0)
        m = mark_row(b)
        hi, lo = lax.div(m, B), lax.rem(m, B)
        onehot = (lax.rem(iota((2 * groups, B), 0), groups) == hi).astype(BF16)
        found = dot(base2, onehot)
        return [
            (sym, (rows_at(b, SUB), slice(None)), g),
            (inside, (s, slice(None)), both[:B] + both[B:]),
            (lanes, (s, slice(None)), stack.T.astype(BF16)),
            (base_e, (pl.ds(b, 1), slice(None)), jnp.sum(jnp.where(li == lo, found, 0.0), axis=0, keepdims=True)),
        ]

    batched(blocks, 2 * UNROLL, within)

    for copy in state_copies:
        copy.wait()
    start = [zero, zero]
    after = [jnp.zeros((1, B), F32)] * 2
    t_end = jnp.zeros((1, B), F32)
    for t in range(n):
        held = summaries[t % half, t // half]
        span = held[count : count + 1]
        t_end = t_end + span
        for j in range(2):
            mark = q + j * half
            start[j] = jnp.where(t < mark, start[j] * jnp.exp(-d8 * span) + held[0:count], start[j])
            after[j] = after[j] + jnp.where(t > mark, span, 0.0)
    recur(tuple(start), True, True)
    for j in range(2):
        at = slice(j * shard_blocks, (j + 1) * shard_blocks)
        ends[at, :] = ends[at, :] + after[j]

    fill = jnp.zeros((B - 3 * width, B), F32)

    def forward(b):
        s = rows_at(b, B)
        sh, sl = halves(states[rows_at(b, width), :])
        value = inside[s, :] + dot(lanes[s, :], jnp.concatenate([sh, sl, sh, fill], 0).astype(BF16))
        product = value * pltpu.roll(rows[s, :], edge, 1)
        tot = jnp.sum(product.T[:edge], axis=0, keepdims=True)
        return [
            (excitation, (s, slice(None)), value),
            (partial, (pl.ds(b, 1), slice(None)), tot * (1.0 / rank)),
        ]

    spot = mine * 2 + r

    def part_copies(g):
        s = rows_at(g, UNROLL)
        copies = []
        for i, t in enumerate([(twin, mine)] + [(t, o) for o in others for t in (me, twin)]):
            copies.append(
                pltpu.make_async_remote_copy(
                    src_ref=partial.at[s, :], dst_ref=total.at[spot, s, :],
                    send_sem=p_send.at[i, g], recv_sem=p_recv.at[i, g],
                    device_id={"tm": t[0], "mark": t[1]}, device_id_type=MESH,
                )
            )
        return copies

    def send_part(g):
        for copy in part_copies(g):
            copy.start()

    batched(blocks, UNROLL, forward, send_part)
    total[spot] = partial[...]

    def rest(b):
        left = w8 * (1.0 - jnp.exp(-d8 * (u[pl.ds(b, 1), :] * -1.0 + lengths_row(b) + ends[pl.ds(b, 1), :])))
        rem = jnp.sum(left, axis=0, keepdims=True)
        return rem, two(jnp.broadcast_to(rem, (8, B)), rows[rows_at(b, B), :].astype(BF16))

    def lengths_row(b):
        return u[pl.ds(b, 1), B - 1 :]

    def summed(values):
        while len(values) > 1:
            values = [sum(values[i : i + 2]) for i in range(0, len(values), 2)]
        return values[0]

    def rests(g, comp):
        found = [rest(g * UNROLL + i) for i in range(UNROLL)]
        remain[rows_at(g, UNROLL), :] = jnp.concatenate([f[0] for f in found], 0)
        return comp + summed([f[1] for f in found])

    comp = lax.fori_loop(0, blocks // UNROLL, rests, jnp.zeros((8, B), F32))

    row8 = iota((8, B), 0)

    def thirds(a, places):
        high, rest = halves(a)
        mid, low = halves(rest)
        out = jnp.zeros((8, B), F32)
        for term, where in zip((high, mid, low), places):
            for k in where:
                out = jnp.where(row8 == k, term, out)
        return out

    xstack = thirds(xtot * (-1.0 / types), ((0, 2, 5), (1, 4), (3,)))
    fill24 = jnp.zeros((B - 3 * width - 8, B), F32)

    def prepare_turn(b):
        lh, ll = halves(parted(w8 * jnp.exp(-d8 * (te[pl.ds(b, 1), :] - u[pl.ds(b, 1), :]))))
        rstack = thirds(remain[pl.ds(b, 1), :], ((0, 1, 3), (2, 4), (5,)))
        turn = jnp.concatenate([lh, lh, ll, rstack, fill24], 0).T.astype(BF16)
        return [(lanes, (rows_at(b, B), slice(None)), turn)]

    batched(blocks, 2 * UNROLL, prepare_turn)
    for g in range(blocks // UNROLL):
        for copy in part_copies(g):
            copy.wait()
    intensity = base_e[...]
    for j in range(2 * lanes_n):
        intensity = intensity + total[j]
    inverse[...] = 1.0 / intensity

    def reverse(b):
        e8 = d8 * jnp.exp(-d8 * (u[pl.ds(b, 1), :] - ts[pl.ds(b, 1), :])) * inverse[pl.ds(b, 1), :]
        return [(sums, (rows_at(b, width), slice(None)), two(parted(e8), rows[rows_at(b, B), :].astype(BF16)))]

    batched(blocks, 2 * UNROLL, reverse)

    for j, state in enumerate(recur((zero, zero), False, False)):
        behind[j * count : (j + 1) * count, :] = state
    behind[2 * count :, :] = comp
    back_copies = share(behind, back, b_send, b_recv)

    def spread(b):
        m = mark_row(b)
        hi, lo = lax.div(m, B), lax.rem(m, B)
        ih, il = halves(inverse[pl.ds(b, 1), :])
        wide = jnp.concatenate([jnp.broadcast_to(ih, (groups, B)), jnp.broadcast_to(il, (groups, B))], 0)
        left = jnp.where(lax.rem(iota((2 * groups, B), 0), groups) == hi, wide, 0.0).astype(BF16)
        right = (li == lo).astype(BF16)
        return left, right

    def spreads(g, both):
        pairs = [spread(r * shard_blocks + g * 8 + i) for i in range(8)]
        left = jnp.concatenate([p[0] for p in pairs], 1)
        right = jnp.concatenate([p[1] for p in pairs], 1)
        return both + lax.dot_general(left, right, NT, preferred_element_type=F32)

    both = lax.fori_loop(0, shard_blocks // 8, spreads, jnp.zeros((2 * groups, B), F32))
    base_own[...] = (both[:groups] + both[groups:]).reshape(base_own.shape)
    base_copies = []
    for i, p in enumerate(peers):
        copy = pltpu.make_async_remote_copy(
            src_ref=base_own.at[p], dst_ref=base_parts.at[me], send_sem=g_send.at[i], recv_sem=g_recv.at[i],
            device_id={"tm": p}, device_id_type=MESH,
        )
        copy.start()
        base_copies.append(copy)
    base_parts[me] = base_own[me]

    def feedback(b):
        s = rows_at(b, B)
        ir = inverse[pl.ds(b, 1), :]
        high, low = halves(jnp.where(subi < subj, sym[rows_at(b, SUB), :] * ir, 0.0))
        left = jnp.concatenate([parted(high), parted(low)], 0).astype(BF16)
        both = dot(left, rows[s, :].astype(BF16))
        return [(inside, (s, slice(None)), jnp.where(lane < edge, excitation[s, :] * turned(ir), both[:B] + both[B:]))]

    batched(blocks, 2 * UNROLL, feedback)

    for copy in back_copies:
        copy.wait()
    pending = [zero, zero]
    comp_all = jnp.zeros((8, B), F32)
    for p in range(half):
        comp_all = comp_all + back[p, 2 * count :, :]
    for t in reversed(range(n)):
        p, k = t % half, t // half
        span = summaries[p, k, count : count + 1, :]
        for j in range(2):
            pending[j] = jnp.where(
                t > q + j * half,
                pending[j] * jnp.exp(-d8 * span) + back[p, k * count : (k + 1) * count, :],
                pending[j],
            )
    recur(tuple(pending), True, False)
    events_all = blocks * B * half
    for copy in base_copies:
        copy.wait()
    base_all = base_parts[0]
    for p in range(1, n):
        base_all = base_all + base_parts[p]
    grad_base[...] = base_all * (types / events_all) - t_end * (1.0 / events_all)
    minus[...] = jnp.where(lane < edge, comp_all * (1.0 / events_all), 0.0)
    finals = [
        pltpu.make_async_copy(grad_base, base_out, end_sem.at[1]),
        pltpu.make_async_copy(minus, minus_out, end_sem.at[2]),
    ]
    for copy in finals:
        copy.start()

    def distant(b):
        s = rows_at(b, B)
        sh, sl = halves(states[rows_at(b, width), :])
        stack = jnp.concatenate([sh, sl, sh, xstack, fill24], 0)
        value = dot(lanes[s, :], jnp.where(lane < edge, 0.0, stack).astype(BF16))
        return [(values, (s, slice(None)), inside[s, :] + value)]

    def piece(g):
        s = rows_at(g, UNROLL * B)
        return pltpu.make_async_copy(values.at[s, :], values_out.at[s, :], out_sem.at[g])

    batched(blocks, UNROLL, distant, lambda g: piece(g).start())

    for copy in gathers:
        copy.wait_send()
    for copy in finals + [marks_copy]:
        copy.wait()
    for g in range(blocks // UNROLL):
        piece(g).wait()


def scatter_kernel(marks_in, values_in, out, marks, values, load_sem, out_sem, *tables):
    count = len(tables)
    types = out.shape[0]
    loads = [
        pltpu.make_async_copy(values_in, values, load_sem.at[0]),
        pltpu.make_async_copy(marks_in, marks, load_sem.at[1]),
    ]
    for copy in loads:
        copy.start()

    def zero(i, _):
        for t in tables:
            t[rows_at(i, 32), :] = jnp.zeros((32, B), F32)
        return 0

    lax.fori_loop(0, types // 32, zero, 0, unroll=4)
    for copy in loads:
        copy.wait()
    shards, blocks, _ = marks.shape
    for j in range(shards):

        def block(b, _):
            for i in range(B):
                t = tables[i % count]
                m = marks[j, b, i]
                e = (j * blocks + b) * B + i
                t[pl.ds(m, 1), :] = t[pl.ds(m, 1), :] + values[pl.ds(e, 1), :]
            return 0

        lax.fori_loop(0, blocks, block, 0)

    result = values if values.shape[0] >= types else tables[0]
    pieces = out_sem.shape[0]
    size = types // pieces

    def piece(c):
        s = rows_at(c, size)
        return pltpu.make_async_copy(result.at[s, :], out.at[s, :], out_sem.at[c])

    def total(c, _):
        def add(i, _):
            s = pl.ds(pl.multiple_of(c * size + i * 32, 32), 32)
            acc = [t[s, :] for t in tables]
            while len(acc) > 1:
                acc = [acc[i] + acc[i + 1] for i in range(0, len(acc), 2)]
            result[s, :] = acc[0]
            return 0

        lax.fori_loop(0, size // 32, add, 0, unroll=16)
        piece(c).start()
        return 0

    lax.fori_loop(0, pieces, total, 0)
    for c in range(pieces):
        piece(c).wait()


def ring_kernel(n, factor, minus, source, grad_excite, grad_source, dense, load_sem, slots, pieces, twin_in, send, recv, t_send, t_recv):
    half = n // 2
    per = dense.shape[0] // n
    rows = per // 2
    edge = B // 2
    ranks = grad_excite.shape[0] // 2
    me = lax.axis_index("tm")
    r = lax.div(me, half)
    q = lax.rem(me, half)
    odd = lax.rem(q, 2)
    at = lax.div(q, 2) + odd * (lax.div(2 * half - 1 - q, 2) - lax.div(q, 2))
    twin = q + (1 - r) * half

    def member(place):
        c = lax.rem(place + 2 * half, half)
        return 2 * c + lax.div(c, half // 2) * (2 * half - 1 - 4 * c)

    towards = [member(at + 1) + r * half, member(at - 1) + r * half]
    load = pltpu.make_async_copy(source, dense, load_sem.at[0])
    load.start()
    barrier = pltpu.get_barrier_semaphore()
    for p in towards + [twin]:
        pl.semaphore_signal(barrier, inc=1, device_id={"tm": p}, device_id_type=MESH)
    pl.semaphore_wait(barrier, 3)

    def span(j, step):
        way, kind = j % 2, j // 2
        place = at + 1 + step if way else at - 1 - step
        where = (1 - r) if kind == 0 else r
        block = member(place) + where * half
        return pl.ds(pl.multiple_of(block * per + way * rows, 8), rows)

    def copy(j, step, source):
        return pltpu.make_async_remote_copy(
            src_ref=source, dst_ref=slots.at[j, step], send_sem=send.at[j, step], recv_sem=recv.at[j, step],
            device_id={"tm": towards[j % 2]}, device_id_type=MESH,
        )

    chains = range(4)
    for j in chains:
        copy(j, 0, source.at[span(j, 0), :]).start()
    load.wait()

    def step(s, _):
        for j in chains:
            held = slots.at[j, s - 1]
            copy(j, s - 1, held).wait_recv()
            held[...] += dense[span(j, s), :]
            copy(j, s, held).start()
        return 0

    lax.fori_loop(1, half - 1, step, 0)

    def twin_copy(j):
        return pltpu.make_async_remote_copy(
            src_ref=pieces.at[j], dst_ref=twin_in.at[j], send_sem=t_send.at[j], recv_sem=t_recv.at[j],
            device_id={"tm": twin}, device_id_type=MESH,
        )

    for j in chains:
        copy(j, half - 2, slots.at[j, half - 2]).wait_recv()
        pieces[j] = (slots[j, half - 2] + dense[span(j, half - 1), :]) * factor - minus[0:1, :]
        if j < 2:
            twin_copy(j).start()
    low = r == 0
    for j in range(2):
        twin_copy(j).wait_recv()
        for i in range(rows // B):
            s = slice(i * B, (i + 1) * B)
            mine, their = pieces[2 + j, s, :].T, twin_in[j, s, :].T
            first = jnp.where(low, mine, their)
            second = jnp.where(low, their, mine)
            t = slice(j * rows + i * B, j * rows + (i + 1) * B)
            grad_excite[:ranks, t] = first[:ranks]
            grad_excite[ranks:, t] = second[:ranks]
            grad_source[:ranks, t] = first[edge : edge + ranks]
            grad_source[ranks:, t] = second[edge : edge + ranks]

    def sent(s, _):
        for j in chains:
            copy(j, s, slots.at[j, s]).wait_send()
        return 0

    lax.fori_loop(0, half - 1, sent, 0)
    for j in range(2):
        twin_copy(j).wait_send()


def square_kernel(
    n, factor, minus, source, grad_excite, grad_source,
    dense, load_sem, first, second, pieces, twin_in, a_send, a_recv, b_send, b_recv, t_send, t_recv,
):
    half = n // 2
    per = source.shape[0] // n
    rows = per // 4
    edge = B // 2
    ranks = grad_excite.shape[0] // 2
    me = lax.axis_index("tm")
    r = lax.div(me, half)
    q = lax.rem(me, half)
    qa, qb = lax.div(q, 2), lax.rem(q, 2)
    near = r * half + qa * 2 + 1 - qb
    far = r * half + (1 - qa) * 2 + qb
    twin = q + (1 - r) * half
    load = pltpu.make_async_copy(source, dense, load_sem.at[0])
    load.start()
    barrier = pltpu.get_barrier_semaphore()
    for p in (near, far, twin):
        pl.semaphore_signal(barrier, inc=1, device_id={"tm": p}, device_id_type=MESH)
    pl.semaphore_wait(barrier, 3)

    def span(j, a, b):
        block = a * 2 + b + ((1 - r) if j < 4 else r) * half
        return pl.ds(pl.multiple_of(block * per + (j % 4) * rows, 8), rows)

    def across(j):
        return j % 4 == 3

    def place(j, k, theirs):
        if across(j):
            return span(j, 1 - qa if theirs else qa, qb if k else 1 - qb)
        return span(j, qa if k else 1 - qa, 1 - qb if theirs else qb)

    def copy_a(j, k):
        return pltpu.make_async_remote_copy(
            src_ref=source.at[place(j, k, True), :], dst_ref=first.at[j, k],
            send_sem=a_send.at[j, k], recv_sem=a_recv.at[j, k],
            device_id={"tm": far if across(j) else near}, device_id_type=MESH,
        )

    def copy_b(j):
        return pltpu.make_async_remote_copy(
            src_ref=first.at[j, 0], dst_ref=second.at[j], send_sem=b_send.at[j], recv_sem=b_recv.at[j],
            device_id={"tm": near if across(j) else far}, device_id_type=MESH,
        )

    def copy_t(j):
        return pltpu.make_async_remote_copy(
            src_ref=pieces.at[j], dst_ref=twin_in.at[j], send_sem=t_send.at[j], recv_sem=t_recv.at[j],
            device_id={"tm": twin}, device_id_type=MESH,
        )

    def begin(j):
        for k in range(2):
            copy_a(j, k).start()

    def middle(j):
        copy_a(j, 0).wait_recv()
        first[j, 0] = first[j, 0] + dense[place(j, 0, False), :]
        copy_b(j).start()

    def put(value, j, who):
        for i in range(rows // B):
            t = value[i * B : (i + 1) * B].T
            lanes = slice((j % 4) * rows + i * B, (j % 4) * rows + (i + 1) * B)
            at = pl.ds(pl.multiple_of(who * ranks, ranks), ranks)
            grad_excite[at, lanes] = t[:ranks]
            grad_source[at, lanes] = t[edge : edge + ranks]

    def last(j):
        copy_a(j, 1).wait_recv()
        copy_b(j).wait_recv()
        value = (second[j] + first[j, 1] + dense[place(j, 1, False), :]) * factor - minus[0:1, :]
        if j < 4:
            pieces[j] = value
            copy_t(j).start()
        else:
            put(value, j, r)

    copy_a(0, 0).start()
    copy_a(3, 0).start()
    copy_a(1, 0).start()
    copy_a(0, 1).start()
    copy_a(3, 1).start()
    load.wait()
    middle(0)
    copy_a(2, 0).start()
    copy_a(1, 1).start()
    middle(3)
    copy_a(7, 0).start()
    middle(1)
    copy_a(4, 0).start()
    copy_a(2, 1).start()
    last(0)
    middle(2)
    copy_a(5, 0).start()
    copy_a(7, 1).start()
    last(3)
    last(1)
    middle(4)
    copy_a(6, 0).start()
    copy_a(4, 1).start()
    last(2)
    middle(7)
    middle(5)
    copy_a(5, 1).start()
    copy_a(6, 1).start()
    last(4)
    last(7)
    middle(6)
    last(5)
    for j in (0, 3, 1):
        copy_t(j).wait_recv()
        put(twin_in[j], j, 1 - r)
    last(6)
    copy_t(2).wait_recv()
    put(twin_in[2], 2, 1 - r)
    for j in range(8):
        for k in range(2):
            copy_a(j, k).wait_send()
        copy_b(j).wait_send()
    for j in range(4):
        copy_t(j).wait_send()


def body(marks, gaps, excite, source, base_rate, weights, decay):
    shard = marks.shape[0]
    slices, types = excite.shape
    n = lax.axis_size("tm")
    lanes_n = lax.axis_size("mark")
    half = n // 2
    rank = slices * lanes_n
    count = decay.shape[0]
    shard_blocks = shard // B
    blocks = 2 * shard_blocks
    events = 2 * shard
    groups = types // B
    width = count * PARTS
    dma = pltpu.SemaphoreType.DMA
    plane = pltpu.VMEM((blocks, B), F32)
    tall = pltpu.VMEM((events, B), F32)
    small = pltpu.VMEM((blocks * width, B), F32)
    types_own = types // n

    values, grad_base, minus, marks_all = pl.pallas_call(
        functools.partial(front_kernel, n, lanes_n, rank),
        out_shape=[
            jax.ShapeDtypeStruct((events, B), F32),
            jax.ShapeDtypeStruct((groups // n, B), F32),
            jax.ShapeDtypeStruct((8, B), F32),
            jax.ShapeDtypeStruct((2, shard_blocks, B), jnp.int32),
        ],
        in_specs=[HBM] * 7,
        out_specs=[HBM] * 4,
        scratch_shapes=[
            pltpu.VMEM((B, types), BF16),
            pltpu.VMEM((types, B), F32),
            tall,
            pltpu.SMEM((2, shard_blocks, B), jnp.int32),
            pltpu.VMEM((shard_blocks, B), jnp.int32),
            pltpu.VMEM((2, shard_blocks, B), jnp.int32),
            plane, plane, plane,
            pltpu.VMEM((blocks * SUB, B), F32),
            tall, tall,
            pltpu.VMEM((events, B), BF16),
            small, small, small,
            plane, plane, plane, plane,
            pltpu.VMEM((2, count + 8, B), F32), pltpu.VMEM((half, 2, count + 8, B), F32),
            plane, pltpu.VMEM((2 * lanes_n, blocks, B), F32),
            pltpu.VMEM((half, 2 * count + 8, B), F32), pltpu.VMEM((2 * count + 8, B), F32),
            pltpu.VMEM((n, groups // n, B), F32),
            pltpu.VMEM((n, groups // n, B), F32),
            dma((2,)), dma((2,)),
            dma((2,)), dma((2,)),
            dma((half - 1,)), dma((half - 1,)),
            dma((2 * lanes_n - 1, blocks // UNROLL)), dma((2 * lanes_n - 1, blocks // UNROLL)),
            dma((half - 1,)), dma((half - 1,)),
            dma((n - 1,)), dma((n - 1,)),
            tall, dma((blocks // UNROLL,)),
            pltpu.SMEM((count,), F32), pltpu.SMEM((count,), F32),
            pltpu.VMEM((shard_blocks, B), jnp.int32), pltpu.VMEM((shard_blocks, B), jnp.int32),
            pltpu.VMEM((groups, B), F32), pltpu.VMEM((groups // n, B), F32), pltpu.VMEM((8, B), F32),
            pltpu.VMEM((2, shard_blocks, B), jnp.int32), dma((5,)), dma((3,)),
        ],
        compiler_params=pltpu.CompilerParams(
            collective_id=0, has_side_effects=True, vmem_limit_bytes=ALL_VMEM
        ),
    )(weights, decay, marks.reshape(shard_blocks, B), gaps.reshape(shard_blocks, B), source, excite,
      base_rate.reshape(groups, B))

    dense = pl.pallas_call(
        scatter_kernel,
        out_shape=jax.ShapeDtypeStruct((types, B), F32),
        in_specs=[HBM] * 2,
        out_specs=HBM,
        scratch_shapes=[pltpu.SMEM((2, shard_blocks, B), jnp.int32), tall, dma((2,)), dma((8,))] + [pltpu.VMEM((types, B), F32)] * 8,
        compiler_params=pltpu.CompilerParams(vmem_limit_bytes=ALL_VMEM),
    )(marks_all, values)

    quarter = types_own // 4
    if half == 4 and quarter % B == 0:
        kernel = square_kernel
        scratch = [
            pltpu.VMEM((8, 2, quarter, B), F32),
            pltpu.VMEM((8, quarter, B), F32),
            pltpu.VMEM((4, quarter, B), F32),
            pltpu.VMEM((4, quarter, B), F32),
            dma((8, 2)), dma((8, 2)), dma((8,)), dma((8,)), dma((4,)), dma((4,)),
        ]
    else:
        kernel = ring_kernel
        scratch = [
            pltpu.VMEM((4, half - 1, types_own // 2, B), F32),
            pltpu.VMEM((4, types_own // 2, B), F32),
            pltpu.VMEM((2, types_own // 2, B), F32),
            dma((4, half - 1)), dma((4, half - 1)), dma((2,)), dma((2,)),
        ]
    grad_excite, grad_source = pl.pallas_call(
        functools.partial(kernel, n, types / (events * half)),
        out_shape=[jax.ShapeDtypeStruct((slices, types_own), F32)] * 2,
        in_specs=[VMEM, HBM],
        out_specs=[VMEM] * 2,
        scratch_shapes=[pltpu.VMEM((types, B), F32), dma((1,))] + scratch,
        compiler_params=pltpu.CompilerParams(
            collective_id=1, has_side_effects=True, vmem_limit_bytes=52 * 2**20
        ),
    )(minus, dense)
    return grad_excite, grad_source, grad_base.reshape(types_own)


def solution(mesh):
    return jax.shard_map(
        body,
        mesh=mesh,
        in_specs=(P("tm"), P("tm"), P("mark", None), P("mark", None), P(), P(), P()),
        out_specs=(P("mark", "tm"), P("mark", "tm"), P("tm")),
        check_vma=False,
    )
```

```python
import functools

import jax
import jax.numpy as jnp
from jax import lax
from jax.experimental import pallas as pl
from jax.experimental.pallas import tpu as pltpu
from jax.sharding import PartitionSpec as P

F32 = jnp.float32
BF16 = jnp.bfloat16
B = 128
SUB = 32
UNROLL = 16
ALL_VMEM = 60 * 2**20
PARTS = B // SUB
HIGH = lax.Precision.HIGHEST
MESH = pl.DeviceIdType.MESH
VMEM = pl.BlockSpec(memory_space=pltpu.VMEM)
SMEM = pl.BlockSpec(memory_space=pltpu.SMEM)
HBM = pl.BlockSpec(memory_space=pltpu.HBM)
NT = (((1,), (1,)), ((), ()))


def iota(shape, axis):
    return lax.broadcasted_iota(jnp.int32, shape, axis)


def dot(a, b):
    return jnp.dot(a, b, preferred_element_type=F32)


def halves(a):
    high = a.astype(BF16).astype(F32)
    return high, a - high


def down(ref, count):
    row = iota((count, B), 0)
    out = jnp.zeros((count, B), F32)
    for k in range(count):
        out = jnp.where(row == k, ref[k], out)
    return out


def parted(a):
    part = lax.div(iota(a.shape, 1), SUB)
    return jnp.concatenate([jnp.where(part == c, a, 0.0) for c in range(PARTS)], 0)


def turned(row):
    return jnp.broadcast_to(row, (B, B)).T


def batched(count, size, one, then=None):
    def body(g, _):
        stores = []
        for i in range(size):
            stores += one(g * size + i)
        for ref, where, value in stores:
            ref[where] = value
        if then is not None:
            then(g)
        return 0

    lax.fori_loop(0, count // size, body, 0)


def rows_at(b, size):
    return pl.ds(pl.multiple_of(b * size, size), size)


def front_kernel(
    n, lanes_n, rank,
    weights_in, decay_in, marks_in, gaps_in, src, exc, base_in,
    values_out, base_out, minus_out, marks_all,
    factors, table, rows, smarks, own, gshard, u, te, ts, sym, inside, excitation, lanes, states, sums, dec, base_e,
    inverse, remain, ends, device, summaries, partial, total, back, behind, base_own, base_parts,
    load_sem, mark_sem, ag_send, ag_recv, f_send, f_recv, p_send, p_recv, b_send, b_recv, g_send, g_recv, values, out_sem,
    weights, decay, marks, gaps, base, grad_base, minus, marks_out, in_sem, end_sem,
):
    count = decay.shape[0]
    width = count * PARTS
    half = n // 2
    shard_blocks = marks.shape[0]
    blocks = 2 * shard_blocks
    types = table.shape[0]
    groups = types // B
    ranks = src.shape[0] // 2
    edge = B // 2
    me = lax.axis_index("tm")
    mine = lax.axis_index("mark")
    r = lax.div(me, half)
    q = lax.rem(me, half)
    peers = [lax.rem(me + i, n) for i in range(1, n)]
    mates = [r * half + lax.rem(q + i, half) for i in range(1, half)]
    others = [lax.rem(mine + i, lanes_n) for i in range(1, lanes_n)]
    twin = q + (1 - r) * half

    if ranks < edge:
        for a in range(2):
            factors[a * edge + ranks : (a + 1) * edge, :] = jnp.zeros((edge - ranks, types), BF16)
    barrier = pltpu.get_barrier_semaphore()
    targets = [{"tm": p, "mark": mine} for p in peers]
    targets += [{"tm": t, "mark": o} for o in others for t in (me, twin)]
    for t in targets:
        pl.semaphore_signal(barrier, inc=1, device_id=t, device_id_type=MESH)
    small = [
        pltpu.make_async_copy(a, b, in_sem.at[i])
        for i, (a, b) in enumerate(
            ((marks_in, marks), (gaps_in, gaps), (weights_in, weights), (decay_in, decay), (base_in, base))
        )
    ]
    for copy in small:
        copy.start()
    loads = []
    for a, ref in enumerate((src, exc)):
        copy = pltpu.make_async_copy(
            ref.at[pl.ds(pl.multiple_of(r * ranks, ranks), ranks), :],
            factors.at[a * edge : a * edge + ranks, :],
            load_sem.at[a],
        )
        copy.start()
        loads.append(copy)

    small[0].wait()
    small[1].wait()
    own[...] = marks[...]
    marks_out[r] = marks[...]
    gshard[r] = gaps[...]
    first_move = pltpu.make_async_copy(own, smarks.at[r], mark_sem.at[0])
    first_move.start()
    gathers = []
    pl.semaphore_wait(barrier, len(targets))
    for a, (ref, dst) in enumerate(((own, marks_out), (gaps, gshard))):
        copy = pltpu.make_async_remote_copy(
            src_ref=ref, dst_ref=dst.at[r], send_sem=ag_send.at[a], recv_sem=ag_recv.at[a],
            device_id={"tm": twin}, device_id_type=MESH,
        )
        copy.start()
        gathers.append(copy)

    for copy in loads:
        copy.wait()

    def build(c, acc):
        s = rows_at(c, B)
        t = factors[:, s].astype(F32).T
        table[s, :] = t
        return acc + jnp.sum(t.reshape(B // 8, 8, B), axis=0)

    acc = lax.fori_loop(0, groups, build, jnp.zeros((8, B), F32), unroll=8)
    xtot = jnp.sum(acc, axis=0, keepdims=True)

    for copy in small[2:]:
        copy.wait()
    d8, w8 = down(decay, count), down(weights, count)
    li, lj = iota((B, B), 0), iota((B, B), 1)
    start_lane = lax.div(lj, SUB) * SUB
    part_row = lax.div(iota((1, B), 1), SUB)
    lane = iota((1, B), 1)

    def pick(mask, a):
        return jnp.dot(a, mask.astype(F32), precision=HIGH, preferred_element_type=F32)

    def two(a, b):
        k = a.shape[0]
        high, low = halves(a)
        both = dot(jnp.concatenate([high, low], 0).astype(BF16), b)
        return both[:k] + both[k:]

    def prepare(j):
        gap = gshard[j].astype(F32)
        uv = pick(li <= lj, gap)
        at = rows_at(j, shard_blocks)
        u[at, :] = uv
        te[at, :] = pick(li <= start_lane + SUB - 1, gap)
        ts[at, :] = pick(li < start_lane, gap)
        lengths = jnp.broadcast_to(uv[:, B - 1 :], (shard_blocks, B))
        later = (iota((shard_blocks, shard_blocks), 1) > iota((shard_blocks, shard_blocks), 0)).astype(F32)
        left = jnp.dot(later, lengths, precision=HIGH, preferred_element_type=F32)
        ends[at, :] = left
        device[j, count:, :] = jnp.broadcast_to(left[0:1, :] + lengths[0:1, :], (8, B))

    def fetch(j):
        def block(b, _):
            for k in range(4):
                for i in range(B):
                    m = smarks[j, b * 4 + k, i]
                    rows[pl.ds((j * shard_blocks + b * 4 + k) * B + i, 1), :] = table[pl.ds(m, 1), :]
            return 0

        lax.fori_loop(0, shard_blocks // 4, block, 0)

    def emit(b):
        ur, er, sr = u[pl.ds(b, 1), :], te[pl.ds(b, 1), :], ts[pl.ds(b, 1), :]
        vals = rows[rows_at(b, B), :].astype(BF16)
        span = er - sr
        decays = [jnp.exp(-d8 * span[:, c * SUB : c * SUB + 1]) for c in range(PARTS)]
        spot = (rows_at(b, width), slice(None))
        return [
            (sums, spot, two(parted(d8 * jnp.exp(-d8 * (er - ur))), vals)),
            (dec, spot, jnp.concatenate([jnp.broadcast_to(t, (count, B)) for t in decays], 0)),
        ]

    prepare(r)
    first_move.wait()
    fetch(r)
    batched(shard_blocks, 2 * UNROLL, lambda b: emit(r * shard_blocks + b))
    for copy in gathers:
        copy.wait_recv()
    second_move = pltpu.make_async_copy(marks_out.at[1 - r], smarks.at[1 - r], mark_sem.at[1])
    second_move.start()
    marks_copy = pltpu.make_async_copy(marks_out, marks_all, end_sem.at[0])
    marks_copy.start()
    prepare(1 - r)
    second_move.wait()
    fetch(1 - r)
    batched(shard_blocks, 2 * UNROLL, lambda b: emit((1 - r) * shard_blocks + b))

    zero = jnp.zeros((count, B), F32)

    def recur(start, keep, ahead):
        def step(i, pair):
            b = i if ahead else shard_blocks - 1 - i
            for c in range(PARTS) if ahead else reversed(range(PARTS)):
                nxt = []
                for j in range(2):
                    s = pl.ds(pl.multiple_of((j * shard_blocks + b) * width + c * count, count), count)
                    if keep:
                        states[s, :] = pair[j]
                    nxt.append(pair[j] * dec[s, :] + sums[s, :])
                pair = tuple(nxt)
            return pair

        return lax.fori_loop(0, shard_blocks, step, start, unroll=8)

    def share(source, dest, send, recv):
        copies = []
        for i, p in enumerate(mates):
            copies.append(
                pltpu.make_async_remote_copy(
                    src_ref=source, dst_ref=dest.at[q], send_sem=send.at[i], recv_sem=recv.at[i],
                    device_id={"tm": p}, device_id_type=MESH,
                )
            )
        for copy in copies:
            copy.start()
        dest[q] = source[...]
        return copies

    for j, state in enumerate(recur((zero, zero), False, True)):
        device[j, 0:count, :] = state
    state_copies = share(device, summaries, f_send, f_recv)

    base_high, base_low = halves(base[...])
    base2 = jnp.concatenate([base_high, base_low], 0).T.astype(BF16)
    subi = iota((SUB, B), 0)
    subj = lax.rem(iota((SUB, B), 1), SUB)

    def mark_row(b):
        return marks_out[lax.div(b, shard_blocks), pl.ds(lax.rem(b, shard_blocks), 1), :]

    def within(b):
        ur, sr = u[pl.ds(b, 1), :], ts[pl.ds(b, 1), :]
        s = rows_at(b, B)
        col = turned(ur)
        colc = col[0:SUB]
        for c in range(1, PARTS):
            colc = jnp.where(part_row == c, col[c * SUB : (c + 1) * SUB], colc)
        apart = jnp.abs(colc - ur)
        g = jnp.zeros((SUB, B), F32)
        for k in range(count):
            g = g + (weights[k] * decay[k]) * jnp.exp(-decay[k] * apart)
        high, low = halves(jnp.where(subi > subj, g, 0.0))
        left = jnp.concatenate([parted(high), parted(low)], 0).astype(BF16)
        both = dot(left, rows[s, :].astype(BF16))
        lh, ll = halves(parted(w8 * jnp.exp(-d8 * (ur - sr))))
        stack = jnp.concatenate([lh, lh, ll, jnp.zeros((B - 3 * width, B), F32)], 0)
        m = mark_row(b)
        hi, lo = lax.div(m, B), lax.rem(m, B)
        onehot = (lax.rem(iota((2 * groups, B), 0), groups) == hi).astype(BF16)
        found = dot(base2, onehot)
        return [
            (sym, (rows_at(b, SUB), slice(None)), g),
            (inside, (s, slice(None)), both[:B] + both[B:]),
            (lanes, (s, slice(None)), stack.T.astype(BF16)),
            (base_e, (pl.ds(b, 1), slice(None)), jnp.sum(jnp.where(li == lo, found, 0.0), axis=0, keepdims=True)),
        ]

    batched(blocks, 2 * UNROLL, within)

    for copy in state_copies:
        copy.wait()
    start = [zero, zero]
    after = [jnp.zeros((1, B), F32)] * 2
    t_end = jnp.zeros((1, B), F32)
    for t in range(n):
        held = summaries[t % half, t // half]
        span = held[count : count + 1]
        t_end = t_end + span
        for j in range(2):
            mark = q + j * half
            start[j] = jnp.where(t < mark, start[j] * jnp.exp(-d8 * span) + held[0:count], start[j])
            after[j] = after[j] + jnp.where(t > mark, span, 0.0)
    recur(tuple(start), True, True)
    for j in range(2):
        at = slice(j * shard_blocks, (j + 1) * shard_blocks)
        ends[at, :] = ends[at, :] + after[j]

    fill = jnp.zeros((B - 3 * width, B), F32)

    def forward(b):
        s = rows_at(b, B)
        sh, sl = halves(states[rows_at(b, width), :])
        value = inside[s, :] + dot(lanes[s, :], jnp.concatenate([sh, sl, sh, fill], 0).astype(BF16))
        product = value * pltpu.roll(rows[s, :], edge, 1)
        tot = jnp.sum(product.T[:edge], axis=0, keepdims=True)
        return [
            (excitation, (s, slice(None)), value),
            (partial, (pl.ds(b, 1), slice(None)), tot * (1.0 / rank)),
        ]

    spot = mine * 2 + r

    def part_copies(g):
        s = rows_at(g, UNROLL)
        copies = []
        for i, t in enumerate([(twin, mine)] + [(t, o) for o in others for t in (me, twin)]):
            copies.append(
                pltpu.make_async_remote_copy(
                    src_ref=partial.at[s, :], dst_ref=total.at[spot, s, :],
                    send_sem=p_send.at[i, g], recv_sem=p_recv.at[i, g],
                    device_id={"tm": t[0], "mark": t[1]}, device_id_type=MESH,
                )
            )
        return copies

    def send_part(g):
        for copy in part_copies(g):
            copy.start()

    batched(blocks, UNROLL, forward, send_part)
    total[spot] = partial[...]

    def rest(b):
        left = w8 * (1.0 - jnp.exp(-d8 * (u[pl.ds(b, 1), :] * -1.0 + lengths_row(b) + ends[pl.ds(b, 1), :])))
        rem = jnp.sum(left, axis=0, keepdims=True)
        return rem, two(jnp.broadcast_to(rem, (8, B)), rows[rows_at(b, B), :].astype(BF16))

    def lengths_row(b):
        return u[pl.ds(b, 1), B - 1 :]

    def summed(values):
        while len(values) > 1:
            values = [sum(values[i : i + 2]) for i in range(0, len(values), 2)]
        return values[0]

    def rests(g, comp):
        found = [rest(g * 2 * UNROLL + i) for i in range(2 * UNROLL)]
        remain[rows_at(g, 2 * UNROLL), :] = jnp.concatenate([f[0] for f in found], 0)
        return comp + summed([f[1] for f in found])

    comp = lax.fori_loop(0, blocks // (2 * UNROLL), rests, jnp.zeros((8, B), F32))

    row8 = iota((8, B), 0)

    def thirds(a, places):
        high, rest = halves(a)
        mid, low = halves(rest)
        out = jnp.zeros((8, B), F32)
        for term, where in zip((high, mid, low), places):
            for k in where:
                out = jnp.where(row8 == k, term, out)
        return out

    xstack = thirds(xtot * (-1.0 / types), ((0, 2, 5), (1, 4), (3,)))
    fill24 = jnp.zeros((B - 3 * width - 8, B), F32)

    def prepare_turn(b):
        lh, ll = halves(parted(w8 * jnp.exp(-d8 * (te[pl.ds(b, 1), :] - u[pl.ds(b, 1), :]))))
        rstack = thirds(remain[pl.ds(b, 1), :], ((0, 1, 3), (2, 4), (5,)))
        turn = jnp.concatenate([lh, lh, ll, rstack, fill24], 0).T.astype(BF16)
        return [(lanes, (rows_at(b, B), slice(None)), turn)]

    batched(blocks, 2 * UNROLL, prepare_turn)
    for g in range(blocks // UNROLL):
        for copy in part_copies(g):
            copy.wait()
    intensity = base_e[...]
    for j in range(2 * lanes_n):
        intensity = intensity + total[j]
    inverse[...] = 1.0 / intensity

    def reverse(b):
        e8 = d8 * jnp.exp(-d8 * (u[pl.ds(b, 1), :] - ts[pl.ds(b, 1), :])) * inverse[pl.ds(b, 1), :]
        return [(sums, (rows_at(b, width), slice(None)), two(parted(e8), rows[rows_at(b, B), :].astype(BF16)))]

    batched(blocks, 2 * UNROLL, reverse)

    for j, state in enumerate(recur((zero, zero), False, False)):
        behind[j * count : (j + 1) * count, :] = state
    behind[2 * count :, :] = comp
    back_copies = share(behind, back, b_send, b_recv)

    def spread(b):
        m = mark_row(b)
        hi, lo = lax.div(m, B), lax.rem(m, B)
        ih, il = halves(inverse[pl.ds(b, 1), :])
        wide = jnp.concatenate([jnp.broadcast_to(ih, (groups, B)), jnp.broadcast_to(il, (groups, B))], 0)
        left = jnp.where(lax.rem(iota((2 * groups, B), 0), groups) == hi, wide, 0.0).astype(BF16)
        right = (li == lo).astype(BF16)
        return left, right

    def spreads(g, both):
        pairs = [spread(r * shard_blocks + g * 16 + i) for i in range(16)]
        left = jnp.concatenate([p[0] for p in pairs], 1)
        right = jnp.concatenate([p[1] for p in pairs], 1)
        return both + lax.dot_general(left, right, NT, preferred_element_type=F32)

    both = lax.fori_loop(0, shard_blocks // 16, spreads, jnp.zeros((2 * groups, B), F32))
    base_own[...] = (both[:groups] + both[groups:]).reshape(base_own.shape)
    base_copies = []
    for i, p in enumerate(peers):
        copy = pltpu.make_async_remote_copy(
            src_ref=base_own.at[p], dst_ref=base_parts.at[me], send_sem=g_send.at[i], recv_sem=g_recv.at[i],
            device_id={"tm": p}, device_id_type=MESH,
        )
        copy.start()
        base_copies.append(copy)
    base_parts[me] = base_own[me]

    def feedback(b):
        s = rows_at(b, B)
        ir = inverse[pl.ds(b, 1), :]
        high, low = halves(jnp.where(subi < subj, sym[rows_at(b, SUB), :] * ir, 0.0))
        left = jnp.concatenate([parted(high), parted(low)], 0).astype(BF16)
        both = dot(left, rows[s, :].astype(BF16))
        return [(inside, (s, slice(None)), jnp.where(lane < edge, excitation[s, :] * turned(ir), both[:B] + both[B:]))]

    batched(blocks, 2 * UNROLL, feedback)

    for copy in back_copies:
        copy.wait()
    pending = [zero, zero]
    comp_all = jnp.zeros((8, B), F32)
    for p in range(half):
        comp_all = comp_all + back[p, 2 * count :, :]
    for t in reversed(range(n)):
        p, k = t % half, t // half
        span = summaries[p, k, count : count + 1, :]
        for j in range(2):
            pending[j] = jnp.where(
                t > q + j * half,
                pending[j] * jnp.exp(-d8 * span) + back[p, k * count : (k + 1) * count, :],
                pending[j],
            )
    recur(tuple(pending), True, False)
    events_all = blocks * B * half
    for copy in base_copies:
        copy.wait()
    base_all = base_parts[0]
    for p in range(1, n):
        base_all = base_all + base_parts[p]
    grad_base[...] = base_all * (types / events_all) - t_end * (1.0 / events_all)
    minus[...] = jnp.where(lane < edge, comp_all * (1.0 / events_all), 0.0)
    finals = [
        pltpu.make_async_copy(grad_base, base_out, end_sem.at[1]),
        pltpu.make_async_copy(minus, minus_out, end_sem.at[2]),
    ]
    for copy in finals:
        copy.start()

    def distant(b):
        s = rows_at(b, B)
        sh, sl = halves(states[rows_at(b, width), :])
        stack = jnp.concatenate([sh, sl, sh, xstack, fill24], 0)
        value = dot(lanes[s, :], jnp.where(lane < edge, 0.0, stack).astype(BF16))
        return [(values, (s, slice(None)), inside[s, :] + value)]

    def piece(g):
        s = rows_at(g, UNROLL * B)
        return pltpu.make_async_copy(values.at[s, :], values_out.at[s, :], out_sem.at[g])

    batched(blocks, UNROLL, distant, lambda g: piece(g).start())

    for copy in gathers:
        copy.wait_send()
    for copy in finals + [marks_copy]:
        copy.wait()
    for g in range(blocks // UNROLL):
        piece(g).wait()


def scatter_kernel(marks_in, values_in, out, marks, values, load_sem, out_sem, *tables):
    count = len(tables)
    types = out.shape[0]
    loads = [
        pltpu.make_async_copy(values_in, values, load_sem.at[0]),
        pltpu.make_async_copy(marks_in, marks, load_sem.at[1]),
    ]
    for copy in loads:
        copy.start()

    def zero(i, _):
        for t in tables:
            t[rows_at(i, 32), :] = jnp.zeros((32, B), F32)
        return 0

    lax.fori_loop(0, types // 32, zero, 0, unroll=4)
    for copy in loads:
        copy.wait()
    shards, blocks, _ = marks.shape
    for j in range(shards):

        def block(b, _):
            for i in range(B):
                t = tables[i % count]
                m = marks[j, b, i]
                e = (j * blocks + b) * B + i
                t[pl.ds(m, 1), :] = t[pl.ds(m, 1), :] + values[pl.ds(e, 1), :]
            return 0

        lax.fori_loop(0, blocks, block, 0)

    result = values if values.shape[0] >= types else tables[0]
    pieces = out_sem.shape[0]
    size = types // pieces

    def piece(c):
        s = rows_at(c, size)
        return pltpu.make_async_copy(result.at[s, :], out.at[s, :], out_sem.at[c])

    def total(c, _):
        def add(i, _):
            s = pl.ds(pl.multiple_of(c * size + i * 32, 32), 32)
            acc = [t[s, :] for t in tables]
            while len(acc) > 1:
                acc = [acc[i] + acc[i + 1] for i in range(0, len(acc), 2)]
            result[s, :] = acc[0]
            return 0

        lax.fori_loop(0, size // 32, add, 0, unroll=16)
        piece(c).start()
        return 0

    lax.fori_loop(0, pieces, total, 0)
    for c in range(pieces):
        piece(c).wait()


def ring_kernel(n, factor, minus, source, grad_excite, grad_source, dense, load_sem, slots, pieces, twin_in, send, recv, t_send, t_recv):
    half = n // 2
    per = dense.shape[0] // n
    rows = per // 2
    edge = B // 2
    ranks = grad_excite.shape[0] // 2
    me = lax.axis_index("tm")
    r = lax.div(me, half)
    q = lax.rem(me, half)
    odd = lax.rem(q, 2)
    at = lax.div(q, 2) + odd * (lax.div(2 * half - 1 - q, 2) - lax.div(q, 2))
    twin = q + (1 - r) * half

    def member(place):
        c = lax.rem(place + 2 * half, half)
        return 2 * c + lax.div(c, half // 2) * (2 * half - 1 - 4 * c)

    towards = [member(at + 1) + r * half, member(at - 1) + r * half]
    load = pltpu.make_async_copy(source, dense, load_sem.at[0])
    load.start()
    barrier = pltpu.get_barrier_semaphore()
    for p in towards + [twin]:
        pl.semaphore_signal(barrier, inc=1, device_id={"tm": p}, device_id_type=MESH)
    pl.semaphore_wait(barrier, 3)

    def span(j, step):
        way, kind = j % 2, j // 2
        place = at + 1 + step if way else at - 1 - step
        where = (1 - r) if kind == 0 else r
        block = member(place) + where * half
        return pl.ds(pl.multiple_of(block * per + way * rows, 8), rows)

    def copy(j, step, source):
        return pltpu.make_async_remote_copy(
            src_ref=source, dst_ref=slots.at[j, step], send_sem=send.at[j, step], recv_sem=recv.at[j, step],
            device_id={"tm": towards[j % 2]}, device_id_type=MESH,
        )

    chains = range(4)
    for j in chains:
        copy(j, 0, source.at[span(j, 0), :]).start()
    load.wait()

    def step(s, _):
        for j in chains:
            held = slots.at[j, s - 1]
            copy(j, s - 1, held).wait_recv()
            held[...] += dense[span(j, s), :]
            copy(j, s, held).start()
        return 0

    lax.fori_loop(1, half - 1, step, 0)

    def twin_copy(j):
        return pltpu.make_async_remote_copy(
            src_ref=pieces.at[j], dst_ref=twin_in.at[j], send_sem=t_send.at[j], recv_sem=t_recv.at[j],
            device_id={"tm": twin}, device_id_type=MESH,
        )

    for j in chains:
        copy(j, half - 2, slots.at[j, half - 2]).wait_recv()
        pieces[j] = (slots[j, half - 2] + dense[span(j, half - 1), :]) * factor - minus[0:1, :]
        if j < 2:
            twin_copy(j).start()
    low = r == 0
    for j in range(2):
        twin_copy(j).wait_recv()
        for i in range(rows // B):
            s = slice(i * B, (i + 1) * B)
            mine, their = pieces[2 + j, s, :].T, twin_in[j, s, :].T
            first = jnp.where(low, mine, their)
            second = jnp.where(low, their, mine)
            t = slice(j * rows + i * B, j * rows + (i + 1) * B)
            grad_excite[:ranks, t] = first[:ranks]
            grad_excite[ranks:, t] = second[:ranks]
            grad_source[:ranks, t] = first[edge : edge + ranks]
            grad_source[ranks:, t] = second[edge : edge + ranks]

    def sent(s, _):
        for j in chains:
            copy(j, s, slots.at[j, s]).wait_send()
        return 0

    lax.fori_loop(0, half - 1, sent, 0)
    for j in range(2):
        twin_copy(j).wait_send()


def square_kernel(
    n, factor, minus, source, grad_excite, grad_source,
    dense, load_sem, first, second, pieces, twin_in, a_send, a_recv, b_send, b_recv, t_send, t_recv,
):
    half = n // 2
    per = source.shape[0] // n
    rows = per // 4
    edge = B // 2
    ranks = grad_excite.shape[0] // 2
    me = lax.axis_index("tm")
    r = lax.div(me, half)
    q = lax.rem(me, half)
    qa, qb = lax.div(q, 2), lax.rem(q, 2)
    near = r * half + qa * 2 + 1 - qb
    far = r * half + (1 - qa) * 2 + qb
    twin = q + (1 - r) * half
    load = pltpu.make_async_copy(source, dense, load_sem.at[0])
    load.start()
    barrier = pltpu.get_barrier_semaphore()
    for p in (near, far, twin):
        pl.semaphore_signal(barrier, inc=1, device_id={"tm": p}, device_id_type=MESH)
    pl.semaphore_wait(barrier, 3)

    def span(j, a, b):
        block = a * 2 + b + ((1 - r) if j < 4 else r) * half
        return pl.ds(pl.multiple_of(block * per + (j % 4) * rows, 8), rows)

    def across(j):
        return j % 4 == 3

    def place(j, k, theirs):
        if across(j):
            return span(j, 1 - qa if theirs else qa, qb if k else 1 - qb)
        return span(j, qa if k else 1 - qa, 1 - qb if theirs else qb)

    def copy_a(j, k):
        return pltpu.make_async_remote_copy(
            src_ref=source.at[place(j, k, True), :], dst_ref=first.at[j, k],
            send_sem=a_send.at[j, k], recv_sem=a_recv.at[j, k],
            device_id={"tm": far if across(j) else near}, device_id_type=MESH,
        )

    def copy_b(j):
        return pltpu.make_async_remote_copy(
            src_ref=first.at[j, 0], dst_ref=second.at[j], send_sem=b_send.at[j], recv_sem=b_recv.at[j],
            device_id={"tm": near if across(j) else far}, device_id_type=MESH,
        )

    def copy_t(j):
        return pltpu.make_async_remote_copy(
            src_ref=pieces.at[j], dst_ref=twin_in.at[j], send_sem=t_send.at[j], recv_sem=t_recv.at[j],
            device_id={"tm": twin}, device_id_type=MESH,
        )

    def begin(j):
        for k in range(2):
            copy_a(j, k).start()

    def middle(j):
        copy_a(j, 0).wait_recv()
        first[j, 0] = first[j, 0] + dense[place(j, 0, False), :]
        copy_b(j).start()

    def put(value, j, who):
        for i in range(rows // B):
            t = value[i * B : (i + 1) * B].T
            lanes = slice((j % 4) * rows + i * B, (j % 4) * rows + (i + 1) * B)
            at = pl.ds(pl.multiple_of(who * ranks, ranks), ranks)
            grad_excite[at, lanes] = t[:ranks]
            grad_source[at, lanes] = t[edge : edge + ranks]

    def last(j):
        copy_a(j, 1).wait_recv()
        copy_b(j).wait_recv()
        value = (second[j] + first[j, 1] + dense[place(j, 1, False), :]) * factor - minus[0:1, :]
        if j < 4:
            pieces[j] = value
            copy_t(j).start()
        else:
            put(value, j, r)

    copy_a(0, 0).start()
    copy_a(3, 0).start()
    copy_a(1, 0).start()
    copy_a(0, 1).start()
    copy_a(3, 1).start()
    load.wait()
    middle(0)
    copy_a(2, 0).start()
    copy_a(1, 1).start()
    middle(3)
    copy_a(7, 0).start()
    middle(1)
    copy_a(4, 0).start()
    copy_a(2, 1).start()
    last(0)
    middle(2)
    copy_a(5, 0).start()
    copy_a(7, 1).start()
    last(3)
    last(1)
    middle(4)
    copy_a(6, 0).start()
    copy_a(4, 1).start()
    last(2)
    middle(7)
    middle(5)
    copy_a(5, 1).start()
    copy_a(6, 1).start()
    last(4)
    last(7)
    middle(6)
    last(5)
    for j in (0, 3, 1):
        copy_t(j).wait_recv()
        put(twin_in[j], j, 1 - r)
    last(6)
    copy_t(2).wait_recv()
    put(twin_in[2], 2, 1 - r)
    for j in range(8):
        for k in range(2):
            copy_a(j, k).wait_send()
        copy_b(j).wait_send()
    for j in range(4):
        copy_t(j).wait_send()


def body(marks, gaps, excite, source, base_rate, weights, decay):
    shard = marks.shape[0]
    slices, types = excite.shape
    n = lax.axis_size("tm")
    lanes_n = lax.axis_size("mark")
    half = n // 2
    rank = slices * lanes_n
    count = decay.shape[0]
    shard_blocks = shard // B
    blocks = 2 * shard_blocks
    events = 2 * shard
    groups = types // B
    width = count * PARTS
    dma = pltpu.SemaphoreType.DMA
    plane = pltpu.VMEM((blocks, B), F32)
    tall = pltpu.VMEM((events, B), F32)
    small = pltpu.VMEM((blocks * width, B), F32)
    types_own = types // n

    values, grad_base, minus, marks_all = pl.pallas_call(
        functools.partial(front_kernel, n, lanes_n, rank),
        out_shape=[
            jax.ShapeDtypeStruct((events, B), F32),
            jax.ShapeDtypeStruct((groups // n, B), F32),
            jax.ShapeDtypeStruct((8, B), F32),
            jax.ShapeDtypeStruct((2, shard_blocks, B), jnp.int32),
        ],
        in_specs=[HBM] * 7,
        out_specs=[HBM] * 4,
        scratch_shapes=[
            pltpu.VMEM((B, types), BF16),
            pltpu.VMEM((types, B), F32),
            tall,
            pltpu.SMEM((2, shard_blocks, B), jnp.int32),
            pltpu.VMEM((shard_blocks, B), jnp.int32),
            pltpu.VMEM((2, shard_blocks, B), jnp.int32),
            plane, plane, plane,
            pltpu.VMEM((blocks * SUB, B), F32),
            tall, tall,
            pltpu.VMEM((events, B), BF16),
            small, small, small,
            plane, plane, plane, plane,
            pltpu.VMEM((2, count + 8, B), F32), pltpu.VMEM((half, 2, count + 8, B), F32),
            plane, pltpu.VMEM((2 * lanes_n, blocks, B), F32),
            pltpu.VMEM((half, 2 * count + 8, B), F32), pltpu.VMEM((2 * count + 8, B), F32),
            pltpu.VMEM((n, groups // n, B), F32),
            pltpu.VMEM((n, groups // n, B), F32),
            dma((2,)), dma((2,)),
            dma((2,)), dma((2,)),
            dma((half - 1,)), dma((half - 1,)),
            dma((2 * lanes_n - 1, blocks // UNROLL)), dma((2 * lanes_n - 1, blocks // UNROLL)),
            dma((half - 1,)), dma((half - 1,)),
            dma((n - 1,)), dma((n - 1,)),
            tall, dma((blocks // UNROLL,)),
            pltpu.SMEM((count,), F32), pltpu.SMEM((count,), F32),
            pltpu.VMEM((shard_blocks, B), jnp.int32), pltpu.VMEM((shard_blocks, B), jnp.int32),
            pltpu.VMEM((groups, B), F32), pltpu.VMEM((groups // n, B), F32), pltpu.VMEM((8, B), F32),
            pltpu.VMEM((2, shard_blocks, B), jnp.int32), dma((5,)), dma((3,)),
        ],
        compiler_params=pltpu.CompilerParams(
            collective_id=0, has_side_effects=True, vmem_limit_bytes=ALL_VMEM
        ),
    )(weights, decay, marks.reshape(shard_blocks, B), gaps.reshape(shard_blocks, B), source, excite,
      base_rate.reshape(groups, B))

    dense = pl.pallas_call(
        scatter_kernel,
        out_shape=jax.ShapeDtypeStruct((types, B), F32),
        in_specs=[HBM] * 2,
        out_specs=HBM,
        scratch_shapes=[pltpu.SMEM((2, shard_blocks, B), jnp.int32), tall, dma((2,)), dma((8,))] + [pltpu.VMEM((types, B), F32)] * 8,
        compiler_params=pltpu.CompilerParams(vmem_limit_bytes=ALL_VMEM),
    )(marks_all, values)

    quarter = types_own // 4
    if half == 4 and quarter % B == 0:
        kernel = square_kernel
        scratch = [
            pltpu.VMEM((8, 2, quarter, B), F32),
            pltpu.VMEM((8, quarter, B), F32),
            pltpu.VMEM((4, quarter, B), F32),
            pltpu.VMEM((4, quarter, B), F32),
            dma((8, 2)), dma((8, 2)), dma((8,)), dma((8,)), dma((4,)), dma((4,)),
        ]
    else:
        kernel = ring_kernel
        scratch = [
            pltpu.VMEM((4, half - 1, types_own // 2, B), F32),
            pltpu.VMEM((4, types_own // 2, B), F32),
            pltpu.VMEM((2, types_own // 2, B), F32),
            dma((4, half - 1)), dma((4, half - 1)), dma((2,)), dma((2,)),
        ]
    grad_excite, grad_source = pl.pallas_call(
        functools.partial(kernel, n, types / (events * half)),
        out_shape=[jax.ShapeDtypeStruct((slices, types_own), F32)] * 2,
        in_specs=[VMEM, HBM],
        out_specs=[VMEM] * 2,
        scratch_shapes=[pltpu.VMEM((types, B), F32), dma((1,))] + scratch,
        compiler_params=pltpu.CompilerParams(
            collective_id=1, has_side_effects=True, vmem_limit_bytes=52 * 2**20
        ),
    )(minus, dense)
    return grad_excite, grad_source, grad_base.reshape(types_own)


def solution(mesh):
    return jax.shard_map(
        body,
        mesh=mesh,
        in_specs=(P("tm"), P("tm"), P("mark", None), P("mark", None), P(), P(), P()),
        out_specs=(P("mark", "tm"), P("mark", "tm"), P("tm")),
        check_vma=False,
    )
```
